128 devices in a mesh: dp: 16 (over z, x), gx: 2 (over core), gy: 4 (over y).
Axes of the slice: x: 4, y: 4, z: 4, core: 2. Of those that a mesh axis runs over, the one named last changes fastest.
Arguments:
- layer_input: bfloat16 [16384, 1536], P(('dp', 'gy'), 'gx'), may hold values from -6 to 6
- norm1_gain: float32 [1536], P('gx'), may hold values from 0.5 to 1.5
- q_weight: bfloat16 [1536, 1536], P('gx', 'gy'), may hold values from -0.15625 to 0.15625
- q_bias: float32 [1536], P('gy'), may hold values from -3 to 3
- kv_weight: bfloat16 [1536, 512], P('gx'), may hold values from -0.15625 to 0.15625
- kv_bias: float32 [512], replicated, may hold values from -3 to 3
- o_weight: bfloat16 [1536, 1536], P('gy', 'gx'), may hold values from -1.25 to 1.25
- norm2_gain: float32 [1536], P('gx'), may hold values from 0.5 to 1.5
- gate_weight: bfloat16 [1536, 8960], P('gx', 'gy'), may hold values from -0.15625 to 0.15625
- up_weight: bfloat16 [1536, 8960], P('gx', 'gy'), may hold values from -0.15625 to 0.15625
- down_weight: bfloat16 [8960, 1536], P('gy', 'gx'), may hold values from -0.0625 to 0.0625
- seq_lengths: int32 [16, 4], P('dp'), may hold values from 0 to 1024, as said below
- out_grad: bfloat16 [16384, 1536], P(('dp', 'gy'), 'gx'), may hold values from -6 to 6
Outputs:
- block_out: float32 [16384, 1536], P(('dp', 'gy'), 'gx')
- input_grad: float32 [16384, 1536], P(('dp', 'gy'), 'gx')
- norm1_gain_grad: float32 [1536], P('gx')
- q_weight_grad: float32 [1536, 1536], P('gx', 'gy')
- q_bias_grad: float32 [1536], P('gy')
- kv_weight_grad: float32 [1536, 512], P('gx')
- kv_bias_grad: float32 [512], replicated
- o_weight_grad: float32 [1536, 1536], P('gy', 'gx')
- norm2_gain_grad: float32 [1536], P('gx')
- gate_weight_grad: float32 [1536, 8960], P('gx', 'gy')
- up_weight_grad: float32 [1536, 8960], P('gx', 'gy')
- down_weight_grad: float32 [8960, 1536], P('gy', 'gx')
The draws below stay inside these ranges and needn't reach their ends.
Inputs may be any that keep to these rules, and one draw needn't show every extreme that they name: `seq_lengths`: row g holds the lengths of data group g's packed sequences in order; they sum to 1024 or less, the rest of the group's tokens being padding. In every row one sequence, in a slot drawn from the seed, is at least 832 tokens long and starts within the first 192 tokens; in one row it is exactly 1024 and the other slots are 0. The rows whose index differs in parity from that row leave one or more padding tokens; the others have none.
All inputs are finite; a program needn't handle non-finite values.
Results may differ from the reference program's by a relative error of at most 0.022.
Values may be sent and summed in bfloat16 or wider, within the bound.
A program may use at most 192 MiB of HBM per device.

```python
import jax
import jax.numpy as jnp
from jax import lax

D = 1536
FF = 8960
QUERY_HEADS = 12
KEY_VALUE_HEADS = 2
HEAD_SIZE = 128
SLOTS = 4
GROUP_TOKENS = 1024
TOKENS = 16384
QD = 1536
KVD = 512
N_DP = 16


def draw_seq_lengths(key, part):
    key = jax.random.fold_in(key, 7)
    full_group = jax.random.randint(jax.random.fold_in(key, 1), (), 0, N_DP)

    def one_group(group_index):
        group_key = jax.random.fold_in(key, group_index + 2)
        long_key, cut_key, slot_key, total_key = jax.random.split(group_key, 4)
        longest = jax.random.randint(long_key, (), 13 * GROUP_TOKENS // 16, 15 * GROUP_TOKENS // 16 + 1)
        longest = jnp.where(group_index == full_group, GROUP_TOKENS, longest).astype(jnp.int32)
        remainder = (GROUP_TOKENS - longest).astype(jnp.int32)
        padded_row = (group_index + full_group) % 2 == 1
        short_total = jax.random.randint(total_key, (), 0, jnp.maximum(remainder, 1)).astype(jnp.int32)
        others_total = jnp.where(padded_row, short_total, remainder).astype(jnp.int32)
        cut_points = jnp.sort(jax.random.randint(cut_key, (SLOTS - 1,), 0, others_total + 1)).astype(jnp.int32)
        bound_list = jnp.concatenate([jnp.zeros((1,), jnp.int32), cut_points, others_total[None]])
        pieces = bound_list[1:] - bound_list[:-1]
        chosen = jax.random.randint(slot_key, (), 0, SLOTS)
        places = jnp.arange(SLOTS, dtype=jnp.int32)
        others = pieces[jnp.clip(places - (places > chosen).astype(jnp.int32), 0, SLOTS - 2)]
        return jnp.where(places == chosen, longest, others).astype(jnp.int32)
    return jax.vmap(one_group)(jnp.arange(N_DP, dtype=jnp.int32))


def levels(key, extent, cuts, smallest, top_value):
    def one(axis_at, blocks):
        steps = jax.random.uniform(jax.random.fold_in(jax.random.fold_in(key, 6), axis_at), (blocks,), jnp.float32, smallest / len(cuts), top_value / len(cuts))
        return jnp.repeat(jnp.exp(steps), extent[axis_at] // blocks).reshape((-1,) + (1,) * (len(extent) - axis_at - 1))

    factor_of = one(*cuts[0])
    for cut in cuts[1:]:
        factor_of = factor_of * one(*cut)
    return factor_of


def scatter_about(key, dims, width, reach, cuts=(), held_as=jnp.bfloat16):
    loudness = levels(key, dims, cuts, -0.22, 0.18) if cuts else 1.0
    values = jax.random.normal(key, dims, jnp.float32) * width * loudness
    return jnp.minimum(jnp.maximum(values, -reach), reach).astype(held_as)


def setup_inputs(seed: int = 0) -> dict:
    streams_of = jax.random.split(jax.random.key(seed), 14)
    layer_input = scatter_about(streams_of[0], (TOKENS, D), 1.0, 6.0, ((0, 64), (1, 2)))
    norm1_gain = jnp.clip(1.0 + 0.1 * jax.random.normal(streams_of[1], (D,), jnp.float32), 0.5, 1.5)
    q_weight = scatter_about(streams_of[2], (D, QD), D ** -0.5, 0.15625, ((0, 2), (1, 4)))
    q_bias = scatter_about(streams_of[3], (QD,), 0.5, 3.0, ((0, 4),), jnp.float32)
    kv_weight = scatter_about(streams_of[4], (D, KVD), D ** -0.5, 0.15625, ((0, 2),))
    kv_bias = scatter_about(streams_of[5], (KVD,), 0.5, 3.0, (), jnp.float32)
    o_weight = scatter_about(streams_of[6], (QD, D), (QD // 64) ** -0.5, 1.25, ((0, 4), (1, 2)))
    norm2_gain = jnp.clip(1.0 + 0.1 * jax.random.normal(streams_of[7], (D,), jnp.float32), 0.5, 1.5)
    gate_weight = scatter_about(streams_of[8], (D, FF), D ** -0.5, 0.15625, ((0, 2), (1, 4)))
    up_weight = scatter_about(streams_of[9], (D, FF), D ** -0.5, 0.15625, ((0, 2), (1, 4)))
    down_weight = scatter_about(streams_of[10], (FF, D), FF ** -0.5, 0.0625, ((0, 4), (1, 2)))
    seq_lengths = draw_seq_lengths(jax.random.fold_in(streams_of[13], 71), 0)
    out_grad = scatter_about(streams_of[12], (TOKENS, D), 1.0, 6.0, ((0, 64), (1, 2)))
    return dict(layer_input=layer_input, norm1_gain=norm1_gain, q_weight=q_weight, q_bias=q_bias, kv_weight=kv_weight, kv_bias=kv_bias, o_weight=o_weight, norm2_gain=norm2_gain, gate_weight=gate_weight, up_weight=up_weight, down_weight=down_weight, seq_lengths=seq_lengths, out_grad=out_grad)


EPSILON = 1e-06
THETA = 1000000.0
NEGATIVE = -1e+30

@jax.custom_vjp
def low(v):
    return lax.optimization_barrier(v.astype(jnp.bfloat16)).astype(jnp.float32)

@jax.custom_vjp
def low_back(v):
    return v

def low_keep(v):
    return (low(v), None)

def low_pass(kept, grad):
    return (grad,)

def back_keep(v):
    return (v, None)

def back_low(kept, grad):
    return (low(grad),)
low.defvjp(low_keep, low_pass)
low_back.defvjp(back_keep, back_low)

def layout(lengths):
    places = jnp.arange(GROUP_TOKENS, dtype=jnp.int32)
    endings = jnp.cumsum(lengths).astype(jnp.int32)
    passed = places[:, None] >= endings[None, :]
    segment = lax.optimization_barrier(jnp.sum(passed.astype(jnp.int32), axis=1)).astype(jnp.int32)
    opening = lax.optimization_barrier(jnp.max(jnp.where(passed, endings[None, :], 0), axis=1)).astype(jnp.int32)
    return (segment, places - opening)

def tables(position):
    freqs = THETA ** (-jnp.arange(0, HEAD_SIZE, 2).astype(jnp.float32) / HEAD_SIZE)
    angles = position.astype(jnp.float32)[:, None] * freqs[None, :]
    angles = jnp.concatenate([angles, angles], axis=1)
    return (jnp.cos(angles), jnp.sin(angles))

def rotate(value_rows, cosine, sine):
    half_dim = HEAD_SIZE // 2
    turned = jnp.concatenate([-value_rows[..., half_dim:], value_rows[..., :half_dim]], axis=-1)
    return value_rows * cosine + turned * sine

def rms_norm(value_rows, gain):
    return value_rows * lax.rsqrt(lax.optimization_barrier(jnp.mean(value_rows * value_rows, axis=-1, keepdims=True)) + EPSILON) * gain

def matmul(left, right):
    return jnp.dot(left, right, precision=lax.Precision.HIGHEST)

def forward(inputs, gain_one, weight_query, bias_query, weight_pair, bias_pair, weight_out, gain_two, weight_gate, weight_up, weight_down, segment, position):
    cosine, sine = tables(position)
    cos_heads = cosine[:, None, :]
    sin_heads = sine[:, None, :]
    normed = low(rms_norm(inputs, gain_one))
    query_pre = low_back(matmul(normed, weight_query) + bias_query)
    paired_preactivation = low_back(matmul(normed, weight_pair) + bias_pair)
    queries = low(rotate(query_pre.reshape(GROUP_TOKENS, QUERY_HEADS, HEAD_SIZE), cos_heads, sin_heads))
    key_value_pairs = paired_preactivation.reshape(GROUP_TOKENS, KEY_VALUE_HEADS, 2, HEAD_SIZE)
    key_rows = low(rotate(key_value_pairs[:, :, 0], cos_heads, sin_heads))
    value_rows = low(key_value_pairs[:, :, 1])
    key_rows = jnp.repeat(key_rows, QUERY_HEADS // KEY_VALUE_HEADS, axis=1)
    value_rows = jnp.repeat(value_rows, QUERY_HEADS // KEY_VALUE_HEADS, axis=1)
    scores = low_back(jnp.einsum('qhd,khd->hqk', queries, key_rows, precision=lax.Precision.HIGHEST) * HEAD_SIZE ** (-0.5))
    places = jnp.arange(GROUP_TOKENS)
    allowed = (segment[:, None] == segment[None, :]) & (places[None, :] <= places[:, None])
    scores = jnp.where(allowed[None], scores, NEGATIVE)
    weights_low = low(jax.nn.softmax(scores, axis=-1))
    attended = jnp.einsum('hqk,khd->qhd', weights_low, value_rows, precision=lax.Precision.HIGHEST).reshape(GROUP_TOKENS, QD)
    attended = low_back(low(attended))
    middle = inputs + low_back(matmul(attended, weight_out))
    normed_two = low(rms_norm(middle, gain_two))
    gate = low_back(matmul(normed_two, weight_gate))
    upward = low_back(matmul(normed_two, weight_up))
    hidden = low(jax.nn.silu(gate) * upward)
    return middle + low_back(matmul(hidden, weight_down))

def reference(layer_input, norm1_gain, q_weight, q_bias, kv_weight, kv_bias, o_weight, norm2_gain, gate_weight, up_weight, down_weight, seq_lengths, out_grad):
    params = tuple((item.astype(jnp.float32) for item in (norm1_gain, q_weight, q_bias, kv_weight, kv_bias, o_weight, norm2_gain, gate_weight, up_weight, down_weight)))
    inputs = layer_input.astype(jnp.float32).reshape(N_DP, GROUP_TOKENS, D)
    cotangent = out_grad.astype(jnp.float32).reshape(N_DP, GROUP_TOKENS, D)

    def one_group(running, slices):
        group_inputs, group_cotangent, lengths = slices
        segment, position = layout(lengths)

        def layer(layer_inputs, *layer_params):
            return forward(layer_inputs, *layer_params, segment, position)
        output, pull = jax.vjp(layer, group_inputs, *params)
        grads = pull(group_cotangent)
        summed = tuple((older + fresh for older, fresh in zip(running, grads[1:])))
        return (summed, (output, grads[0]))
    zeros = tuple((jnp.zeros_like(item) for item in params))
    totals, (outputs, input_grads) = lax.scan(one_group, zeros, (inputs, cotangent, seq_lengths))
    return (outputs.reshape(TOKENS, D), input_grads.reshape(TOKENS, D), totals[0], totals[1], totals[2], totals[3], totals[4], totals[5], totals[6], totals[7], totals[8], totals[9])
```

```python
import jax
import jax.numpy as jnp
import numpy as np
from jax import lax
from jax.experimental import pallas as pl
from jax.experimental.pallas import tpu as pltpu
from jax.sharding import PartitionSpec as P

f32 = jnp.float32
bf16 = jnp.bfloat16
MESH = pl.DeviceIdType.MESH
EPSILON = 1e-06
THETA = 1000000.0
NEGATIVE = -1e30
D = 1536
HALF = 768
BLOCK = 256
TOKENS = 1024
COLS = 1152
REAL = 1120
HEADS = 3
HEAD = 128


def dg(left, right, left_dim, right_dim):
    return lax.dot_general(
        left, right, (((left_dim,), (right_dim,)), ((), ())), preferred_element_type=f32
    )


def dot(left, right):
    return jnp.dot(left, right, preferred_element_type=f32)


class Names:
    def __init__(self, pairs):
        self.__dict__.update(pairs)


def rows_of(block, size=BLOCK):
    return pl.ds(pl.multiple_of(block * size, size), size)


class Copy:
    def __init__(self, copy, remote):
        self.copy, self.remote = copy, remote
        self.left = self.came = False
        copy.start()

    def wait_send(self):
        if not self.left:
            self.left = True
            self.copy.wait_send()

    def wait_recv(self):
        if not self.came:
            self.came = True
            self.copy.wait_recv()

    def wait(self):
        if not self.left:
            self.left = True
            self.copy.wait()


class Moves:
    def __init__(self, send, recv, local):
        self.send, self.recv, self.local = send, recv, local
        self.remotes = []
        self.locals = []

    def to(self, device, src, dst):
        i = len(self.remotes)
        copy = Copy(pltpu.make_async_remote_copy(
            src_ref=src, dst_ref=dst, send_sem=self.send.at[i], recv_sem=self.recv.at[i],
            device_id=device, device_id_type=MESH), True)
        self.remotes.append(copy)
        return copy

    def own(self, src, dst):
        copy = Copy(pltpu.make_async_copy(src, dst, self.local.at[len(self.locals)]), False)
        self.locals.append(copy)
        return copy

    out = own

    def settle(self, copies):
        for copy in copies:
            copy.wait_send()

    def finish(self):
        for copy in self.remotes:
            copy.wait_send()
            copy.wait_recv()
        for copy in self.locals:
            copy.wait()


class Place:
    def __init__(self):
        self.gx = lax.axis_index("gx")
        self.gy = lax.axis_index("gy")
        self.up = {"gy": lax.rem(self.gy + 1, 4)}
        self.down = {"gy": lax.rem(self.gy + 3, 4)}
        self.pal = {"gx": 1 - self.gx}
        self.blk = [lax.rem(self.gy + i, 4) for i in range(4)]
        self.cols = pl.ds(pl.multiple_of(self.gx * HALF, 128), HALF)


class GatherY:
    def __init__(self, moves, place, src, buf):
        self.m, self.p, self.src, self.buf = moves, place, src, buf

    def part(self, block, first, count):
        r = pl.ds(pl.multiple_of(block * BLOCK + first, 128), count)
        return self.buf.at[r, self.p.cols]

    def start(self):
        p = self.p
        there = self.part(p.blk[0], 0, BLOCK)
        self.a = self.m.to(p.up, self.src, there)
        self.b = self.m.to(p.down, self.src, there)
        self.c = self.m.to(p.pal, self.src, there)

    def own_ready(self):
        self.c.wait_recv()

    def relay(self):
        p, m = self.p, self.m
        low, high = p.blk[3], p.blk[1]
        self.a.wait_recv()
        x = self.part(low, 0, 128)
        self.d = m.to(p.up, x, x)
        self.b.wait_recv()
        x = self.part(high, 128, 128)
        self.e = m.to(p.down, x, x)
        x = self.part(low, 0, BLOCK)
        self.f = m.to(p.pal, x, x)
        x = self.part(high, 0, BLOCK)
        self.g = m.to(p.pal, x, x)

    def low_ready(self):
        self.f.wait_recv()

    def high_ready(self):
        self.g.wait_recv()

    def relay_pal(self):
        p, m = self.p, self.m
        far = p.blk[2]
        self.d.wait_recv()
        x = self.part(far, 0, 128)
        self.h = m.to(p.pal, x, x)
        self.e.wait_recv()
        x = self.part(far, 128, 128)
        self.i = m.to(p.pal, x, x)

    def far_ready(self):
        self.h.wait_recv()
        self.i.wait_recv()


class ScatterY:
    def __init__(self, moves, place, staged, held, low_half, high_half, from_low, from_high):
        self.m, self.p = moves, place
        self.staged, self.held = staged, held
        self.low_half, self.high_half = low_half, high_half
        self.from_low, self.from_high = from_low, from_high

    def far(self, value):
        p, m = self.p, self.m
        self.staged[0] = value.astype(bf16)
        self.a = m.to(p.up, self.staged.at[0, pl.ds(0, 128)], self.low_half)
        self.b = m.to(p.down, self.staged.at[0, pl.ds(128, 128)], self.high_half)

    def next_up(self, value):
        p, m = self.p, self.m
        self.staged[1, 128:] = value[128:].astype(bf16)
        self.c = m.to(p.up, self.staged.at[1, pl.ds(128, 128)], self.from_low.at[pl.ds(128, 128)])
        self.held[0] = value[:128]

    def next_down(self, value):
        p, m = self.p, self.m
        self.staged[2, :128] = value[:128].astype(bf16)
        self.d = m.to(p.down, self.staged.at[2, pl.ds(0, 128)], self.from_high.at[pl.ds(0, 128)])
        self.held[1] = value[128:]

    def relay(self):
        p, m = self.p, self.m
        self.a.wait_recv()
        self.staged[1, :128] = (self.held[0] + self.low_half[...].astype(f32)).astype(bf16)
        self.e = m.to(p.up, self.staged.at[1, pl.ds(0, 128)], self.from_low.at[pl.ds(0, 128)])
        self.b.wait_recv()
        self.staged[2, 128:] = (self.held[1] + self.high_half[...].astype(f32)).astype(bf16)
        self.f = m.to(p.down, self.staged.at[2, pl.ds(128, 128)], self.from_high.at[pl.ds(128, 128)])

    def result(self, own):
        self.c.wait_recv()
        self.d.wait_recv()
        self.e.wait_recv()
        self.f.wait_recv()
        return own + self.from_low[...].astype(f32) + self.from_high[...].astype(f32)


def enter(devices):
    barrier = pltpu.get_barrier_semaphore()
    for device in devices:
        pl.semaphore_signal(barrier, inc=1, device_id=device, device_id_type=MESH)
    pl.semaphore_wait(barrier, len(devices))


def turned(value, cosine, signed_sine):
    return value * cosine + pltpu.roll(value, 64, 1) * signed_sine


def opening_of(ends, places):
    opening = jnp.zeros_like(places)
    for e in ends:
        opening = jnp.where(places >= e, jnp.maximum(opening, e), opening)
    return opening


def front_body(n):
    m = Moves(n.send, n.recv, n.local)
    front_steps(n, m)
    m.finish()


def front_steps(n, m):
    p = Place()
    gx, gy = p.gx, p.gy

    mine = pl.ds(pl.multiple_of(gx * REAL, 16), REAL)
    theirs = pl.ds(pl.multiple_of((1 - gx) * REAL, 16), REAL)
    weights = ((n.dw, n.Wd, 0), (n.gw, n.Wgu, 0), (n.uw, n.Wgu, COLS))
    loads = [m.own(w.at[mine], W.at[pl.ds(at, REAL), p.cols]) for w, W, at in weights]
    n.g1f[:, p.cols] = jnp.broadcast_to(n.g1[...].reshape(1, HALF), (8, HALF))
    enter([p.up, p.down, p.pal])

    gather_x = GatherY(m, p, n.x, n.xb)
    gather_x.start()
    gain_move = m.to(p.pal, n.g1f.at[:, p.cols], n.g1f.at[:, p.cols])
    pair = p.gy // 2
    pair_cols = pl.ds(pl.multiple_of(pair * 256, 128), 256)
    own_rows = pl.ds(pl.multiple_of(gx * HALF, 128), HALF)
    kv_move = m.to(p.pal, n.kvw.at[:, pair_cols], n.Wkv.at[own_rows])
    q_move = m.to(p.pal, n.qw, n.Wq.at[own_rows])
    o_move = m.to(p.pal, n.ow, n.Wo.at[:, p.cols])

    n.xb[rows_of(gy), p.cols] = n.x[...]
    n.Wkv[own_rows, :] = n.kvw[:, pair_cols]
    n.Wq[own_rows, :] = n.qw[...]
    n.Wo[:, p.cols] = n.ow[...]

    ends = []
    running = jnp.int32(0)
    for k in range(4):
        running = running + n.seq[0, k]
        ends.append(running)
    lane = lax.broadcasted_iota(jnp.int32, (BLOCK, HEAD), 1)

    def table(i):
        places = lax.broadcasted_iota(jnp.int32, (BLOCK, HEAD), 0) + i * BLOCK
        position = places - opening_of(ends, places)
        angles = position.astype(f32) * n.freqs[...]
        r = rows_of(i)
        n.cosT[r, :] = jnp.cos(angles)
        n.sinT[r, :] = jnp.where(lane < 64, -jnp.sin(angles), jnp.sin(angles))

    pl.loop(0, 4)(table)
    m.out(n.cosT, n.cosO)
    m.out(n.sinT, n.sinO)

    gather_x.relay()

    def norm_block(block):
        r = rows_of(block)
        xf = n.xb[r, :].astype(f32)
        inverse = lax.rsqrt(jnp.sum(xf * xf, axis=1, keepdims=True) * (1.0 / D) + EPSILON)
        normed = (xf * inverse * n.g1f[0:1, :]).astype(bf16)
        n.nx[r, :] = normed
        kv = dot(normed, n.Wkv[...]) + n.kvb[pair_cols].reshape(1, 256)
        n.K[r, :] = turned(kv[:, :HEAD], n.cosT[r, :], n.sinT[r, :]).astype(bf16)
        n.V[r, :] = kv[:, HEAD:].astype(bf16)
        return inverse

    gain_move.wait_recv()
    kv_move.wait_recv()
    gather_x.own_ready()
    inverse = norm_block(p.blk[0])
    n.r1T[...] = jnp.broadcast_to(inverse, (BLOCK, HEAD))
    m.out(n.r1T, n.r1)
    gather_x.low_ready()
    norm_block(p.blk[3])
    gather_x.high_ready()
    norm_block(p.blk[1])
    gather_x.relay_pal()
    gather_og = GatherY(m, p, n.og, n.ogb)
    gather_og.start()
    weight_moves = [m.to(p.pal, w.at[theirs], W.at[pl.ds(at, REAL), p.cols]) for w, W, at in weights]
    n.ogb[rows_of(gy), p.cols] = n.og[...]
    for _, W, at in weights:
        W[at + REAL:at + COLS, :] = jnp.zeros((COLS - REAL, D), bf16)
    gather_x.far_ready()
    norm_block(p.blk[2])
    m.out(n.nx.at[:, p.cols], n.nxO)
    m.out(n.K, n.KO)
    m.out(n.V, n.VO)

    q_move.wait_recv()
    own_blocks = [gx, 3 - gx]
    for i, b in enumerate(own_blocks):
        r = rows_of(b)
        q = dot(n.nx[r, :], n.Wq[...]) + n.qb[...].reshape(1, 384)
        for h in range(HEADS):
            c = slice(h * HEAD, (h + 1) * HEAD)
            n.Q[i * BLOCK:(i + 1) * BLOCK, c] = turned(q[:, c], n.cosT[r, :], n.sinT[r, :]).astype(bf16)
    m.out(n.Q, n.QO)

    def attention(i, h):
        b = own_blocks[i]
        keys = 512 * (i + 1)
        at = 512 * i
        c = slice(h * HEAD, (h + 1) * HEAD)
        s = dg(n.Q[i * BLOCK:(i + 1) * BLOCK, c], n.K[:keys, :], 1, 1) * HEAD ** (-0.5)
        query = lax.broadcasted_iota(jnp.int32, (BLOCK, 1), 0) + b * BLOCK
        opening = opening_of(ends, query)
        key = lax.broadcasted_iota(jnp.int32, (BLOCK, keys), 1)
        s = jnp.where((key >= opening) & (key <= query), s, NEGATIVE)
        e = jnp.exp(s - jnp.max(s, axis=1, keepdims=True))
        probs = (e / jnp.sum(e, axis=1, keepdims=True)).astype(bf16)
        n.Pr[h * BLOCK:(h + 1) * BLOCK, at:at + keys] = probs
        out = dot(probs, n.V[:keys, :])
        n.att[rows_of(b), c] = out.astype(bf16)

    att_moves = []
    for i in (1, 0):
        for h in range(HEADS):
            attention(i, h)
        b = rows_of(own_blocks[i])
        att_moves.append(m.to(p.pal, n.att.at[b], n.att.at[b]))
        if i == 1:
            gather_og.relay()
    m.out(n.Pr, n.PO)
    gather_og.own_ready()
    loads[0].wait()
    weight_moves[0].wait_recv()

    def hidden_grad(block):
        r = rows_of(block)
        n.HG[r, :] = dg(n.ogb[r, :], n.Wd[...], 1, 1)

    for copy in att_moves:
        copy.wait_recv()

    m.settle([gather_x.a, gather_x.b, gather_x.c, gather_x.d, gather_x.e, gather_x.f, gather_x.g, gather_x.h, gather_x.i])

    def out_part(block):
        return dot(n.att[rows_of(block), :], n.ow[...])

    rs = ScatterY(m, p, n.staged, n.held, n.low_half, n.high_half, n.from_low, n.from_high)
    rs.far(out_part(p.blk[2]))
    rs.next_up(out_part(p.blk[1]))
    rs.next_down(out_part(p.blk[3]))
    n.mid[...] = out_part(p.blk[0]) + n.x[...].astype(f32)
    m.out(n.att, n.attO)
    gather_og.relay_pal()
    rs.relay()
    hidden_grad(p.blk[0])
    gather_og.low_ready()
    hidden_grad(p.blk[3])
    gather_og.high_ready()
    hidden_grad(p.blk[1])
    n.mid[...] = rs.result(n.mid[...])
    m.out(n.mid, n.midO)
    mid = n.mid[...]
    n.sums[0] = jnp.broadcast_to(jnp.sum(mid * mid, axis=1, keepdims=True), (BLOCK, HEAD))
    sum_move = m.to(p.pal, n.sums.at[0], n.sums.at[1])
    sum_move.wait_recv()
    r2 = lax.rsqrt((n.sums[0] + n.sums[1]) * (1.0 / D) + EPSILON)
    n.r2T[...] = r2
    m.out(n.r2T, n.r2)
    n.nto[...] = (n.mid[...] * r2[:, :1] * n.g2[...].reshape(1, HALF)).astype(bf16)
    gather_n = GatherY(m, p, n.nto, n.xb)
    gather_n.start()
    n.xb[rows_of(gy), p.cols] = n.nto[...]
    gather_og.far_ready()
    hidden_grad(p.blk[2])
    for k in (1, 2):
        loads[k].wait()
        weight_moves[k].wait_recv()
    m.out(n.Wgu, n.WguO)
    m.out(n.Wd, n.WdO)

    def feed_forward(block):
        r = rows_of(block)
        a = n.xb[r, :]
        gate = dg(a, n.Wgu[:COLS, :], 1, 1)
        upward = dg(a, n.Wgu[COLS:, :], 1, 1)
        back = n.HG[r, :]
        sg = jax.nn.sigmoid(gate)
        gs = gate * sg
        n.hid[r, :] = (gs * upward).astype(bf16)
        n.gu[r, :COLS] = (back * upward * sg * (1.0 + gate * (1.0 - sg))).astype(bf16)
        n.gu[r, COLS:] = (back * gs).astype(bf16)

    gather_n.own_ready()
    feed_forward(p.blk[0])
    gather_n.relay()
    gather_n.low_ready()
    feed_forward(p.blk[3])
    gather_n.high_ready()
    feed_forward(p.blk[1])
    gather_n.relay_pal()
    gather_n.far_ready()
    feed_forward(p.blk[2])
    m.out(n.hid, n.hidO)
    m.out(n.gu, n.guO)

    for k, (left, at, right) in enumerate(((n.hid, 0, n.ogb), (n.gu, 0, n.xb), (n.gu, COLS, n.xb))):
        @pl.loop(0, 4)
        def _(i, left=left, at=at, right=right, k=k):
            c = pl.ds(pl.multiple_of(i * BLOCK + at, 128), BLOCK)
            r = pl.ds(pl.multiple_of(i * BLOCK + k * REAL, 32), BLOCK)
            n.Gs[r, :] = dg(left[:, c], right[...], 0, 0).astype(bf16)

        tail = dg(left[:, at + 4 * BLOCK:at + COLS], right[...], 0, 0).astype(bf16)
        n.Gs[k * REAL + 4 * BLOCK:(k + 1) * REAL, :] = tail[:REAL - 4 * BLOCK]
        r = pl.ds(k * REAL, REAL)
        m.out(n.Gs.at[r], n.GO.at[r])

    o_move.wait_recv()
    m.out(n.Wo, n.WoO)


def kernel_call(name, body, inputs, outputs, scratch, collective_id, flops=0, moved=0):
    order = list(inputs) + list(outputs) + list(scratch)

    def kernel(*refs):
        body(Names(dict(zip(order, refs))))

    results = pl.pallas_call(
        kernel,
        out_shape=tuple(jax.ShapeDtypeStruct(s, d) for s, d, _ in outputs.values()),
        in_specs=[pl.BlockSpec(memory_space=s) for _, s in inputs.values()],
        out_specs=tuple(pl.BlockSpec(memory_space=s) for _, _, s in outputs.values()),
        scratch_shapes=list(scratch.values()),
        compiler_params=pltpu.CompilerParams(
            collective_id=collective_id, has_side_effects=True, vmem_limit_bytes=62 * 2**20),
        cost_estimate=pl.CostEstimate(flops=flops, bytes_accessed=moved, transcendentals=0),
        name=name,
    )(*[a for a, _ in inputs.values()])
    return Names(dict(zip(outputs, results)))


def frequencies():
    freqs = np.float32(THETA) ** (-np.arange(0, HEAD, 2, dtype=np.float32) / np.float32(HEAD))
    return np.concatenate([freqs, freqs])[None, :]


def front(layer_input, norm1_gain, q_weight, q_bias, kv_weight, kv_bias, o_weight, norm2_gain,
          gate_weight, up_weight, down_weight, seq_lengths, out_grad):
    vm, hbm, sm = pltpu.VMEM, pl.ANY, pltpu.SMEM
    inputs = dict(
        x=(layer_input, vm), og=(out_grad, vm), g1=(norm1_gain, vm), g2=(norm2_gain, vm),
        qw=(q_weight, vm), qb=(q_bias, vm), kvw=(kv_weight, vm), kvb=(kv_bias, vm),
        ow=(o_weight, vm), gw=(gate_weight.T, hbm), uw=(up_weight.T, hbm), dw=(down_weight, hbm),
        seq=(seq_lengths, sm), freqs=(frequencies(), vm))
    outputs = dict(
        GO=((3 * REAL, D), bf16, hbm),
        hidO=((TOKENS, COLS), bf16, hbm), guO=((TOKENS, 2 * COLS), bf16, hbm),
        WguO=((2 * COLS, D), bf16, hbm), WdO=((COLS, D), bf16, hbm),
        midO=((BLOCK, HALF), f32, hbm), r1=((BLOCK, HEAD), f32, hbm), r2=((BLOCK, HEAD), f32, hbm),
        attO=((TOKENS, 384), bf16, hbm), PO=((HEADS * BLOCK, 1536), bf16, hbm), QO=((512, 384), bf16, hbm),
        KO=((TOKENS, HEAD), bf16, hbm), VO=((TOKENS, HEAD), bf16, hbm),
        cosO=((TOKENS, HEAD), f32, hbm), sinO=((TOKENS, HEAD), f32, hbm), nxO=((TOKENS, HALF), bf16, hbm),
        WoO=((384, D), bf16, hbm))
    v = pltpu.VMEM
    scratch = dict(
        Wgu=v((2 * COLS, D), bf16), Wd=v((COLS, D), bf16),
        Wkv=v((D, 256), bf16), Wq=v((D, 384), bf16), Wo=v((384, D), bf16), g1f=v((8, D), f32),
        xb=v((TOKENS, D), bf16), nx=v((TOKENS, D), bf16), ogb=v((TOKENS, D), bf16),
        cosT=v((TOKENS, HEAD), f32), sinT=v((TOKENS, HEAD), f32),
        K=v((TOKENS, HEAD), bf16), V=v((TOKENS, HEAD), bf16), Q=v((512, 384), bf16),
        Pr=v((HEADS * BLOCK, 1536), bf16), att=v((TOKENS, 384), bf16),
        staged=v((3, BLOCK, HALF), bf16), held=v((2, 128, HALF), f32),
        low_half=v((128, HALF), bf16), high_half=v((128, HALF), bf16),
        from_low=v((BLOCK, HALF), bf16), from_high=v((BLOCK, HALF), bf16),
        mid=v((BLOCK, HALF), f32), sums=v((2, BLOCK, HEAD), f32), r1T=v((BLOCK, HEAD), f32),
        r2T=v((BLOCK, HEAD), f32), nto=v((BLOCK, HALF), bf16),
        HG=v((TOKENS, COLS), f32), hid=v((TOKENS, COLS), bf16), gu=v((TOKENS, 2 * COLS), bf16),
        Gs=v((3 * REAL, D), bf16),
        send=pltpu.SemaphoreType.DMA((48,)), recv=pltpu.SemaphoreType.DMA((48,)),
        local=pltpu.SemaphoreType.DMA((48,)))
    return kernel_call("front", front_body, inputs, outputs, scratch, 1, flops=30 * 10**9, moved=60 * 2**20)


UNITS = (4, 5, 4)
LEFT = 3328
SCALE = HEAD ** (-0.5)


class Ring:
    def __init__(self, place, along_x):
        z, x = place.z, place.x
        if isinstance(along_x, bool):
            c = x if along_x else z
            ids = [z * 4 + lax.rem(x + s, 4) if along_x else lax.rem(z + s, 4) * 4 + x for s in (1, 3)]
        else:
            c = jnp.where(along_x, x, z)
            ids = [jnp.where(along_x, z * 4 + lax.rem(x + s, 4), lax.rem(z + s, 4) * 4 + x) for s in (1, 3)]
        self.c, self.up, self.down = c, {"dp": ids[0]}, {"dp": ids[1]}
        self.next, self.far, self.last = [lax.rem(c + s, 4) for s in (1, 2, 3)]


def scatter_sum(m, ring, src, base, own, out, a, s1, s2, w):
    low, high = slice(0, w), slice(w, None)
    k1 = m.to(ring.up, src(ring.far, low), s1[0])
    k2 = m.to(ring.down, src(ring.far, high), s1[1])
    k3 = m.to(ring.up, src(ring.next, high), s2[0].at[:, w:])
    k4 = m.to(ring.down, src(ring.last, low), s2[1].at[:, :w])
    yield
    k1.wait_recv()
    a[0][...] = (base(0).astype(f32) + s1[0][...].astype(f32)).astype(bf16)
    k5 = m.to(ring.up, a[0], s2[0].at[:, :w])
    k2.wait_recv()
    a[1][...] = (base(1).astype(f32) + s1[1][...].astype(f32)).astype(bf16)
    k6 = m.to(ring.down, a[1], s2[1].at[:, w:])
    yield
    for k in (k3, k4, k5, k6):
        k.wait_recv()
    out[...] = (own().astype(f32) + s2[0][...].astype(f32) + s2[1][...].astype(f32)).astype(bf16)
    yield


def gather_ring(m, ring, part):
    k1 = m.to(ring.up, part(ring.c, None), part(ring.c, None))
    k2 = m.to(ring.down, part(ring.c, None), part(ring.c, None))
    yield
    k1.wait_recv()
    x = part(ring.last, 0)
    k3 = m.to(ring.up, x, x)
    k2.wait_recv()
    x = part(ring.next, 1)
    k4 = m.to(ring.down, x, x)
    yield
    k3.wait_recv()
    k4.wait_recv()
    yield


def aligned(start, size, unit=16):
    return pl.ds(pl.multiple_of(start, unit), size)


def main_piece(n, m, p, i):
    k = UNITS[i]
    base = 256 * sum(UNITS[:i])
    r1, r2 = 64 * k, 16 * k
    own, a, s1, s2 = (getattr(n, f"{name}{i}") for name in ("own", "a", "s1", "s2"))
    b, t1, t2, T2 = (getattr(n, f"{name}{i}") for name in ("b", "t1", "t2", "T"))
    rings = [Ring(p, True), Ring(p, False)]
    loads = []
    first, second = [], []
    for h in range(2):
        one, two = rings[h], rings[1 - h]

        def src(j, lanes, h=h):
            lo, hi = lanes.start + h * HALF, (lanes.stop or HALF) + h * HALF
            return n.G.at[aligned(base + j * r1, r1, 64), pl.ds(lo, hi - lo)]

        loads.append([m.own(src(one.c, slice(0, HALF)), own.at[h]),
                      m.own(src(one.next, slice(0, 384)), a.at[h, 0]),
                      m.own(src(one.last, slice(384, HALF)), a.at[h, 1])])
        first.append(scatter_sum(
            m, one, src, lambda d, h=h: a[h, d], lambda h=h: own[h], own.at[h],
            [a.at[h, 0], a.at[h, 1]], [s1.at[h, 0], s1.at[h, 1]], [s2.at[h, 0], s2.at[h, 1]], 384))

        def src2(j, lanes, h=h):
            return own.at[h, aligned(j * r2, r2), pl.ds(lanes.start, (lanes.stop or HALF) - lanes.start)]

        def base2(d, h=h, two=two):
            if d == 0:
                return own[h, aligned(two.next * r2, r2), :384]
            return own[h, aligned(two.last * r2, r2), 384:]

        second.append(scatter_sum(
            m, two, src2, base2, lambda h=h, two=two: own[h, aligned(two.c * r2, r2), :], T2.at[h],
            [b.at[h, 0], b.at[h, 1]], [t1.at[h, 0], t1.at[h, 1]], [t2.at[h, 0], t2.at[h, 1]], 384))
    yield
    for g in first:
        next(g)
    yield
    for l in loads:
        for c in l:
            c.wait()
    for g in first:
        next(g)
    yield
    for g, g2 in zip(first, second):
        next(g)
        next(g2)
    yield
    for g in second:
        next(g)
    yield
    for g in second:
        next(g)
    one = Ring(p, p.gx == 0)
    two = Ring(p, p.gx != 0)

    def place(c1, c2, rows):
        return aligned(base + c1 * r1 + c2 * r2, rows)

    there = (Ring(p, p.gx != 0), Ring(p, p.gx == 0))
    mine = m.own(T2.at[p.gx], n.O.at[p.gx, place(one.c, two.c, r2)])
    swap = m.to(p.pal, T2.at[1 - p.gx], n.O.at[p.gx, place(there[0].c, there[1].c, r2)])
    yield
    mine.wait()
    swap.wait_recv()

    def part_two(j, half):
        r = place(one.c, j, r2)
        return n.O.at[:, r] if half is None else n.O.at[half, r]

    def part_one(j, half):
        r = place(j, jnp.int32(0), r1)
        return n.O.at[:, r] if half is None else n.O.at[half, r]

    g = gather_ring(m, two, part_two)
    next(g)
    yield
    next(g)
    yield
    next(g)
    g = gather_ring(m, one, part_one)
    next(g)
    yield
    next(g)
    yield
    next(g)
    yield


def small_piece(n, m, p):
    rings = [Ring(p, True), Ring(p, False)]
    r1, r2, W = 256, 64, 384
    first, second = [], []
    for h in range(2):
        one, two = rings[h], rings[1 - h]
        w = (256, 128)[h]
        a, s1, b, t1 = ([getattr(n, f"{name}m{h}{d}") for d in range(2)] for name in ("a", "s1", "b", "t1"))
        s2, t2 = ([getattr(n, f"{name}m").at[h, d] for d in range(2)] for name in ("s2", "t2"))

        def src(j, lanes, h=h):
            lo, hi = lanes.start + h * W, (lanes.stop or W) + h * W
            return n.M.at[aligned(j * r1, r1), pl.ds(lo, hi - lo)]

        def base1(d, h=h, one=one, w=w):
            if d == 0:
                return n.M[aligned(one.next * r1, r1), h * W:h * W + w]
            return n.M[aligned(one.last * r1, r1), h * W + w:(h + 1) * W]

        first.append(scatter_sum(
            m, one, src, base1, lambda h=h, one=one: n.M[aligned(one.c * r1, r1), h * W:(h + 1) * W],
            n.Tm.at[h], a, s1, s2, w))

        def src2(j, lanes, h=h):
            return n.Tm.at[h, aligned(j * r2, r2), pl.ds(lanes.start, (lanes.stop or W) - lanes.start)]

        def base2(d, h=h, two=two, w=w):
            if d == 0:
                return n.Tm[h, aligned(two.next * r2, r2), :w]
            return n.Tm[h, aligned(two.last * r2, r2), w:]

        second.append(scatter_sum(
            m, two, src2, base2, lambda h=h, two=two: n.Tm[h, aligned(two.c * r2, r2), :], n.Um.at[h],
            b, t1, t2, w))
    for g in first:
        next(g)
    yield
    for g in first:
        next(g)
    yield
    for g, g2 in zip(first, second):
        next(g)
        next(g2)
    yield
    for g in second:
        next(g)
    yield
    for g in second:
        next(g)
    mine = []
    for h in range(2):
        one, two = rings[h], rings[1 - h]
        mine.append(m.own(n.Um.at[h], n.O4.at[aligned(one.c * r1 + two.c * r2, r2), pl.ds(h * W, W)]))
    yield
    gathers = []
    for h in range(2):
        one, two = rings[h], rings[1 - h]
        mine[h].wait()

        def part(j, half, h=h, one=one):
            at, rows = (0, r2) if half is None else (half * r2 // 2, r2 // 2)
            return n.O4.at[aligned(one.c * r1 + j * r2 + at, rows), pl.ds(h * W, W)]

        gathers.append(gather_ring(m, two, part))
        next(gathers[h])
    yield
    for g in gathers:
        next(g)
    yield
    for h in range(2):
        next(gathers[h])

        def part(j, half, h=h):
            at, rows = (0, r1) if half is None else (half * r1 // 2, r1 // 2)
            return n.O4.at[aligned(j * r1 + at, rows), pl.ds(h * W, W)]

        gathers[h] = gather_ring(m, rings[h], part)
        next(gathers[h])
    yield
    for g in gathers:
        next(g)
    yield
    for g in gathers:
        next(g)
    block = pl.ds(832, 144)
    far = {"gy": lax.rem(p.gy + 2, 4)}
    moves = [m.to(d, n.O4.at[block], n.Oy.at[p.gy]) for d in (p.up, p.down, far)]
    rest = [m.own(n.O4.at[block], n.Oy.at[p.gy])]
    for core in range(2):
        rest.append(m.own(n.O4.at[pl.ds(768 + 32 * core, 32)], n.O.at[core, pl.ds(LEFT, 32)]))
    yield
    for c in moves:
        c.wait_recv()
    for c in rest:
        c.wait()
    yield


def back_body(n):
    m = Moves(n.send, n.recv, n.local)
    back_steps(n, m)
    m.finish()


def back_steps(n, m):
    p = Place()
    dp = lax.axis_index("dp")
    p.z, p.x = lax.div(dp, 4), lax.rem(dp, 4)
    gx, gy = p.gx, p.gy
    pal_cols = pl.ds(pl.multiple_of((1 - gx) * HALF, 128), HALF)
    vm = Names({})
    load = {}

    def bring(name, src, dst):
        load[name] = m.own(src, dst)

    bring("gu", n.gu, n.guV)
    bring("Wgu", n.Wgu, n.WguV)
    bring("mid", n.mid, n.midV)
    bring("r2", n.r2, n.r2V)
    rings = [Ring(p, True), Ring(p, False)]
    gens = {str(i): main_piece(n, m, p, i) for i in range(3)}
    for i in range(3):
        next(gens[str(i)])
    for name in ("att", "Q", "K", "V", "cos", "sin", "nx", "Wo", "r1"):
        bring(name, getattr(n, name), getattr(n, name + "V"))
    left_row = aligned(768 + gx * 32, 32, 32)
    bring("left", n.G.at[pl.ds(LEFT, 32), p.cols], n.M.at[left_row])

    enter([p.up, p.down, p.pal, rings[0].up, rings[0].down, rings[1].up, rings[1].down])

    def ar(names):
        for name in names:
            next(gens[name], None)

    ar("01")
    left_move = m.to(p.pal, n.G.at[pl.ds(LEFT, 32), pal_cols], n.M.at[left_row])

    load["gu"].wait()
    load["Wgu"].wait()

    def two_sided(left, weight, take, give, held, names):
        order = (2, 1, 3, 0)
        moves = []
        for k, which in enumerate(order):
            r = rows_of(p.blk[which])
            if k >= 2:
                moves[k - 2].wait_send()
            give[k % 2] = dot(left(r), weight(pal_cols)).astype(bf16)
            moves.append(m.to(p.pal, give.at[k % 2], take.at[k]))
            held[k % 2] = dot(left(r), weight(p.cols))
            if k:
                moves[k - 1].wait_recv()
                yield held[(k - 1) % 2] + take[k - 1].astype(f32)
            ar(names[k])
        moves[3].wait_recv()
        moves[2].wait_send()
        moves[3].wait_send()
        yield held[1] + take[3].astype(f32)

    def scatter(letter):
        return ScatterY(m, p, n.staged, n.held, *(getattr(n, letter + name) for name in ("low", "high", "flow", "fhigh")))

    g = two_sided(lambda r: n.guV[r, :], lambda c: n.WguV[:, c], n.take, n.give, n.two, ("", "0", "1", ""))
    rs = scatter("A")
    rs.far(next(g))
    rs.next_up(next(g))
    rs.next_down(next(g))
    n.part[...] = next(g)
    ar("2")
    bring("hid", n.hid, n.guV.at[:, pl.ds(0, COLS)])
    bring("Wd", n.Wd, n.WguV.at[pl.ds(0, COLS)])
    bring("P", n.P, n.WguV.at[pl.ds(COLS, HEADS * BLOCK)])
    rs.relay()
    ar("01")
    n.part[...] = rs.result(n.part[...])
    load["mid"].wait()
    load["r2"].wait()
    r2 = n.r2V[:, :1]
    y2 = n.midV[...] * r2
    w2 = n.part[...] * n.g2[...].reshape(1, HALF)
    n.gain2[...] = jnp.broadcast_to(jnp.sum(n.part[...] * y2, axis=0, keepdims=True), (8, HALF))
    n.sums[0] = jnp.broadcast_to(jnp.sum(w2 * y2, axis=1, keepdims=True), (BLOCK, HEAD))
    sum_move = m.to(p.pal, n.sums.at[0], n.sums.at[1])
    sum_move.wait_recv()
    total = (n.sums[0] + n.sums[1])[:, :1] * (1.0 / D)
    n.mg[...] = n.og[...].astype(f32) + r2 * (w2 - y2 * total)
    n.mlo[...] = n.mg[...].astype(bf16)
    gather = GatherY(m, p, n.mlo, n.ml)
    gather.start()
    n.ml[rows_of(gy), p.cols] = n.mlo[...]
    ar("2")

    load["hid"].wait()
    load["Wd"].wait()
    g = two_sided(lambda r: n.guV[r, :COLS], lambda c: n.WguV[:COLS, c], n.take, n.give, n.two, ("0", "", "1", ""))
    n.far_part[...] = next(g)
    n.up_part[...] = next(g)
    n.down_part[...] = next(g)
    n.part[...] = next(g) + n.midV[...]
    gather.relay()
    ar("2")
    gather.relay_pal()
    m.settle([rs.a, rs.b, rs.c, rs.d, rs.e, rs.f])
    rs = scatter("B")
    rs.far(n.far_part[...])
    rs.next_up(n.up_part[...])
    rs.next_down(n.down_part[...])
    gather.own_ready()
    gather.low_ready()
    gather.high_ready()
    ar("01")

    for name in ("att", "Q", "K", "V", "cos", "sin", "nx", "Wo", "r1", "P", "left"):
        load[name].wait()
    gather.far_ready()
    n.M[0:384, :] = dg(n.attV[...], n.ml[:, p.cols], 0, 0).astype(bf16)
    own_blocks = [gx, 3 - gx]
    q_moves = []
    for i in (1, 0):
        b = rows_of(own_blocks[i])
        keys, at = 512 * (i + 1), 512 * i
        n.ag[...] = dg(n.ml[b, :], n.WoV[...], 1, 1).astype(bf16)
        for h in range(HEADS):
            c = slice(h * HEAD, (h + 1) * HEAD)
            probs = n.WguV[COLS + h * BLOCK:COLS + (h + 1) * BLOCK, at:at + keys]
            probs_f = probs.astype(f32)
            prob_grads = dg(n.ag[:, c], n.VV[:keys, :], 1, 1)
            centre = jnp.sum(probs_f * prob_grads, axis=1, keepdims=True)
            score_grads = (probs_f * (prob_grads - centre)).astype(bf16)
            dq = dot(score_grads, n.KV[:keys, :]) * SCALE
            dk = dg(score_grads, n.QV[i * BLOCK:(i + 1) * BLOCK, c], 0, 0) * SCALE
            dv = dg(probs, n.ag[:, c], 0, 0)
            if i == 1 and h == 0:
                n.dkv[:, :HEAD] = dk
                n.dkv[:, HEAD:] = dv
            else:
                n.dkv[:keys, :HEAD] += dk
                n.dkv[:keys, HEAD:] += dv
            n.ql[b, c] = turned(dq, n.cosV[b, :], -n.sinV[b, :]).astype(bf16)
        q_moves.append(m.to(p.pal, n.ql.at[b], n.ql.at[b]))
        ar("2" if i == 1 else "0")
        if i == 1:
            rs.relay()
    n.S[0] = n.dkv[...].astype(bf16)
    s_move = m.to(p.pal, n.S.at[0], n.S.at[1])
    n.block_out[...] = rs.result(n.part[...])
    s_move.wait_recv()
    both = n.S[0].astype(f32) + n.S[1].astype(f32)
    n.dkv[...] = both
    n.S2[...] = both.astype(bf16)
    odd = lax.rem(gy, 2)
    pair = {"gy": gy + 1 - 2 * odd}
    pair_move = m.to(pair, n.S2.at[:, pl.ds(pl.multiple_of((1 - odd) * HEAD, HEAD), HEAD)], n.pin)
    ar("12")
    for copy in q_moves:
        copy.wait_recv()
    n.M[384:768, :] = dg(n.ql[...], n.nxV[...], 0, 0).astype(bf16)
    pair_move.wait_recv()
    kv = n.dkv[:, pl.ds(pl.multiple_of(odd * HEAD, HEAD), HEAD)] + n.pin[...].astype(f32)
    is_key = (1 - odd).astype(f32)
    cosine = n.cosV[...] * is_key + (1.0 - is_key)
    sine = n.sinV[...] * is_key
    n.plow[...] = turned(kv, cosine, -sine).astype(bf16)
    n.M[832:960, :] = dg(n.plow[...], n.nxV[...], 0, 0).astype(bf16)
    ar("0")

    def norm_one_part(block):
        r = rows_of(block)
        kvw = n.kvw[:, pl.ds(pl.multiple_of(gy * HEAD, HEAD), HEAD)]
        return dg(n.ql[r, :], n.qw[...], 1, 1) + dg(n.plow[r, :], kvw, 1, 1)

    m.settle([rs.a, rs.b, rs.c, rs.d, rs.e, rs.f])
    rs = scatter("A")
    rs.far(norm_one_part(p.blk[2]))
    rs.next_up(norm_one_part(p.blk[1]))
    rs.next_down(norm_one_part(p.blk[3]))
    n.part[...] = norm_one_part(p.blk[0])
    ar("12")
    rs.relay()
    ar("0")
    n.part[...] = rs.result(n.part[...])
    r1 = n.r1V[:, :1]
    y1 = n.x[...].astype(f32) * r1
    w1 = n.part[...] * n.g1[...].reshape(1, HALF)
    gain1 = jnp.sum(n.part[...] * y1, axis=0, keepdims=True)
    m.settle([sum_move])
    n.sums[0] = jnp.broadcast_to(jnp.sum(w1 * y1, axis=1, keepdims=True), (BLOCK, HEAD))
    sum_move = m.to(p.pal, n.sums.at[0], n.sums.at[2])
    bias = jnp.concatenate([
        jnp.sum(n.ql[...].astype(f32), axis=0, keepdims=True),
        jnp.sum(n.plow[...].astype(f32), axis=0, keepdims=True),
        jnp.zeros((1, 256), f32)], axis=1)
    row = lax.broadcasted_iota(jnp.int32, (64, HALF), 0)
    vectors = jnp.where(row == 0, gain1, jnp.where(row == 1, n.gain2[0:1, :], jnp.where(row == 2, bias, 0.0)))
    n.M[960:, :] = vectors.astype(bf16)
    left_move.wait_recv()
    gens["m"] = small_piece(n, m, p)
    ar("m1")
    sum_move.wait_recv()
    total = (n.sums[0] + n.sums[2])[:, :1] * (1.0 / D)
    n.input_grad[...] = n.mg[...] + r1 * (w1 - y1 * total)
    for _ in range(14):
        ar("2m01")


def back(f, layer_input, norm1_gain, q_weight, kv_weight, norm2_gain, out_grad):
    vm, hbm = pltpu.VMEM, pl.ANY
    inputs = dict(
        x=(layer_input, vm), og=(out_grad, vm), g1=(norm1_gain, vm), g2=(norm2_gain, vm),
        qw=(q_weight, vm), kvw=(kv_weight, vm),
        G=(f.GO, hbm), gu=(f.guO, hbm), Wgu=(f.WguO, hbm), hid=(f.hidO, hbm), Wd=(f.WdO, hbm), mid=(f.midO, hbm),
        r1=(f.r1, hbm), r2=(f.r2, hbm), att=(f.attO, hbm), P=(f.PO, hbm), Q=(f.QO, hbm), K=(f.KO, hbm),
        V=(f.VO, hbm), cos=(f.cosO, hbm), sin=(f.sinO, hbm), nx=(f.nxO, hbm), Wo=(f.WoO, hbm))
    outputs = dict(
        block_out=((BLOCK, HALF), f32, vm), input_grad=((BLOCK, HALF), f32, vm),
        O=((2, 3 * REAL, HALF), bf16, hbm), O4=((TOKENS, HALF), bf16, hbm), Oy=((4, 144, HALF), bf16, hbm))
    v = pltpu.VMEM
    scratch = dict(
        guV=v((TOKENS, 2 * COLS), bf16), WguV=v((2 * COLS, D), bf16), midV=v((BLOCK, HALF), f32),
        r1V=v((BLOCK, HEAD), f32), r2V=v((BLOCK, HEAD), f32), attV=v((TOKENS, 384), bf16), QV=v((512, 384), bf16),
        KV=v((TOKENS, HEAD), bf16), VV=v((TOKENS, HEAD), bf16), cosV=v((TOKENS, HEAD), f32),
        sinV=v((TOKENS, HEAD), f32), nxV=v((TOKENS, HALF), bf16), WoV=v((384, D), bf16),
        take=v((4, BLOCK, HALF), bf16), give=v((2, BLOCK, HALF), bf16), two=v((2, BLOCK, HALF), f32),
        staged=v((3, BLOCK, HALF), bf16), held=v((2, 128, HALF), f32),
        part=v((BLOCK, HALF), f32), far_part=v((BLOCK, HALF), f32), up_part=v((BLOCK, HALF), f32),
        down_part=v((BLOCK, HALF), f32), gain2=v((8, HALF), f32), sums=v((3, BLOCK, HEAD), f32),
        mg=v((BLOCK, HALF), f32), mlo=v((BLOCK, HALF), bf16), ml=v((TOKENS, D), bf16),
        ag=v((BLOCK, 384), bf16), dkv=v((TOKENS, 256), f32), ql=v((TOKENS, 384), bf16), S=v((2, TOKENS, 256), bf16),
        S2=v((TOKENS, 256), bf16), pin=v((TOKENS, HEAD), bf16), plow=v((TOKENS, HEAD), bf16), M=v((TOKENS, HALF), bf16),
        s2m=v((2, 2, 256, 384), bf16), Tm=v((2, 256, 384), bf16), t2m=v((2, 2, 64, 384), bf16), Um=v((2, 64, 384), bf16))
    for letter in "AB":
        scratch.update({letter + "low": v((128, HALF), bf16), letter + "high": v((128, HALF), bf16),
                        letter + "flow": v((BLOCK, HALF), bf16), letter + "fhigh": v((BLOCK, HALF), bf16)})
    for h in range(2):
        for d in range(2):
            w = (256, 128)[(h + d) % 2]
            scratch.update({f"am{h}{d}": v((256, w), bf16), f"s1m{h}{d}": v((256, w), bf16),
                            f"bm{h}{d}": v((64, w), bf16), f"t1m{h}{d}": v((64, w), bf16)})
    for i, k in enumerate(UNITS):
        r1, r2 = 64 * k, 16 * k
        scratch.update({
            f"own{i}": v((2, r1, HALF), bf16), f"a{i}": v((2, 2, r1, 384), bf16), f"s1{i}": v((2, 2, r1, 384), bf16),
            f"s2{i}": v((2, 2, r1, HALF), bf16), f"b{i}": v((2, 2, r2, 384), bf16), f"t1{i}": v((2, 2, r2, 384), bf16),
            f"t2{i}": v((2, 2, r2, HALF), bf16), f"T{i}": v((2, r2, HALF), bf16)})
    scratch.update(send=pltpu.SemaphoreType.DMA((200,)), recv=pltpu.SemaphoreType.DMA((200,)),
                   local=pltpu.SemaphoreType.DMA((64,)))
    return kernel_call("back", back_body, inputs, outputs, scratch, 2, flops=16 * 10**9, moved=60 * 2**20)


def finish(b):
    def cut(t):
        return b.O[:, t * REAL:(t + 1) * REAL].reshape(2 * REAL, HALF).astype(f32)

    vectors = b.Oy[:, 128:131].astype(f32)
    gains = jnp.sum(vectors, axis=0)
    return (
        b.block_out, b.input_grad, gains[0], b.O4[384:768].astype(f32).T, b.O4[962, :384].astype(f32),
        b.Oy[:, :128].reshape(512, HALF).astype(f32).T, vectors[:, 2, 384:512].reshape(512),
        b.O4[:384].astype(f32), gains[1], cut(1).T, cut(2).T, cut(0))


def per_device(layer_input, norm1_gain, q_weight, q_bias, kv_weight, kv_bias, o_weight, norm2_gain,
               gate_weight, up_weight, down_weight, seq_lengths, out_grad):
    f = front(layer_input, norm1_gain, q_weight, q_bias, kv_weight, kv_bias, o_weight, norm2_gain,
              gate_weight, up_weight, down_weight, seq_lengths, out_grad)
    b = back(f, layer_input, norm1_gain, q_weight, kv_weight, norm2_gain, out_grad)
    return finish(b)


def solution(mesh):
    rows, width = P(("dp", "gy"), "gx"), P("gx", "gy")
    return jax.shard_map(
        per_device,
        mesh=mesh,
        in_specs=(rows, P("gx"), width, P("gy"), P("gx", None), P(), P("gy", "gx"), P("gx"), width, width,
                  P("gy", "gx"), P("dp", None), rows),
        out_specs=(rows, rows, P("gx"), width, P("gy"), P("gx", None), P(), P("gy", "gx"), P("gx"), width, width,
                   P("gy", "gx")),
        check_vma=False,
    )
```

```python
import jax
import jax.numpy as jnp
import numpy as np
from jax import lax
from jax.experimental import pallas as pl
from jax.experimental.pallas import tpu as pltpu
from jax.sharding import PartitionSpec as P

f32 = jnp.float32
bf16 = jnp.bfloat16
MESH = pl.DeviceIdType.MESH
EPSILON = 1e-06
THETA = 1000000.0
NEGATIVE = -1e30
D = 1536
HALF = 768
BLOCK = 256
TOKENS = 1024
COLS = 1152
REAL = 1120
HEADS = 3
HEAD = 128


def dg(left, right, left_dim, right_dim):
    return lax.dot_general(
        left, right, (((left_dim,), (right_dim,)), ((), ())), preferred_element_type=f32
    )


def dot(left, right):
    return jnp.dot(left, right, preferred_element_type=f32)


class Names:
    def __init__(self, pairs):
        self.__dict__.update(pairs)


def rows_of(block, size=BLOCK):
    return pl.ds(pl.multiple_of(block * size, size), size)


class Copy:
    def __init__(self, copy, remote):
        self.copy, self.remote = copy, remote
        self.left = self.came = False
        copy.start()

    def wait_send(self):
        if not self.left:
            self.left = True
            self.copy.wait_send()

    def wait_recv(self):
        if not self.came:
            self.came = True
            self.copy.wait_recv()

    def wait(self):
        if not self.left:
            self.left = True
            self.copy.wait()


class Moves:
    def __init__(self, send, recv, local):
        self.send, self.recv, self.local = send, recv, local
        self.remotes = []
        self.locals = []

    def to(self, device, src, dst):
        i = len(self.remotes)
        copy = Copy(pltpu.make_async_remote_copy(
            src_ref=src, dst_ref=dst, send_sem=self.send.at[i], recv_sem=self.recv.at[i],
            device_id=device, device_id_type=MESH), True)
        self.remotes.append(copy)
        return copy

    def own(self, src, dst):
        copy = Copy(pltpu.make_async_copy(src, dst, self.local.at[len(self.locals)]), False)
        self.locals.append(copy)
        return copy

    out = own

    def settle(self, copies):
        for copy in copies:
            copy.wait_send()

    def finish(self):
        for copy in self.remotes:
            copy.wait_send()
            copy.wait_recv()
        for copy in self.locals:
            copy.wait()


class Place:
    def __init__(self):
        self.gx = lax.axis_index("gx")
        self.gy = lax.axis_index("gy")
        self.up = {"gy": lax.rem(self.gy + 1, 4)}
        self.down = {"gy": lax.rem(self.gy + 3, 4)}
        self.pal = {"gx": 1 - self.gx}
        self.blk = [lax.rem(self.gy + i, 4) for i in range(4)]
        self.cols = pl.ds(pl.multiple_of(self.gx * HALF, 128), HALF)


class GatherY:
    def __init__(self, moves, place, src, buf):
        self.m, self.p, self.src, self.buf = moves, place, src, buf

    def part(self, block, first, count):
        r = pl.ds(pl.multiple_of(block * BLOCK + first, 128), count)
        return self.buf.at[r, self.p.cols]

    def start(self):
        p = self.p
        there = self.part(p.blk[0], 0, BLOCK)
        self.a = self.m.to(p.up, self.src, there)
        self.b = self.m.to(p.down, self.src, there)
        self.c = self.m.to(p.pal, self.src, there)

    def own_ready(self):
        self.c.wait_recv()

    def relay(self):
        p, m = self.p, self.m
        low, high = p.blk[3], p.blk[1]
        self.a.wait_recv()
        x = self.part(low, 0, 128)
        self.d = m.to(p.up, x, x)
        self.b.wait_recv()
        x = self.part(high, 128, 128)
        self.e = m.to(p.down, x, x)
        x = self.part(low, 0, BLOCK)
        self.f = m.to(p.pal, x, x)
        x = self.part(high, 0, BLOCK)
        self.g = m.to(p.pal, x, x)

    def low_ready(self):
        self.f.wait_recv()

    def high_ready(self):
        self.g.wait_recv()

    def relay_pal(self):
        p, m = self.p, self.m
        far = p.blk[2]
        self.d.wait_recv()
        x = self.part(far, 0, 128)
        self.h = m.to(p.pal, x, x)
        self.e.wait_recv()
        x = self.part(far, 128, 128)
        self.i = m.to(p.pal, x, x)

    def far_ready(self):
        self.h.wait_recv()
        self.i.wait_recv()


class ScatterY:
    def __init__(self, moves, place, staged, held, low_half, high_half, from_low, from_high):
        self.m, self.p = moves, place
        self.staged, self.held = staged, held
        self.low_half, self.high_half = low_half, high_half
        self.from_low, self.from_high = from_low, from_high

    def far(self, value):
        p, m = self.p, self.m
        self.staged[0] = value.astype(bf16)
        self.a = m.to(p.up, self.staged.at[0, pl.ds(0, 128)], self.low_half)
        self.b = m.to(p.down, self.staged.at[0, pl.ds(128, 128)], self.high_half)

    def next_up(self, value):
        p, m = self.p, self.m
        self.staged[1, 128:] = value[128:].astype(bf16)
        self.c = m.to(p.up, self.staged.at[1, pl.ds(128, 128)], self.from_low.at[pl.ds(128, 128)])
        self.held[0] = value[:128]

    def next_down(self, value):
        p, m = self.p, self.m
        self.staged[2, :128] = value[:128].astype(bf16)
        self.d = m.to(p.down, self.staged.at[2, pl.ds(0, 128)], self.from_high.at[pl.ds(0, 128)])
        self.held[1] = value[128:]

    def relay(self):
        p, m = self.p, self.m
        self.a.wait_recv()
        self.staged[1, :128] = (self.held[0] + self.low_half[...].astype(f32)).astype(bf16)
        self.e = m.to(p.up, self.staged.at[1, pl.ds(0, 128)], self.from_low.at[pl.ds(0, 128)])
        self.b.wait_recv()
        self.staged[2, 128:] = (self.held[1] + self.high_half[...].astype(f32)).astype(bf16)
        self.f = m.to(p.down, self.staged.at[2, pl.ds(128, 128)], self.from_high.at[pl.ds(128, 128)])

    def result(self, own):
        self.c.wait_recv()
        self.d.wait_recv()
        self.e.wait_recv()
        self.f.wait_recv()
        return own + self.from_low[...].astype(f32) + self.from_high[...].astype(f32)


def enter(devices):
    barrier = pltpu.get_barrier_semaphore()
    for device in devices:
        pl.semaphore_signal(barrier, inc=1, device_id=device, device_id_type=MESH)
    pl.semaphore_wait(barrier, len(devices))


def turned(value, cosine, signed_sine):
    return value * cosine + pltpu.roll(value, 64, 1) * signed_sine


def opening_of(ends, places):
    opening = jnp.zeros_like(places)
    for e in ends:
        opening = jnp.where(places >= e, jnp.maximum(opening, e), opening)
    return opening


def front_body(n):
    m = Moves(n.send, n.recv, n.local)
    front_steps(n, m)
    m.finish()


def front_steps(n, m):
    p = Place()
    gx, gy = p.gx, p.gy

    mine = pl.ds(pl.multiple_of(gx * REAL, 16), REAL)
    theirs = pl.ds(pl.multiple_of((1 - gx) * REAL, 16), REAL)
    weights = ((n.dw, n.Wd, 0), (n.gw, n.Wgu, 0), (n.uw, n.Wgu, COLS))
    loads = [m.own(w.at[mine], W.at[pl.ds(at, REAL), p.cols]) for w, W, at in weights]
    n.g1f[:, p.cols] = jnp.broadcast_to(n.g1[...].reshape(1, HALF), (8, HALF))
    enter([p.up, p.down, p.pal])

    gather_x = GatherY(m, p, n.x, n.xb)
    gather_x.start()
    gain_move = m.to(p.pal, n.g1f.at[:, p.cols], n.g1f.at[:, p.cols])
    pair = p.gy // 2
    pair_cols = pl.ds(pl.multiple_of(pair * 256, 128), 256)
    own_rows = pl.ds(pl.multiple_of(gx * HALF, 128), HALF)
    kv_move = m.to(p.pal, n.kvw.at[:, pair_cols], n.Wkv.at[own_rows])
    q_move = m.to(p.pal, n.qw, n.Wq.at[own_rows])
    o_move = m.to(p.pal, n.ow, n.Wo.at[:, p.cols])

    n.xb[rows_of(gy), p.cols] = n.x[...]
    n.Wkv[own_rows, :] = n.kvw[:, pair_cols]
    n.Wq[own_rows, :] = n.qw[...]
    n.Wo[:, p.cols] = n.ow[...]

    ends = []
    running = jnp.int32(0)
    for k in range(4):
        running = running + n.seq[0, k]
        ends.append(running)
    lane = lax.broadcasted_iota(jnp.int32, (BLOCK, HEAD), 1)

    def table(i):
        places = lax.broadcasted_iota(jnp.int32, (BLOCK, HEAD), 0) + i * BLOCK
        position = places - opening_of(ends, places)
        angles = position.astype(f32) * n.freqs[...]
        r = rows_of(i)
        n.cosT[r, :] = jnp.cos(angles)
        n.sinT[r, :] = jnp.where(lane < 64, -jnp.sin(angles), jnp.sin(angles))

    pl.loop(0, 4)(table)
    m.out(n.cosT, n.cosO)
    m.out(n.sinT, n.sinO)

    gather_x.relay()

    def norm_block(block):
        r = rows_of(block)
        xf = n.xb[r, :].astype(f32)
        inverse = lax.rsqrt(jnp.sum(xf * xf, axis=1, keepdims=True) * (1.0 / D) + EPSILON)
        normed = (xf * inverse * n.g1f[0:1, :]).astype(bf16)
        n.nx[r, :] = normed
        kv = dot(normed, n.Wkv[...]) + n.kvb[pair_cols].reshape(1, 256)
        n.K[r, :] = turned(kv[:, :HEAD], n.cosT[r, :], n.sinT[r, :]).astype(bf16)
        n.V[r, :] = kv[:, HEAD:].astype(bf16)
        return inverse

    gain_move.wait_recv()
    kv_move.wait_recv()
    gather_x.own_ready()
    inverse = norm_block(p.blk[0])
    n.r1T[...] = jnp.broadcast_to(inverse, (BLOCK, HEAD))
    m.out(n.r1T, n.r1)
    gather_x.low_ready()
    norm_block(p.blk[3])
    gather_x.high_ready()
    norm_block(p.blk[1])
    gather_x.relay_pal()
    gather_og = GatherY(m, p, n.og, n.ogb)
    gather_og.start()
    weight_moves = [m.to(p.pal, w.at[theirs], W.at[pl.ds(at, REAL), p.cols]) for w, W, at in weights]
    n.ogb[rows_of(gy), p.cols] = n.og[...]
    for _, W, at in weights:
        W[at + REAL:at + COLS, :] = jnp.zeros((COLS - REAL, D), bf16)
    gather_x.far_ready()
    norm_block(p.blk[2])
    m.out(n.nx.at[:, p.cols], n.nxO)
    m.out(n.K, n.KO)
    m.out(n.V, n.VO)

    q_move.wait_recv()
    own_blocks = [gx, 3 - gx]
    for i, b in enumerate(own_blocks):
        r = rows_of(b)
        q = dot(n.nx[r, :], n.Wq[...]) + n.qb[...].reshape(1, 384)
        for h in range(HEADS):
            c = slice(h * HEAD, (h + 1) * HEAD)
            n.Q[i * BLOCK:(i + 1) * BLOCK, c] = turned(q[:, c], n.cosT[r, :], n.sinT[r, :]).astype(bf16)
    m.out(n.Q, n.QO)

    def attention(i, h):
        b = own_blocks[i]
        keys = 512 * (i + 1)
        at = 512 * i
        c = slice(h * HEAD, (h + 1) * HEAD)
        s = dg(n.Q[i * BLOCK:(i + 1) * BLOCK, c], n.K[:keys, :], 1, 1) * HEAD ** (-0.5)
        query = lax.broadcasted_iota(jnp.int32, (BLOCK, 1), 0) + b * BLOCK
        opening = opening_of(ends, query)
        key = lax.broadcasted_iota(jnp.int32, (BLOCK, keys), 1)
        s = jnp.where((key >= opening) & (key <= query), s, NEGATIVE)
        e = jnp.exp(s - jnp.max(s, axis=1, keepdims=True))
        probs = (e / jnp.sum(e, axis=1, keepdims=True)).astype(bf16)
        n.Pr[h * BLOCK:(h + 1) * BLOCK, at:at + keys] = probs
        out = dot(probs, n.V[:keys, :])
        n.att[rows_of(b), c] = out.astype(bf16)

    att_moves = []
    for i in (1, 0):
        for h in range(HEADS):
            attention(i, h)
        b = rows_of(own_blocks[i])
        att_moves.append(m.to(p.pal, n.att.at[b], n.att.at[b]))
        if i == 1:
            gather_og.relay()
    m.out(n.Pr, n.PO)
    gather_og.own_ready()
    loads[0].wait()
    weight_moves[0].wait_recv()

    def hidden_grad(block):
        r = rows_of(block)
        n.HG[r, :] = dg(n.ogb[r, :], n.Wd[...], 1, 1)

    for copy in att_moves:
        copy.wait_recv()

    m.settle([gather_x.a, gather_x.b, gather_x.c, gather_x.d, gather_x.e, gather_x.f, gather_x.g, gather_x.h, gather_x.i])

    def out_part(block):
        return dot(n.att[rows_of(block), :], n.ow[...])

    rs = ScatterY(m, p, n.staged, n.held, n.low_half, n.high_half, n.from_low, n.from_high)
    rs.far(out_part(p.blk[2]))
    rs.next_up(out_part(p.blk[1]))
    rs.next_down(out_part(p.blk[3]))
    n.mid[...] = out_part(p.blk[0]) + n.x[...].astype(f32)
    m.out(n.att, n.attO)
    gather_og.relay_pal()
    rs.relay()
    hidden_grad(p.blk[0])
    gather_og.low_ready()
    hidden_grad(p.blk[3])
    gather_og.high_ready()
    hidden_grad(p.blk[1])
    n.mid[...] = rs.result(n.mid[...])
    m.out(n.mid, n.midO)
    mid = n.mid[...]
    n.sums[0] = jnp.broadcast_to(jnp.sum(mid * mid, axis=1, keepdims=True), (BLOCK, HEAD))
    sum_move = m.to(p.pal, n.sums.at[0], n.sums.at[1])
    sum_move.wait_recv()
    r2 = lax.rsqrt((n.sums[0] + n.sums[1]) * (1.0 / D) + EPSILON)
    n.r2T[...] = r2
    m.out(n.r2T, n.r2)
    n.nto[...] = (n.mid[...] * r2[:, :1] * n.g2[...].reshape(1, HALF)).astype(bf16)
    gather_n = GatherY(m, p, n.nto, n.xb)
    gather_n.start()
    n.xb[rows_of(gy), p.cols] = n.nto[...]
    gather_og.far_ready()
    m.out(n.ogb, n.ogO)
    hidden_grad(p.blk[2])
    for k in (1, 2):
        loads[k].wait()
        weight_moves[k].wait_recv()
    m.out(n.Wgu, n.WguO)
    m.out(n.Wd, n.WdO)

    def feed_forward(block):
        r = rows_of(block)
        a = n.xb[r, :]
        gate = dg(a, n.Wgu[:COLS, :], 1, 1)
        upward = dg(a, n.Wgu[COLS:, :], 1, 1)
        back = n.HG[r, :]
        sg = jax.nn.sigmoid(gate)
        gs = gate * sg
        n.hid[r, :] = (gs * upward).astype(bf16)
        n.gu[r, :COLS] = (back * upward * sg * (1.0 + gate * (1.0 - sg))).astype(bf16)
        n.gu[r, COLS:] = (back * gs).astype(bf16)
        m.out(n.hid.at[r], n.hidO.at[r])
        m.out(n.gu.at[r], n.guO.at[r])

    gather_n.own_ready()
    feed_forward(p.blk[0])
    gather_n.relay()
    gather_n.low_ready()
    feed_forward(p.blk[3])
    gather_n.high_ready()
    feed_forward(p.blk[1])
    gather_n.relay_pal()
    gather_n.far_ready()
    m.out(n.xb, n.ntO)
    feed_forward(p.blk[2])

    o_move.wait_recv()
    m.out(n.Wo, n.WoO)


def kernel_call(name, body, inputs, outputs, scratch, collective_id, flops=0, moved=0):
    order = list(inputs) + list(outputs) + list(scratch)

    def kernel(*refs):
        body(Names(dict(zip(order, refs))))

    results = pl.pallas_call(
        kernel,
        out_shape=tuple(jax.ShapeDtypeStruct(s, d) for s, d, _ in outputs.values()),
        in_specs=[pl.BlockSpec(memory_space=s) for _, s in inputs.values()],
        out_specs=tuple(pl.BlockSpec(memory_space=s) for _, _, s in outputs.values()),
        scratch_shapes=list(scratch.values()),
        compiler_params=pltpu.CompilerParams(
            collective_id=collective_id, has_side_effects=True, vmem_limit_bytes=62 * 2**20),
        cost_estimate=pl.CostEstimate(flops=flops, bytes_accessed=moved, transcendentals=0),
        name=name,
    )(*[a for a, _ in inputs.values()])
    return Names(dict(zip(outputs, results)))


def frequencies():
    freqs = np.float32(THETA) ** (-np.arange(0, HEAD, 2, dtype=np.float32) / np.float32(HEAD))
    return np.concatenate([freqs, freqs])[None, :]


def front(layer_input, norm1_gain, q_weight, q_bias, kv_weight, kv_bias, o_weight, norm2_gain,
          gate_weight, up_weight, down_weight, seq_lengths, out_grad):
    vm, hbm, sm = pltpu.VMEM, pl.ANY, pltpu.SMEM
    inputs = dict(
        x=(layer_input, vm), og=(out_grad, vm), g1=(norm1_gain, vm), g2=(norm2_gain, vm),
        qw=(q_weight, vm), qb=(q_bias, vm), kvw=(kv_weight, vm), kvb=(kv_bias, vm),
        ow=(o_weight, vm), gw=(gate_weight.T, hbm), uw=(up_weight.T, hbm), dw=(down_weight, hbm),
        seq=(seq_lengths, sm), freqs=(frequencies(), vm))
    outputs = dict(
        ogO=((TOKENS, D), bf16, hbm), ntO=((TOKENS, D), bf16, hbm),
        hidO=((TOKENS, COLS), bf16, hbm), guO=((TOKENS, 2 * COLS), bf16, hbm),
        WguO=((2 * COLS, D), bf16, hbm), WdO=((COLS, D), bf16, hbm),
        midO=((BLOCK, HALF), f32, hbm), r1=((BLOCK, HEAD), f32, hbm), r2=((BLOCK, HEAD), f32, hbm),
        attO=((TOKENS, 384), bf16, hbm), PO=((HEADS * BLOCK, 1536), bf16, hbm), QO=((512, 384), bf16, hbm),
        KO=((TOKENS, HEAD), bf16, hbm), VO=((TOKENS, HEAD), bf16, hbm),
        cosO=((TOKENS, HEAD), f32, hbm), sinO=((TOKENS, HEAD), f32, hbm), nxO=((TOKENS, HALF), bf16, hbm),
        WoO=((384, D), bf16, hbm))
    v = pltpu.VMEM
    scratch = dict(
        Wgu=v((2 * COLS, D), bf16), Wd=v((COLS, D), bf16),
        Wkv=v((D, 256), bf16), Wq=v((D, 384), bf16), Wo=v((384, D), bf16), g1f=v((8, D), f32),
        xb=v((TOKENS, D), bf16), nx=v((TOKENS, D), bf16), ogb=v((TOKENS, D), bf16),
        cosT=v((TOKENS, HEAD), f32), sinT=v((TOKENS, HEAD), f32),
        K=v((TOKENS, HEAD), bf16), V=v((TOKENS, HEAD), bf16), Q=v((512, 384), bf16),
        Pr=v((HEADS * BLOCK, 1536), bf16), att=v((TOKENS, 384), bf16),
        staged=v((3, BLOCK, HALF), bf16), held=v((2, 128, HALF), f32),
        low_half=v((128, HALF), bf16), high_half=v((128, HALF), bf16),
        from_low=v((BLOCK, HALF), bf16), from_high=v((BLOCK, HALF), bf16),
        mid=v((BLOCK, HALF), f32), sums=v((2, BLOCK, HEAD), f32), r1T=v((BLOCK, HEAD), f32),
        r2T=v((BLOCK, HEAD), f32), nto=v((BLOCK, HALF), bf16),
        HG=v((TOKENS, COLS), f32), hid=v((TOKENS, COLS), bf16), gu=v((TOKENS, 2 * COLS), bf16),

        send=pltpu.SemaphoreType.DMA((48,)), recv=pltpu.SemaphoreType.DMA((48,)),
        local=pltpu.SemaphoreType.DMA((48,)))
    return kernel_call("front", front_body, inputs, outputs, scratch, 1, flops=30 * 10**9, moved=60 * 2**20)


UNITS = (4, 4, 5)
LEFT = 3328
SCALE = HEAD ** (-0.5)


class Ring:
    def __init__(self, place, along_x):
        z, x = place.z, place.x
        if isinstance(along_x, bool):
            c = x if along_x else z
            ids = [z * 4 + lax.rem(x + s, 4) if along_x else lax.rem(z + s, 4) * 4 + x for s in (1, 3, 2)]
        else:
            c = jnp.where(along_x, x, z)
            ids = [jnp.where(along_x, z * 4 + lax.rem(x + s, 4), lax.rem(z + s, 4) * 4 + x) for s in (1, 3, 2)]
        self.c = c
        self.up, self.down, self.over = ({"dp": i} for i in ids)
        self.next, self.far, self.last = [lax.rem(c + s, 4) for s in (1, 2, 3)]


def scatter_sum(m, ring, src, base, own, out, a, s1, s2, w):
    low, high = slice(0, w), slice(w, None)
    k1 = m.to(ring.up, src(ring.far, low), s1[0])
    k2 = m.to(ring.down, src(ring.far, high), s1[1])
    k3 = m.to(ring.up, src(ring.next, high), s2[0].at[:, w:])
    k4 = m.to(ring.down, src(ring.last, low), s2[1].at[:, :w])
    yield
    k1.wait_recv()
    a[0][...] = (base(0).astype(f32) + s1[0][...].astype(f32)).astype(bf16)
    k5 = m.to(ring.up, a[0], s2[0].at[:, :w])
    k2.wait_recv()
    a[1][...] = (base(1).astype(f32) + s1[1][...].astype(f32)).astype(bf16)
    k6 = m.to(ring.down, a[1], s2[1].at[:, w:])
    yield
    for k in (k3, k4, k5, k6):
        k.wait_recv()
    out[...] = (own().astype(f32) + s2[0][...].astype(f32) + s2[1][...].astype(f32)).astype(bf16)
    yield


def gather_ring(m, ring, part):
    k1 = m.to(ring.up, part(ring.c, None), part(ring.c, None))
    k2 = m.to(ring.down, part(ring.c, None), part(ring.c, None))
    yield
    k1.wait_recv()
    x = part(ring.last, 0)
    k3 = m.to(ring.up, x, x)
    k2.wait_recv()
    x = part(ring.next, 1)
    k4 = m.to(ring.down, x, x)
    yield
    k3.wait_recv()
    k4.wait_recv()
    yield


def aligned_start(start):
    return pl.multiple_of(start, 32)


def aligned(start, size, unit=16):
    return pl.ds(pl.multiple_of(start, unit), size)


def main_piece(n, m, p, i):
    k = UNITS[i]
    base = 256 * sum(UNITS[:i])
    r1, r2 = 64 * k, 16 * k
    own, a, s1, s2 = (getattr(n, f"{name}{i}") for name in ("own", "a", "s1", "s2"))
    b, t1, t2, T2 = (getattr(n, f"{name}{i}") for name in ("b", "t1", "t2", "T"))
    rings = [Ring(p, True), Ring(p, False)]
    loads = []
    first, second = [], []
    for h in range(2):
        one, two = rings[h], rings[1 - h]

        def src(j, lanes, h=h):
            lo, hi = lanes.start + h * HALF, (lanes.stop or HALF) + h * HALF
            return n.G.at[aligned(base + j * r1, r1, 64), pl.ds(lo, hi - lo)]

        loads.append([(src(one.c, slice(0, HALF)), own.at[h]), (src(one.next, slice(0, 384)), a.at[h, 0]),
                      (src(one.last, slice(384, HALF)), a.at[h, 1])])
        first.append(scatter_sum(
            m, one, src, lambda d, h=h: a[h, d], lambda h=h: own[h], own.at[h],
            [a.at[h, 0], a.at[h, 1]], [s1.at[h, 0], s1.at[h, 1]], [s2.at[h, 0], s2.at[h, 1]], 384))

        def src2(j, lanes, h=h):
            return own.at[h, aligned(j * r2, r2), pl.ds(lanes.start, (lanes.stop or HALF) - lanes.start)]

        def base2(d, h=h, two=two):
            if d == 0:
                return own[h, aligned(two.next * r2, r2), :384]
            return own[h, aligned(two.last * r2, r2), 384:]

        second.append(scatter_sum(
            m, two, src2, base2, lambda h=h, two=two: own[h, aligned(two.c * r2, r2), :], T2.at[h],
            [b.at[h, 0], b.at[h, 1]], [t1.at[h, 0], t1.at[h, 1]], [t2.at[h, 0], t2.at[h, 1]], 384))
    for g in first:
        next(g)
    loads = [m.own(*pair) for pairs in loads for pair in pairs]
    yield
    for c in loads:
        c.wait()
    for g in first:
        next(g)
    yield
    for g, g2 in zip(first, second):
        next(g)
        next(g2)
    yield
    for g in second:
        next(g)
    yield
    for g in second:
        next(g)
    one = Ring(p, p.gx == 0)
    two = Ring(p, p.gx != 0)

    def place(c1, c2, rows):
        return aligned(base + c1 * r1 + c2 * r2, rows)

    there = (Ring(p, p.gx != 0), Ring(p, p.gx == 0))
    mine = m.own(T2.at[p.gx], n.O.at[p.gx, place(one.c, two.c, r2)])
    swap = m.to(p.pal, T2.at[1 - p.gx], n.O.at[p.gx, place(there[0].c, there[1].c, r2)])
    yield
    mine.wait()
    swap.wait_recv()

    def part_two(j, half):
        r = place(one.c, j, r2)
        return n.O.at[:, r] if half is None else n.O.at[half, r]

    def part_one(j, half):
        r = place(j, jnp.int32(0), r1)
        return n.O.at[:, r] if half is None else n.O.at[half, r]

    g = gather_ring(m, two, part_two)
    next(g)
    yield
    next(g)
    yield
    next(g)
    g = gather_ring(m, one, part_one)
    next(g)
    yield
    next(g)
    yield
    next(g)
    yield


def small_piece(n, m, p):
    rings = [Ring(p, True), Ring(p, False)]
    r1, r2, W = 256, 64, 384
    lanes = [pl.ds(h * W, W) for h in range(2)]

    def spread(ring, src, dst):
        return [m.to(d, src(j), dst(k)) for k, (d, j) in enumerate(
            ((ring.up, ring.next), (ring.down, ring.last), (ring.over, ring.far)))]

    def total(own, came):
        return (own.astype(f32) + came[0].astype(f32)) + (came[1].astype(f32) + came[2].astype(f32))

    moves = [spread(rings[h], lambda j, h=h: n.M.at[aligned(j * r1, r1), lanes[h]], lambda k, h=h: n.Em.at[h, k])
             for h in range(2)]
    yield
    for h in range(2):
        for c in moves[h]:
            c.wait_recv()
        n.Tm[h] = total(n.M[aligned(rings[h].c * r1, r1), h * W:(h + 1) * W], n.Em[h]).astype(bf16)
        moves[h] = spread(rings[1 - h], lambda j, h=h: n.Tm.at[h, aligned(j * r2, r2)], lambda k, h=h: n.Fm.at[h, k])
    yield
    for h in range(2):
        one, two = rings[h], rings[1 - h]
        for c in moves[h]:
            c.wait_recv()
        n.Um[h] = total(n.Tm[h, aligned(two.c * r2, r2)], n.Fm[h]).astype(bf16)
        there = n.O4.at[aligned(one.c * r1 + two.c * r2, r2), lanes[h]]
        moves[h] = spread(two, lambda j, h=h: n.Um.at[h], lambda k, there=there: there)
        moves[h].append(m.own(n.Um.at[h], there))
    yield
    for h in range(2):
        for c in moves[h][:3]:
            c.wait_recv()
        moves[h][3].wait()
        there = n.O4.at[aligned(rings[h].c * r1, r1), lanes[h]]
        moves[h] = spread(rings[h], lambda j, there=there: there, lambda k, there=there: there)
    yield
    for h in range(2):
        for c in moves[h]:
            c.wait_recv()
    block = pl.ds(832, 144)
    far = {"gy": lax.rem(p.gy + 2, 4)}
    moves = [m.to(d, n.O4.at[block], n.Oy.at[p.gy]) for d in (p.up, p.down, far)]
    rest = [m.own(n.O4.at[block], n.Oy.at[p.gy])]
    for core in range(2):
        rest.append(m.own(n.O4.at[pl.ds(768 + 32 * core, 32)], n.O.at[core, pl.ds(LEFT, 32)]))
    yield
    for c in moves:
        c.wait_recv()
    for c in rest:
        c.wait()
    yield


SCHED = {
    "down": "0", "gate": "1", "up": "02",
    "b0": "", "b1": "", "b2": "", "b3": "", "own": "1", "relay1": "2", "ml": "0",
    "c0": "", "c1": "", "c2": "", "c3": "1", "ml1": "0", "ml2": "", "ml3": "20",
    "a10": "1", "a11": "20", "a12": "1", "relay2": "", "a00": "20", "a01": "1", "a02": "2",
    "pair": "10", "m1": "2m", "m2": "", "m3": "v",
    "tail": "m1v0m2vmv1m2m", "rest": "m012v"}


def vector_sum(n, m, p):
    coordinates = (p.x, p.z, p.gy)
    devices = (lambda s: {"dp": p.z * 4 + lax.rem(p.x + s, 4)}, lambda s: {"dp": lax.rem(p.z + s, 4) * 4 + p.x},
               lambda s: {"gy": lax.rem(p.gy + s, 4)})
    value = n.gain1[...]
    for d in range(3):
        slot = n.vectors.at[d, coordinates[d]]
        slot[...] = value
        moves = [m.to(devices[d](s), slot, slot) for s in (1, 3, 2)]
        yield
        for c in moves:
            c.wait_recv()
        value = (n.vectors[d, 0] + n.vectors[d, 1]) + (n.vectors[d, 2] + n.vectors[d, 3])
    n.gain1_sum[...] = value
    yield


def back_body(n):
    m = Moves(n.send, n.recv, n.local)
    back_steps(n, m)
    m.finish()


def back_steps(n, m):
    p = Place()
    dp = lax.axis_index("dp")
    p.z, p.x = lax.div(dp, 4), lax.rem(dp, 4)
    gx, gy = p.gx, p.gy
    pal_cols = pl.ds(pl.multiple_of((1 - gx) * HALF, 128), HALF)
    vm = Names({})
    load = {}

    def bring(name, src, dst):
        load[name] = m.own(src, dst)

    bring("og", n.ogf, n.WguV.at[pl.ds(TOKENS, TOKENS)])
    bring("hid", n.hid, n.ml.at[:, pl.ds(0, COLS)])
    bring("gu", n.gu, n.guV)
    bring("nt", n.nt, n.WguV.at[pl.ds(0, TOKENS)])
    bring("mid", n.mid, n.midV)
    bring("r2", n.r2, n.r2V)
    bring("Wgu2", n.Wgu.at[pl.ds(2 * TOKENS, 256)], n.WguV.at[pl.ds(2 * TOKENS, 256)])
    for name in ("att", "Q", "K", "V", "cos", "sin", "nx", "Wo", "r1"):
        bring(name, getattr(n, name), getattr(n, name + "V"))
    rings = [Ring(p, True), Ring(p, False)]
    gens = {str(i): main_piece(n, m, p, i) for i in range(3)}
    enter([p.up, p.down, p.pal, rings[0].up, rings[0].down, rings[1].up, rings[1].down])

    def ar(spot):
        for name in SCHED[spot]:
            next(gens[name], None)

    def leave(slot, k, i, rows):
        at = k * REAL + i * BLOCK
        at = pl.multiple_of(at, 32) if isinstance(i, int) else aligned_start(at)
        return pltpu.make_async_copy(
            n.stage.at[slot, pl.ds(0, rows)], n.G.at[pl.ds(at, rows)], n.gsem.at[slot])

    def weight_grad(k, left, at, right):
        @pl.loop(0, 4)
        def _(i):
            slot = lax.rem(i, 2)

            @pl.when(i >= 2)
            def _():
                leave(slot, k, i, BLOCK).wait()

            c = pl.ds(pl.multiple_of(i * BLOCK + at, 128), BLOCK)
            n.stage[slot] = dg(left[:, c], right[...], 0, 0).astype(bf16)
            leave(slot, k, i, BLOCK).start()

        leave(0, k, 2, BLOCK).wait()
        tail = dg(left[:, at + 4 * BLOCK:at + COLS], right[...], 0, 0).astype(bf16)
        n.stage[0, :REAL - 4 * BLOCK] = tail[:REAL - 4 * BLOCK]
        leave(0, k, 4, REAL - 4 * BLOCK).start()
        leave(1, k, 3, BLOCK).wait()
        leave(0, k, 4, REAL - 4 * BLOCK).wait()

    for name in ("og", "hid"):
        load[name].wait()
    weight_grad(0, n.ml, 0, n.WguV.at[pl.ds(TOKENS, TOKENS)])
    ar("down")
    bring("Wgu1", n.Wgu.at[pl.ds(TOKENS, TOKENS)], n.WguV.at[pl.ds(TOKENS, TOKENS)])
    for name in ("gu", "nt"):
        load[name].wait()
    weight_grad(1, n.guV, 0, n.WguV.at[pl.ds(0, TOKENS)])
    ar("gate")
    weight_grad(2, n.guV, COLS, n.WguV.at[pl.ds(0, TOKENS)])
    ar("up")
    bring("Wgu0", n.Wgu.at[pl.ds(0, TOKENS)], n.WguV.at[pl.ds(0, TOKENS)])
    left_row = aligned(768 + gx * 32, 32, 32)
    bring("left", n.G.at[pl.ds(LEFT, 32), p.cols], n.M.at[left_row])
    left_move = m.to(p.pal, n.G.at[pl.ds(LEFT, 32), pal_cols], n.M.at[left_row])

    for name in ("Wgu0", "Wgu1", "Wgu2"):
        load[name].wait()

    def two_sided(left, weight, take, give, held, names):
        order = (2, 1, 3, 0)
        moves = []
        for k, which in enumerate(order):
            r = rows_of(p.blk[which])
            if k >= 2:
                moves[k - 2].wait_send()
            give[k % 2] = dot(left(r), weight(pal_cols)).astype(bf16)
            moves.append(m.to(p.pal, give.at[k % 2], take.at[k]))
            held[k % 2] = dot(left(r), weight(p.cols))
            if k:
                moves[k - 1].wait_recv()
                yield held[(k - 1) % 2] + take[k - 1].astype(f32)
            ar(names[k])
        moves[3].wait_recv()
        moves[2].wait_send()
        moves[3].wait_send()
        yield held[1] + take[3].astype(f32)

    def scatter(letter):
        return ScatterY(m, p, n.staged, n.held, *(getattr(n, letter + name) for name in ("low", "high", "flow", "fhigh")))

    g = two_sided(lambda r: n.guV[r, :], lambda c: n.WguV[:, c], n.take, n.give, n.two, ("b0", "b1", "b2", "b3"))
    rs = scatter("A")
    rs.far(next(g))
    rs.next_up(next(g))
    rs.next_down(next(g))
    n.part[...] = next(g)
    ar("own")
    bring("hid", n.hid, n.guV.at[:, pl.ds(0, COLS)])
    bring("Wd", n.Wd, n.WguV.at[pl.ds(0, COLS)])
    bring("P", n.P, n.WguV.at[pl.ds(COLS, HEADS * BLOCK)])
    rs.relay()
    ar("relay1")
    n.part[...] = rs.result(n.part[...])
    load["mid"].wait()
    load["r2"].wait()
    r2 = n.r2V[:, :1]
    y2 = n.midV[...] * r2
    w2 = n.part[...] * n.g2[...].reshape(1, HALF)
    n.gain2[...] = jnp.broadcast_to(jnp.sum(n.part[...] * y2, axis=0, keepdims=True), (8, HALF))
    n.sums[0] = jnp.broadcast_to(jnp.sum(w2 * y2, axis=1, keepdims=True), (BLOCK, HEAD))
    sum_move = m.to(p.pal, n.sums.at[0], n.sums.at[1])
    sum_move.wait_recv()
    total = (n.sums[0] + n.sums[1])[:, :1] * (1.0 / D)
    n.mg[...] = n.og[...].astype(f32) + r2 * (w2 - y2 * total)
    n.mlo[...] = n.mg[...].astype(bf16)
    gather = GatherY(m, p, n.mlo, n.ml)
    gather.start()
    n.ml[rows_of(gy), p.cols] = n.mlo[...]
    ar("ml")

    load["hid"].wait()
    load["Wd"].wait()
    g = two_sided(lambda r: n.guV[r, :COLS], lambda c: n.WguV[:COLS, c], n.take, n.give, n.two, ("c0", "c1", "c2", "c3"))
    for k in range(3):
        n.later[k] = next(g).astype(bf16)
    n.part[...] = next(g) + n.midV[...]
    ar("ml1")
    gather.relay()
    ar("ml2")
    gather.relay_pal()
    m.settle([rs.a, rs.b, rs.c, rs.d, rs.e, rs.f])
    rs = scatter("B")
    rs.far(n.later[0].astype(f32))
    rs.next_up(n.later[1].astype(f32))
    rs.next_down(n.later[2].astype(f32))
    gather.own_ready()
    gather.low_ready()
    gather.high_ready()
    ar("ml3")

    for name in ("att", "Q", "K", "V", "cos", "sin", "nx", "Wo", "r1", "P", "left"):
        load[name].wait()
    gather.far_ready()
    n.M[0:384, :] = dg(n.attV[...], n.ml[:, p.cols], 0, 0).astype(bf16)
    own_blocks = [gx, 3 - gx]
    q_moves = []
    for i in (1, 0):
        b = rows_of(own_blocks[i])
        keys, at = 512 * (i + 1), 512 * i
        n.ag[...] = dg(n.ml[b, :], n.WoV[...], 1, 1).astype(bf16)
        for h in range(HEADS):
            c = slice(h * HEAD, (h + 1) * HEAD)
            probs = n.WguV[COLS + h * BLOCK:COLS + (h + 1) * BLOCK, at:at + keys]
            probs_f = probs.astype(f32)
            prob_grads = dg(n.ag[:, c], n.VV[:keys, :], 1, 1)
            centre = jnp.sum(probs_f * prob_grads, axis=1, keepdims=True)
            score_grads = (probs_f * (prob_grads - centre)).astype(bf16)
            dq = dot(score_grads, n.KV[:keys, :]) * SCALE
            dk = dg(score_grads, n.QV[i * BLOCK:(i + 1) * BLOCK, c], 0, 0) * SCALE
            dv = dg(probs, n.ag[:, c], 0, 0)
            if i == 1 and h == 0:
                n.dkv[:, :HEAD] = dk
                n.dkv[:, HEAD:] = dv
            else:
                n.dkv[:keys, :HEAD] += dk
                n.dkv[:keys, HEAD:] += dv
            n.ql[b, c] = turned(dq, n.cosV[b, :], -n.sinV[b, :]).astype(bf16)
            ar(f"a{i}{h}")
        q_moves.append(m.to(p.pal, n.ql.at[b], n.ql.at[b]))
        if i == 1:
            rs.relay()
            ar("relay2")
    n.S[0] = n.dkv[...].astype(bf16)
    s_move = m.to(p.pal, n.S.at[0], n.S.at[1])
    n.block_out[...] = rs.result(n.part[...])
    s_move.wait_recv()
    both = n.S[0].astype(f32) + n.S[1].astype(f32)
    n.dkv[...] = both
    n.S2[...] = both.astype(bf16)
    odd = lax.rem(gy, 2)
    pair = {"gy": gy + 1 - 2 * odd}
    pair_move = m.to(pair, n.S2.at[:, pl.ds(pl.multiple_of((1 - odd) * HEAD, HEAD), HEAD)], n.pin)
    ar("pair")
    for copy in q_moves:
        copy.wait_recv()
    n.M[384:768, :] = dg(n.ql[...], n.nxV[...], 0, 0).astype(bf16)
    pair_move.wait_recv()
    kv = n.dkv[:, pl.ds(pl.multiple_of(odd * HEAD, HEAD), HEAD)] + n.pin[...].astype(f32)
    is_key = (1 - odd).astype(f32)
    cosine = n.cosV[...] * is_key + (1.0 - is_key)
    sine = n.sinV[...] * is_key
    n.plow[...] = turned(kv, cosine, -sine).astype(bf16)
    n.M[832:960, :] = dg(n.plow[...], n.nxV[...], 0, 0).astype(bf16)
    bias = jnp.concatenate([
        jnp.sum(n.ql[...].astype(f32), axis=0, keepdims=True),
        jnp.sum(n.plow[...].astype(f32), axis=0, keepdims=True),
        jnp.zeros((1, 256), f32)], axis=1)
    row = lax.broadcasted_iota(jnp.int32, (64, HALF), 0)
    n.M[960:, :] = jnp.where(row == 0, n.gain2[0:1, :], jnp.where(row == 1, bias, 0.0)).astype(bf16)

    def norm_one_part(block):
        r = rows_of(block)
        kvw = n.kvw[:, pl.ds(pl.multiple_of(gy * HEAD, HEAD), HEAD)]
        return dg(n.ql[r, :], n.qw[...], 1, 1) + dg(n.plow[r, :], kvw, 1, 1)

    m.settle([rs.a, rs.b, rs.c, rs.d, rs.e, rs.f])
    rs = scatter("A")
    rs.far(norm_one_part(p.blk[2]))
    rs.next_up(norm_one_part(p.blk[1]))
    rs.next_down(norm_one_part(p.blk[3]))
    n.part[...] = norm_one_part(p.blk[0])
    left_move.wait_recv()
    gens["m"] = small_piece(n, m, p)
    ar("m1")
    rs.relay()
    ar("m2")
    n.part[...] = rs.result(n.part[...])
    r1 = n.r1V[:, :1]
    y1 = n.x[...].astype(f32) * r1
    w1 = n.part[...] * n.g1[...].reshape(1, HALF)
    gain1 = jnp.sum(n.part[...] * y1, axis=0, keepdims=True)
    m.settle([sum_move])
    n.sums[0] = jnp.broadcast_to(jnp.sum(w1 * y1, axis=1, keepdims=True), (BLOCK, HEAD))
    sum_move = m.to(p.pal, n.sums.at[0], n.sums.at[2])
    n.gain1[...] = jnp.broadcast_to(gain1, (8, HALF))
    gens["v"] = vector_sum(n, m, p)
    ar("m3")
    sum_move.wait_recv()
    total = (n.sums[0] + n.sums[2])[:, :1] * (1.0 / D)
    n.input_grad[...] = n.mg[...] + r1 * (w1 - y1 * total)
    ar("tail")
    for _ in range(14):
        ar("rest")


def back(f, layer_input, norm1_gain, q_weight, kv_weight, norm2_gain, out_grad):
    vm, hbm = pltpu.VMEM, pl.ANY
    inputs = dict(
        x=(layer_input, vm), og=(out_grad, vm), g1=(norm1_gain, vm), g2=(norm2_gain, vm),
        qw=(q_weight, vm), kvw=(kv_weight, vm),
        ogf=(f.ogO, hbm), nt=(f.ntO, hbm), gu=(f.guO, hbm), Wgu=(f.WguO, hbm), hid=(f.hidO, hbm), Wd=(f.WdO, hbm), mid=(f.midO, hbm),
        r1=(f.r1, hbm), r2=(f.r2, hbm), att=(f.attO, hbm), P=(f.PO, hbm), Q=(f.QO, hbm), K=(f.KO, hbm),
        V=(f.VO, hbm), cos=(f.cosO, hbm), sin=(f.sinO, hbm), nx=(f.nxO, hbm), Wo=(f.WoO, hbm))
    outputs = dict(
        block_out=((BLOCK, HALF), f32, vm), input_grad=((BLOCK, HALF), f32, vm),
        O=((2, 3 * REAL, HALF), bf16, hbm), O4=((TOKENS, HALF), bf16, hbm), Oy=((4, 144, HALF), bf16, hbm),
        gain1_sum=((8, HALF), f32, vm), G=((3 * REAL, D), bf16, hbm))
    v = pltpu.VMEM
    scratch = dict(
        guV=v((TOKENS, 2 * COLS), bf16), WguV=v((2 * COLS, D), bf16), midV=v((BLOCK, HALF), f32),
        r1V=v((BLOCK, HEAD), f32), r2V=v((BLOCK, HEAD), f32), attV=v((TOKENS, 384), bf16), QV=v((512, 384), bf16),
        KV=v((TOKENS, HEAD), bf16), VV=v((TOKENS, HEAD), bf16), cosV=v((TOKENS, HEAD), f32),
        sinV=v((TOKENS, HEAD), f32), nxV=v((TOKENS, HALF), bf16), WoV=v((384, D), bf16),
        take=v((4, BLOCK, HALF), bf16), give=v((2, BLOCK, HALF), bf16), two=v((2, BLOCK, HALF), f32),
        staged=v((3, BLOCK, HALF), bf16), held=v((2, 128, HALF), f32),
        part=v((BLOCK, HALF), f32), later=v((3, BLOCK, HALF), bf16), stage=v((2, BLOCK, D), bf16),
        gain1=v((8, HALF), f32), vectors=v((3, 4, 8, HALF), f32), gain2=v((8, HALF), f32), sums=v((3, BLOCK, HEAD), f32),
        mg=v((BLOCK, HALF), f32), mlo=v((BLOCK, HALF), bf16), ml=v((TOKENS, D), bf16),
        ag=v((BLOCK, 384), bf16), dkv=v((TOKENS, 256), f32), ql=v((TOKENS, 384), bf16), S=v((2, TOKENS, 256), bf16),
        S2=v((TOKENS, 256), bf16), pin=v((TOKENS, HEAD), bf16), plow=v((TOKENS, HEAD), bf16), M=v((TOKENS, HALF), bf16),
        Em=v((2, 3, 256, 384), bf16), Tm=v((2, 256, 384), bf16), Fm=v((2, 3, 64, 384), bf16), Um=v((2, 64, 384), bf16))
    for letter in "AB":
        scratch.update({letter + "low": v((128, HALF), bf16), letter + "high": v((128, HALF), bf16),
                        letter + "flow": v((BLOCK, HALF), bf16), letter + "fhigh": v((BLOCK, HALF), bf16)})
    for i, k in enumerate(UNITS):
        r1, r2 = 64 * k, 16 * k
        scratch.update({
            f"own{i}": v((2, r1, HALF), bf16), f"a{i}": v((2, 2, r1, 384), bf16), f"s1{i}": v((2, 2, r1, 384), bf16),
            f"s2{i}": v((2, 2, r1, HALF), bf16), f"b{i}": v((2, 2, r2, 384), bf16), f"t1{i}": v((2, 2, r2, 384), bf16),
            f"t2{i}": v((2, 2, r2, HALF), bf16), f"T{i}": v((2, r2, HALF), bf16)})
    scratch.update(send=pltpu.SemaphoreType.DMA((200,)), recv=pltpu.SemaphoreType.DMA((200,)),
                   local=pltpu.SemaphoreType.DMA((64,)), gsem=pltpu.SemaphoreType.DMA((2,)))
    return kernel_call("back", back_body, inputs, outputs, scratch, 2, flops=16 * 10**9, moved=60 * 2**20)


def finish(b):
    PART = 224
    big = b.O.reshape(2, 3, REAL, HALF)

    def kernel(down, gate, up, small, shared, down_out, gate_out, up_out, o_out, q_out, kv_out, bias_out):
        down_out[...] = down[0].astype(f32)
        gate_out[...] = gate[0].astype(f32)
        up_out[...] = up[0].astype(f32)

        @pl.when((pl.program_id(0) == 0) & (pl.program_id(1) == 0))
        def _():
            o_out[...] = small[:384, :].astype(f32)
            q_out[...] = small[384:768, :].astype(f32).T
            for k in range(4):
                kv_out[:, k * HEAD:(k + 1) * HEAD] = shared[k, :HEAD, :].astype(f32).T
            total = jnp.zeros((16, HALF), f32)
            for k in range(4):
                total = total + shared[k, HEAD:, :].astype(f32)
            bias_out[:16] = total
            bias_out[16:32] = small[960:976, :].astype(f32)
            for k in range(4):
                bias_out[32 + 16 * k:48 + 16 * k] = shared[k, HEAD:, :].astype(f32)

    def block(t):
        return pl.BlockSpec((1, 1, PART, HALF), lambda i, j, t=t: (i, t, j, 0))

    def whole(*shape):
        return pl.BlockSpec(shape, lambda i, j: (0,) * len(shape))

    out = pl.BlockSpec((1, PART, HALF), lambda i, j: (i, j, 0))
    weight = jax.ShapeDtypeStruct((2, REAL, HALF), f32)
    down, gate, up, o, q, kv, bias = pl.pallas_call(
        kernel,
        grid=(2, REAL // PART),
        in_specs=[block(0), block(1), block(2), whole(TOKENS, HALF), whole(4, 144, HALF)],
        out_specs=[out, out, out, whole(384, HALF), whole(HALF, 384), whole(HALF, 512), whole(96, HALF)],
        out_shape=[weight, weight, weight, jax.ShapeDtypeStruct((384, HALF), f32),
                   jax.ShapeDtypeStruct((HALF, 384), f32), jax.ShapeDtypeStruct((HALF, 512), f32),
                   jax.ShapeDtypeStruct((96, HALF), f32)],
        compiler_params=pltpu.CompilerParams(vmem_limit_bytes=40 * 2**20),
        name="finish",
    )(big, big, big, b.O4, b.Oy)

    def rows(w):
        return w.reshape(2 * REAL, HALF)

    kv_bias = jnp.concatenate([bias[33 + 16 * k, 384:512] for k in range(4)])
    return (
        b.block_out, b.input_grad, b.gain1_sum[0], q, bias[17, :384], kv, kv_bias, o, bias[0],
        rows(gate).T, rows(up).T, rows(down))


def per_device(layer_input, norm1_gain, q_weight, q_bias, kv_weight, kv_bias, o_weight, norm2_gain,
               gate_weight, up_weight, down_weight, seq_lengths, out_grad):
    f = front(layer_input, norm1_gain, q_weight, q_bias, kv_weight, kv_bias, o_weight, norm2_gain,
              gate_weight, up_weight, down_weight, seq_lengths, out_grad)
    b = back(f, layer_input, norm1_gain, q_weight, kv_weight, norm2_gain, out_grad)
    return finish(b)


def solution(mesh):
    rows, width = P(("dp", "gy"), "gx"), P("gx", "gy")
    return jax.shard_map(
        per_device,
        mesh=mesh,
        in_specs=(rows, P("gx"), width, P("gy"), P("gx", None), P(), P("gy", "gx"), P("gx"), width, width,
                  P("gy", "gx"), P("dp", None), rows),
        out_specs=(rows, rows, P("gx"), width, P("gy"), P("gx", None), P(), P("gy", "gx"), P("gx"), width, width,
                   P("gy", "gx")),
        check_vma=False,
    )
```

```python
import jax
import jax.numpy as jnp
import numpy as np
from jax import lax
from jax.experimental import pallas as pl
from jax.experimental.pallas import tpu as pltpu
from jax.sharding import PartitionSpec as P

f32 = jnp.float32
bf16 = jnp.bfloat16
MESH = pl.DeviceIdType.MESH
EPSILON = 1e-06
THETA = 1000000.0
NEGATIVE = -1e30
D = 1536
HALF = 768
BLOCK = 256
TOKENS = 1024
COLS = 1152
REAL = 1120
HEADS = 3
HEAD = 128


def dg(left, right, left_dim, right_dim):
    return lax.dot_general(
        left, right, (((left_dim,), (right_dim,)), ((), ())), preferred_element_type=f32
    )


def dot(left, right):
    return jnp.dot(left, right, preferred_element_type=f32)


class Names:
    def __init__(self, pairs):
        self.__dict__.update(pairs)


def rows_of(block, size=BLOCK):
    return pl.ds(pl.multiple_of(block * size, size), size)


class Copy:
    def __init__(self, copy, remote):
        self.copy, self.remote = copy, remote
        self.left = self.came = False
        copy.start()

    def wait_send(self):
        if not self.left:
            self.left = True
            self.copy.wait_send()

    def wait_recv(self):
        if not self.came:
            self.came = True
            self.copy.wait_recv()

    def wait(self):
        if not self.left:
            self.left = True
            self.copy.wait()


class Moves:
    def __init__(self, send, recv, local):
        self.send, self.recv, self.local = send, recv, local
        self.remotes = []
        self.locals = []

    def to(self, device, src, dst):
        i = len(self.remotes)
        copy = Copy(pltpu.make_async_remote_copy(
            src_ref=src, dst_ref=dst, send_sem=self.send.at[i], recv_sem=self.recv.at[i],
            device_id=device, device_id_type=MESH), True)
        self.remotes.append(copy)
        return copy

    def own(self, src, dst):
        copy = Copy(pltpu.make_async_copy(src, dst, self.local.at[len(self.locals)]), False)
        self.locals.append(copy)
        return copy

    out = own

    def settle(self, copies):
        for copy in copies:
            copy.wait_send()

    def finish(self):
        for copy in self.remotes:
            copy.wait_send()
            copy.wait_recv()
        for copy in self.locals:
            copy.wait()


class Place:
    def __init__(self):
        self.gx = lax.axis_index("gx")
        self.gy = lax.axis_index("gy")
        self.up = {"gy": lax.rem(self.gy + 1, 4)}
        self.down = {"gy": lax.rem(self.gy + 3, 4)}
        self.pal = {"gx": 1 - self.gx}
        self.blk = [lax.rem(self.gy + i, 4) for i in range(4)]
        self.cols = pl.ds(pl.multiple_of(self.gx * HALF, 128), HALF)


class GatherY:
    def __init__(self, moves, place, src, buf):
        self.m, self.p, self.src, self.buf = moves, place, src, buf

    def part(self, block, first, count):
        r = pl.ds(pl.multiple_of(block * BLOCK + first, 128), count)
        return self.buf.at[r, self.p.cols]

    def start(self):
        p = self.p
        there = self.part(p.blk[0], 0, BLOCK)
        self.a = self.m.to(p.up, self.src, there)
        self.b = self.m.to(p.down, self.src, there)
        self.c = self.m.to(p.pal, self.src, there)

    def own_ready(self):
        self.c.wait_recv()

    def relay(self):
        p, m = self.p, self.m
        low, high = p.blk[3], p.blk[1]
        self.a.wait_recv()
        x = self.part(low, 0, 128)
        self.d = m.to(p.up, x, x)
        self.b.wait_recv()
        x = self.part(high, 128, 128)
        self.e = m.to(p.down, x, x)
        x = self.part(low, 0, BLOCK)
        self.f = m.to(p.pal, x, x)
        x = self.part(high, 0, BLOCK)
        self.g = m.to(p.pal, x, x)

    def low_ready(self):
        self.f.wait_recv()

    def high_ready(self):
        self.g.wait_recv()

    def relay_pal(self):
        p, m = self.p, self.m
        far = p.blk[2]
        self.d.wait_recv()
        x = self.part(far, 0, 128)
        self.h = m.to(p.pal, x, x)
        self.e.wait_recv()
        x = self.part(far, 128, 128)
        self.i = m.to(p.pal, x, x)

    def far_ready(self):
        self.h.wait_recv()
        self.i.wait_recv()


class ScatterY:
    def __init__(self, moves, place, staged, held, low_half, high_half, from_low, from_high):
        self.m, self.p = moves, place
        self.staged, self.held = staged, held
        self.low_half, self.high_half = low_half, high_half
        self.from_low, self.from_high = from_low, from_high

    def far(self, value):
        p, m = self.p, self.m
        self.staged[0] = value.astype(bf16)
        self.a = m.to(p.up, self.staged.at[0, pl.ds(0, 128)], self.low_half)
        self.b = m.to(p.down, self.staged.at[0, pl.ds(128, 128)], self.high_half)

    def next_up(self, value):
        p, m = self.p, self.m
        self.staged[1, 128:] = value[128:].astype(bf16)
        self.c = m.to(p.up, self.staged.at[1, pl.ds(128, 128)], self.from_low.at[pl.ds(128, 128)])
        self.held[0] = value[:128]

    def next_down(self, value):
        p, m = self.p, self.m
        self.staged[2, :128] = value[:128].astype(bf16)
        self.d = m.to(p.down, self.staged.at[2, pl.ds(0, 128)], self.from_high.at[pl.ds(0, 128)])
        self.held[1] = value[128:]

    def relay(self):
        p, m = self.p, self.m
        self.a.wait_recv()
        self.staged[1, :128] = (self.held[0] + self.low_half[...].astype(f32)).astype(bf16)
        self.e = m.to(p.up, self.staged.at[1, pl.ds(0, 128)], self.from_low.at[pl.ds(0, 128)])
        self.b.wait_recv()
        self.staged[2, 128:] = (self.held[1] + self.high_half[...].astype(f32)).astype(bf16)
        self.f = m.to(p.down, self.staged.at[2, pl.ds(128, 128)], self.from_high.at[pl.ds(128, 128)])

    def result(self, own):
        self.c.wait_recv()
        self.d.wait_recv()
        self.e.wait_recv()
        self.f.wait_recv()
        return own + self.from_low[...].astype(f32) + self.from_high[...].astype(f32)


def enter(devices):
    barrier = pltpu.get_barrier_semaphore()
    for device in devices:
        pl.semaphore_signal(barrier, inc=1, device_id=device, device_id_type=MESH)
    return lambda: pl.semaphore_wait(barrier, len(devices))


def turned(value, cosine, signed_sine):
    return value * cosine + pltpu.roll(value, 64, 1) * signed_sine


def opening_of(ends, places):
    opening = jnp.zeros_like(places)
    for e in ends:
        opening = jnp.where(places >= e, jnp.maximum(opening, e), opening)
    return opening


def front_body(n):
    m = Moves(n.send, n.recv, n.local)
    front_steps(n, m)
    m.finish()


def front_steps(n, m):
    p = Place()
    gx, gy = p.gx, p.gy

    mine = pl.ds(pl.multiple_of(gx * REAL, 16), REAL)
    theirs = pl.ds(pl.multiple_of((1 - gx) * REAL, 16), REAL)
    weights = ((n.dw, n.Wd, 0), (n.gw, n.Wgu, 0), (n.uw, n.Wgu, COLS))
    loads = [m.own(w.at[mine], W.at[pl.ds(at, REAL), p.cols]) for w, W, at in weights]
    n.g1f[:, p.cols] = jnp.broadcast_to(n.g1[...].reshape(1, HALF), (8, HALF))
    enter([p.up, p.down, p.pal])()

    gather_x = GatherY(m, p, n.x, n.xb)
    gather_x.start()
    gain_move = m.to(p.pal, n.g1f.at[:, p.cols], n.g1f.at[:, p.cols])
    pair = p.gy // 2
    pair_cols = pl.ds(pl.multiple_of(pair * 256, 128), 256)
    own_rows = pl.ds(pl.multiple_of(gx * HALF, 128), HALF)
    kv_move = m.to(p.pal, n.kvw.at[:, pair_cols], n.Wkv.at[own_rows])
    q_move = m.to(p.pal, n.qw, n.Wq.at[own_rows])
    o_move = m.to(p.pal, n.ow, n.Wo.at[:, p.cols])

    n.xb[rows_of(gy), p.cols] = n.x[...]
    n.Wkv[own_rows, :] = n.kvw[:, pair_cols]
    n.Wq[own_rows, :] = n.qw[...]
    n.Wo[:, p.cols] = n.ow[...]

    ends = []
    running = jnp.int32(0)
    for k in range(4):
        running = running + n.seq[0, k]
        ends.append(running)
    lane = lax.broadcasted_iota(jnp.int32, (BLOCK, HEAD), 1)

    def table(i):
        places = lax.broadcasted_iota(jnp.int32, (BLOCK, HEAD), 0) + i * BLOCK
        position = places - opening_of(ends, places)
        angles = position.astype(f32) * n.freqs[...]
        r = rows_of(i)
        n.cosT[r, :] = jnp.cos(angles)
        n.sinT[r, :] = jnp.where(lane < 64, -jnp.sin(angles), jnp.sin(angles))

    pl.loop(0, 4)(table)
    m.out(n.cosT, n.cosO)
    m.out(n.sinT, n.sinO)

    gather_x.relay()

    def norm_block(block):
        r = rows_of(block)
        xf = n.xb[r, :].astype(f32)
        inverse = lax.rsqrt(jnp.sum(xf * xf, axis=1, keepdims=True) * (1.0 / D) + EPSILON)
        normed = (xf * inverse * n.g1f[0:1, :]).astype(bf16)
        n.nx[r, :] = normed
        kv = dot(normed, n.Wkv[...]) + n.kvb[pair_cols].reshape(1, 256)
        n.K[r, :] = turned(kv[:, :HEAD], n.cosT[r, :], n.sinT[r, :]).astype(bf16)
        n.V[r, :] = kv[:, HEAD:].astype(bf16)
        return inverse

    gain_move.wait_recv()
    kv_move.wait_recv()
    gather_x.own_ready()
    inverse = norm_block(p.blk[0])
    n.r1T[...] = jnp.broadcast_to(inverse, (BLOCK, HEAD))
    m.out(n.r1T, n.r1)
    gather_x.low_ready()
    norm_block(p.blk[3])
    gather_x.high_ready()
    norm_block(p.blk[1])
    gather_x.relay_pal()
    gather_og = GatherY(m, p, n.og, n.ogb)
    gather_og.start()
    weight_moves = [m.to(p.pal, w.at[theirs], W.at[pl.ds(at, REAL), p.cols]) for w, W, at in weights]
    n.ogb[rows_of(gy), p.cols] = n.og[...]
    for _, W, at in weights:
        W[at + REAL:at + COLS, :] = jnp.zeros((COLS - REAL, D), bf16)
    gather_x.far_ready()
    norm_block(p.blk[2])
    m.out(n.nx.at[:, p.cols], n.nxO)
    m.out(n.K, n.KO)
    m.out(n.V, n.VO)

    q_move.wait_recv()
    own_blocks = [gx, 3 - gx]
    for i, b in enumerate(own_blocks):
        r = rows_of(b)
        q = dot(n.nx[r, :], n.Wq[...]) + n.qb[...].reshape(1, 384)
        for h in range(HEADS):
            c = slice(h * HEAD, (h + 1) * HEAD)
            n.Q[i * BLOCK:(i + 1) * BLOCK, c] = turned(q[:, c], n.cosT[r, :], n.sinT[r, :]).astype(bf16)
    m.out(n.Q, n.QO)

    def attention(i, h):
        b = own_blocks[i]
        keys = 512 * (i + 1)
        at = 512 * i
        c = slice(h * HEAD, (h + 1) * HEAD)
        s = dg(n.Q[i * BLOCK:(i + 1) * BLOCK, c], n.K[:keys, :], 1, 1) * HEAD ** (-0.5)
        query = lax.broadcasted_iota(jnp.int32, (BLOCK, 1), 0) + b * BLOCK
        opening = opening_of(ends, query)
        key = lax.broadcasted_iota(jnp.int32, (BLOCK, keys), 1)
        s = jnp.where((key >= opening) & (key <= query), s, NEGATIVE)
        e = jnp.exp(s - jnp.max(s, axis=1, keepdims=True))
        probs = (e / jnp.sum(e, axis=1, keepdims=True)).astype(bf16)
        n.Pr[h * BLOCK:(h + 1) * BLOCK, at:at + keys] = probs
        out = dot(probs, n.V[:keys, :])
        n.att[rows_of(b), c] = out.astype(bf16)

    att_moves = []
    for i in (1, 0):
        for h in range(HEADS):
            attention(i, h)
        b = rows_of(own_blocks[i])
        att_moves.append(m.to(p.pal, n.att.at[b], n.att.at[b]))
        if i == 1:
            gather_og.relay()
    m.out(n.Pr, n.PO)
    gather_og.own_ready()
    loads[0].wait()
    weight_moves[0].wait_recv()

    def hidden_grad(block):
        r = rows_of(block)
        n.HG[r, :] = dg(n.ogb[r, :], n.Wd[...], 1, 1)

    for copy in att_moves:
        copy.wait_recv()

    m.settle([gather_x.a, gather_x.b, gather_x.c, gather_x.d, gather_x.e, gather_x.f, gather_x.g, gather_x.h, gather_x.i])

    def out_part(block):
        return dot(n.att[rows_of(block), :], n.ow[...])

    rs = ScatterY(m, p, n.staged, n.held, n.low_half, n.high_half, n.from_low, n.from_high)
    rs.far(out_part(p.blk[2]))
    rs.next_up(out_part(p.blk[1]))
    rs.next_down(out_part(p.blk[3]))
    n.mid[...] = out_part(p.blk[0]) + n.x[...].astype(f32)
    m.out(n.att, n.attO)
    gather_og.relay_pal()
    rs.relay()
    hidden_grad(p.blk[0])
    gather_og.low_ready()
    hidden_grad(p.blk[3])
    gather_og.high_ready()
    hidden_grad(p.blk[1])
    n.mid[...] = rs.result(n.mid[...])
    m.out(n.mid, n.midO)
    mid = n.mid[...]
    n.sums[0] = jnp.broadcast_to(jnp.sum(mid * mid, axis=1, keepdims=True), (BLOCK, HEAD))
    sum_move = m.to(p.pal, n.sums.at[0], n.sums.at[1])
    sum_move.wait_recv()
    r2 = lax.rsqrt((n.sums[0] + n.sums[1]) * (1.0 / D) + EPSILON)
    n.r2T[...] = r2
    m.out(n.r2T, n.r2)
    n.nto[...] = (n.mid[...] * r2[:, :1] * n.g2[...].reshape(1, HALF)).astype(bf16)
    gather_n = GatherY(m, p, n.nto, n.xb)
    gather_n.start()
    n.xb[rows_of(gy), p.cols] = n.nto[...]
    gather_og.far_ready()
    m.out(n.ogb, n.ogO)
    hidden_grad(p.blk[2])
    for k in (1, 2):
        loads[k].wait()
        weight_moves[k].wait_recv()
    m.out(n.Wgu, n.WguO)
    m.out(n.Wd, n.WdO)

    def feed_forward(block):
        r = rows_of(block)
        a = n.xb[r, :]
        both = dg(a, n.Wgu[...], 1, 1)
        gate = both[:, :COLS]
        upward = both[:, COLS:]
        back = n.HG[r, :]
        sg = jax.nn.sigmoid(gate)
        gs = gate * sg
        n.hid[r, :] = (gs * upward).astype(bf16)
        n.gu[r, :COLS] = (back * upward * sg * (1.0 + gate * (1.0 - sg))).astype(bf16)
        n.gu[r, COLS:] = (back * gs).astype(bf16)
        m.out(n.hid.at[r], n.hidO.at[r])
        m.out(n.gu.at[r], n.guO.at[r])

    gather_n.own_ready()
    feed_forward(p.blk[0])
    gather_n.relay()
    gather_n.low_ready()
    feed_forward(p.blk[3])
    gather_n.high_ready()
    feed_forward(p.blk[1])
    gather_n.relay_pal()
    gather_n.far_ready()
    m.out(n.xb, n.ntO)
    feed_forward(p.blk[2])

    o_move.wait_recv()
    m.out(n.Wo, n.WoO)


def kernel_call(name, body, inputs, outputs, scratch, collective_id, flops=0, moved=0):
    order = list(inputs) + list(outputs) + list(scratch)

    def kernel(*refs):
        body(Names(dict(zip(order, refs))))

    results = pl.pallas_call(
        kernel,
        out_shape=tuple(jax.ShapeDtypeStruct(s, d) for s, d, _ in outputs.values()),
        in_specs=[pl.BlockSpec(memory_space=s) for _, s in inputs.values()],
        out_specs=tuple(pl.BlockSpec(memory_space=s) for _, _, s in outputs.values()),
        scratch_shapes=list(scratch.values()),
        compiler_params=pltpu.CompilerParams(
            collective_id=collective_id, has_side_effects=True, vmem_limit_bytes=62 * 2**20),
        cost_estimate=pl.CostEstimate(flops=flops, bytes_accessed=moved, transcendentals=0),
        name=name,
    )(*[a for a, _ in inputs.values()])
    return Names(dict(zip(outputs, results)))


def frequencies():
    freqs = np.float32(THETA) ** (-np.arange(0, HEAD, 2, dtype=np.float32) / np.float32(HEAD))
    return np.concatenate([freqs, freqs])[None, :]


def front(layer_input, norm1_gain, q_weight, q_bias, kv_weight, kv_bias, o_weight, norm2_gain,
          gate_weight, up_weight, down_weight, seq_lengths, out_grad):
    vm, hbm, sm = pltpu.VMEM, pl.ANY, pltpu.SMEM
    inputs = dict(
        x=(layer_input, vm), og=(out_grad, vm), g1=(norm1_gain, vm), g2=(norm2_gain, vm),
        qw=(q_weight, vm), qb=(q_bias, vm), kvw=(kv_weight, vm), kvb=(kv_bias, vm),
        ow=(o_weight, vm), gw=(gate_weight.T, hbm), uw=(up_weight.T, hbm), dw=(down_weight, hbm),
        seq=(seq_lengths, sm), freqs=(frequencies(), vm))
    outputs = dict(
        ogO=((TOKENS, D), bf16, hbm), ntO=((TOKENS, D), bf16, hbm),
        hidO=((TOKENS, COLS), bf16, hbm), guO=((TOKENS, 2 * COLS), bf16, hbm),
        WguO=((2 * COLS, D), bf16, hbm), WdO=((COLS, D), bf16, hbm),
        midO=((BLOCK, HALF), f32, hbm), r1=((BLOCK, HEAD), f32, hbm), r2=((BLOCK, HEAD), f32, hbm),
        attO=((TOKENS, 384), bf16, hbm), PO=((HEADS * BLOCK, 1536), bf16, hbm), QO=((512, 384), bf16, hbm),
        KO=((TOKENS, HEAD), bf16, hbm), VO=((TOKENS, HEAD), bf16, hbm),
        cosO=((TOKENS, HEAD), f32, hbm), sinO=((TOKENS, HEAD), f32, hbm), nxO=((TOKENS, HALF), bf16, hbm),
        WoO=((384, D), bf16, hbm))
    v = pltpu.VMEM
    scratch = dict(
        Wgu=v((2 * COLS, D), bf16), Wd=v((COLS, D), bf16),
        Wkv=v((D, 256), bf16), Wq=v((D, 384), bf16), Wo=v((384, D), bf16), g1f=v((8, D), f32),
        xb=v((TOKENS, D), bf16), nx=v((TOKENS, D), bf16), ogb=v((TOKENS, D), bf16),
        cosT=v((TOKENS, HEAD), f32), sinT=v((TOKENS, HEAD), f32),
        K=v((TOKENS, HEAD), bf16), V=v((TOKENS, HEAD), bf16), Q=v((512, 384), bf16),
        Pr=v((HEADS * BLOCK, 1536), bf16), att=v((TOKENS, 384), bf16),
        staged=v((3, BLOCK, HALF), bf16), held=v((2, 128, HALF), f32),
        low_half=v((128, HALF), bf16), high_half=v((128, HALF), bf16),
        from_low=v((BLOCK, HALF), bf16), from_high=v((BLOCK, HALF), bf16),
        mid=v((BLOCK, HALF), f32), sums=v((2, BLOCK, HEAD), f32), r1T=v((BLOCK, HEAD), f32),
        r2T=v((BLOCK, HEAD), f32), nto=v((BLOCK, HALF), bf16),
        HG=v((TOKENS, COLS), f32), hid=v((TOKENS, COLS), bf16), gu=v((TOKENS, 2 * COLS), bf16),

        send=pltpu.SemaphoreType.DMA((48,)), recv=pltpu.SemaphoreType.DMA((48,)),
        local=pltpu.SemaphoreType.DMA((48,)))
    return kernel_call("front", front_body, inputs, outputs, scratch, 1, flops=30 * 10**9, moved=60 * 2**20)


UNITS = (4, 4, 5)
LEFT = 3328
SCALE = HEAD ** (-0.5)


class Ring:
    def __init__(self, place, along_x):
        z, x = place.z, place.x
        if isinstance(along_x, bool):
            c = x if along_x else z
            ids = [z * 4 + lax.rem(x + s, 4) if along_x else lax.rem(z + s, 4) * 4 + x for s in (1, 3, 2)]
        else:
            c = jnp.where(along_x, x, z)
            ids = [jnp.where(along_x, z * 4 + lax.rem(x + s, 4), lax.rem(z + s, 4) * 4 + x) for s in (1, 3, 2)]
        self.c = c
        self.up, self.down, self.over = ({"dp": i} for i in ids)
        self.next, self.far, self.last = [lax.rem(c + s, 4) for s in (1, 2, 3)]


def scatter_sum(m, ring, src, base, own, out, a, s1, s2, w):
    low, high = slice(0, w), slice(w, None)
    k1 = m.to(ring.up, src(ring.far, low), s1[0])
    k2 = m.to(ring.down, src(ring.far, high), s1[1])
    k3 = m.to(ring.up, src(ring.next, high), s2[0].at[:, w:])
    k4 = m.to(ring.down, src(ring.last, low), s2[1].at[:, :w])
    yield
    k1.wait_recv()
    a[0][...] = (base(0).astype(f32) + s1[0][...].astype(f32)).astype(bf16)
    k5 = m.to(ring.up, a[0], s2[0].at[:, :w])
    k2.wait_recv()
    a[1][...] = (base(1).astype(f32) + s1[1][...].astype(f32)).astype(bf16)
    k6 = m.to(ring.down, a[1], s2[1].at[:, w:])
    yield
    for k in (k3, k4, k5, k6):
        k.wait_recv()
    out[...] = (own().astype(f32) + s2[0][...].astype(f32) + s2[1][...].astype(f32)).astype(bf16)
    yield


def gather_ring(m, ring, part):
    k1 = m.to(ring.up, part(ring.c, None), part(ring.c, None))
    k2 = m.to(ring.down, part(ring.c, None), part(ring.c, None))
    yield
    k1.wait_recv()
    x = part(ring.last, 0)
    k3 = m.to(ring.up, x, x)
    k2.wait_recv()
    x = part(ring.next, 1)
    k4 = m.to(ring.down, x, x)
    yield
    k3.wait_recv()
    k4.wait_recv()
    yield


def aligned_start(start):
    return pl.multiple_of(start, 32)


def aligned(start, size, unit=16):
    return pl.ds(pl.multiple_of(start, unit), size)


def main_piece(n, m, p, i):
    k = UNITS[i]
    base = 256 * sum(UNITS[:i])
    r1, r2 = 64 * k, 16 * k
    own, a, s1, s2 = (getattr(n, f"{name}{i}") for name in ("own", "a", "s1", "s2"))
    b, t1, t2, T2 = (getattr(n, f"{name}{i}") for name in ("b", "t1", "t2", "T"))
    rings = [Ring(p, True), Ring(p, False)]
    loads = []
    first, second = [], []
    for h in range(2):
        one, two = rings[h], rings[1 - h]

        def src(j, lanes, h=h):
            lo, hi = lanes.start + h * HALF, (lanes.stop or HALF) + h * HALF
            return n.G.at[aligned(base + j * r1, r1, 64), pl.ds(lo, hi - lo)]

        loads.append([(src(one.c, slice(0, HALF)), own.at[h]), (src(one.next, slice(0, 384)), a.at[h, 0]),
                      (src(one.last, slice(384, HALF)), a.at[h, 1])])
        first.append(scatter_sum(
            m, one, src, lambda d, h=h: a[h, d], lambda h=h: own[h], own.at[h],
            [a.at[h, 0], a.at[h, 1]], [s1.at[h, 0], s1.at[h, 1]], [s2.at[h, 0], s2.at[h, 1]], 384))

        def src2(j, lanes, h=h):
            return own.at[h, aligned(j * r2, r2), pl.ds(lanes.start, (lanes.stop or HALF) - lanes.start)]

        def base2(d, h=h, two=two):
            if d == 0:
                return own[h, aligned(two.next * r2, r2), :384]
            return own[h, aligned(two.last * r2, r2), 384:]

        second.append(scatter_sum(
            m, two, src2, base2, lambda h=h, two=two: own[h, aligned(two.c * r2, r2), :], T2.at[h],
            [b.at[h, 0], b.at[h, 1]], [t1.at[h, 0], t1.at[h, 1]], [t2.at[h, 0], t2.at[h, 1]], 384))
    for g in first:
        next(g)
    loads = [m.own(*pair) for pairs in loads for pair in pairs]
    yield
    for c in loads:
        c.wait()
    for g in first:
        next(g)
    yield
    for g, g2 in zip(first, second):
        next(g)
        next(g2)
    yield
    for g in second:
        next(g)
    yield
    for g in second:
        next(g)
    one = Ring(p, p.gx == 0)
    two = Ring(p, p.gx != 0)

    def place(c1, c2, rows):
        return aligned(base + c1 * r1 + c2 * r2, rows)

    there = (Ring(p, p.gx != 0), Ring(p, p.gx == 0))
    mine = m.own(T2.at[p.gx], n.O.at[p.gx, place(one.c, two.c, r2)])
    swap = m.to(p.pal, T2.at[1 - p.gx], n.O.at[p.gx, place(there[0].c, there[1].c, r2)])
    yield
    mine.wait()
    swap.wait_recv()

    def part_two(j, half):
        r = place(one.c, j, r2)
        return n.O.at[:, r] if half is None else n.O.at[half, r]

    def part_one(j, half):
        r = place(j, jnp.int32(0), r1)
        return n.O.at[:, r] if half is None else n.O.at[half, r]

    g = gather_ring(m, two, part_two)
    next(g)
    yield
    next(g)
    yield
    next(g)
    g = gather_ring(m, one, part_one)
    next(g)
    yield
    next(g)
    yield
    next(g)
    yield


def small_piece(n, m, p):
    rings = [Ring(p, True), Ring(p, False)]
    r1, r2, W = 256, 64, 384
    lanes = [pl.ds(h * W, W) for h in range(2)]

    def spread(ring, src, dst):
        return [m.to(d, src(j), dst(k)) for k, (d, j) in enumerate(
            ((ring.up, ring.next), (ring.down, ring.last), (ring.over, ring.far)))]

    def total(own, came):
        return (own.astype(f32) + came[0].astype(f32)) + (came[1].astype(f32) + came[2].astype(f32))

    moves = [spread(rings[h], lambda j, h=h: n.M.at[aligned(j * r1, r1), lanes[h]], lambda k, h=h: n.Em.at[h, k])
             for h in range(2)]
    yield
    for h in range(2):
        for c in moves[h]:
            c.wait_recv()
        n.Tm[h] = total(n.M[aligned(rings[h].c * r1, r1), h * W:(h + 1) * W], n.Em[h]).astype(bf16)
        moves[h] = spread(rings[1 - h], lambda j, h=h: n.Tm.at[h, aligned(j * r2, r2)], lambda k, h=h: n.Fm.at[h, k])
    yield
    for h in range(2):
        one, two = rings[h], rings[1 - h]
        for c in moves[h]:
            c.wait_recv()
        n.Um[h] = total(n.Tm[h, aligned(two.c * r2, r2)], n.Fm[h]).astype(bf16)
        there = n.O4.at[aligned(one.c * r1 + two.c * r2, r2), lanes[h]]
        moves[h] = spread(two, lambda j, h=h: n.Um.at[h], lambda k, there=there: there)
        moves[h].append(m.own(n.Um.at[h], there))
    yield
    for h in range(2):
        for c in moves[h][:3]:
            c.wait_recv()
        moves[h][3].wait()
        there = n.O4.at[aligned(rings[h].c * r1, r1), lanes[h]]
        moves[h] = spread(rings[h], lambda j, there=there: there, lambda k, there=there: there)
    yield
    for h in range(2):
        for c in moves[h]:
            c.wait_recv()
    block = pl.ds(832, 144)
    far = {"gy": lax.rem(p.gy + 2, 4)}
    moves = [m.to(d, n.O4.at[block], n.Oy.at[p.gy]) for d in (p.up, p.down, far)]
    rest = [m.own(n.O4.at[block], n.Oy.at[p.gy])]
    for core in range(2):
        rest.append(m.own(n.O4.at[pl.ds(768 + 32 * core, 32)], n.O.at[core, pl.ds(LEFT, 32)]))
    yield
    for c in moves:
        c.wait_recv()
    for c in rest:
        c.wait()
    yield


SCHED = {
    "down": "0", "b0": "", "b1": "", "b2": "0", "b3": "", "own": "", "gate": "1",
    "result": "0", "ml": "", "up": "102",
    "c0": "", "c1": "", "ml1": "", "c2": "", "c3": "", "ml2": "10", "ml3": "0",
    "a10": "2", "a11": "", "a12": "10", "relay2": "", "a00": "", "a01": "", "a02": "21",
    "pair": "120", "m1": "12m", "m2": "2", "m3": "v1",
    "tail": "vm20vmv2m1m2m", "rest": "m012v"}


def vector_sum(n, m, p):
    coordinates = (p.x, p.z, p.gy)
    devices = (lambda s: {"dp": p.z * 4 + lax.rem(p.x + s, 4)}, lambda s: {"dp": lax.rem(p.z + s, 4) * 4 + p.x},
               lambda s: {"gy": lax.rem(p.gy + s, 4)})
    value = n.gain1[...]
    for d in range(3):
        slot = n.vectors.at[d, coordinates[d]]
        slot[...] = value
        moves = [m.to(devices[d](s), slot, slot) for s in (1, 3, 2)]
        yield
        for c in moves:
            c.wait_recv()
        value = (n.vectors[d, 0] + n.vectors[d, 1]) + (n.vectors[d, 2] + n.vectors[d, 3])
    n.gain1_sum[...] = value
    yield


def back_body(n):
    m = Moves(n.send, n.recv, n.local)
    back_steps(n, m)
    m.finish()


def back_steps(n, m):
    p = Place()
    dp = lax.axis_index("dp")
    p.z, p.x = lax.div(dp, 4), lax.rem(dp, 4)
    gx, gy = p.gx, p.gy
    pal_cols = pl.ds(pl.multiple_of((1 - gx) * HALF, 128), HALF)
    vm = Names({})
    load = {}

    def bring(name, src, dst):
        load[name] = m.own(src, dst)

    bring("og", n.ogf, n.ml)
    bring("hid", n.hid, n.ntV.at[:, pl.ds(0, COLS)])
    bring("gu", n.gu, n.guV)
    bring("Wgu", n.Wgu, n.WguV)
    bring("mid", n.mid, n.midV)
    bring("r2", n.r2, n.r2V)
    for name in ("Q", "K", "V", "cos", "sin", "r1"):
        bring(name, getattr(n, name), getattr(n, name + "V"))
    rings = [Ring(p, True), Ring(p, False)]
    gens = {str(i): main_piece(n, m, p, i) for i in range(3)}
    entered = enter([p.up, p.down, p.pal, rings[0].up, rings[0].down, rings[1].up, rings[1].down])

    def ar(spot):
        for name in SCHED[spot]:
            next(gens[name], None)

    def leave(slot, k, i, rows):
        at = k * REAL + i * BLOCK
        at = pl.multiple_of(at, 32) if isinstance(i, int) else aligned_start(at)
        return pltpu.make_async_copy(
            n.stage.at[slot, pl.ds(0, rows)], n.G.at[pl.ds(at, rows)], n.gsem.at[slot])

    def weight_grad(k, left, at, right, before_tail=lambda: None):
        @pl.loop(0, 4)
        def _(i):
            slot = lax.rem(i, 2)

            @pl.when(i >= 2)
            def _():
                leave(slot, k, i, BLOCK).wait()

            c = pl.ds(pl.multiple_of(i * BLOCK + at, 128), BLOCK)
            n.stage[slot] = dg(left[:, c], right[...], 0, 0).astype(bf16)
            leave(slot, k, i, BLOCK).start()

        leave(0, k, 2, BLOCK).wait()
        leave(1, k, 3, BLOCK).wait()
        before_tail()
        tail = dg(left[:, at + 4 * BLOCK:at + COLS], right[...], 0, 0).astype(bf16)
        n.stage[0, :REAL - 4 * BLOCK] = tail[:REAL - 4 * BLOCK]
        leave(0, k, 4, REAL - 4 * BLOCK).start()
        leave(0, k, 4, REAL - 4 * BLOCK).wait()

    for name in ("og", "hid"):
        load[name].wait()

    def down_ready():
        entered()
        ar("down")

    weight_grad(0, n.ntV, 0, n.ml, down_ready)
    bring("nt", n.nt, n.ntV)

    for name in ("gu", "Wgu"):
        load[name].wait()

    def two_sided(left, weight, take, give, held, names):
        order = (2, 1, 3, 0)
        moves = []
        for k, which in enumerate(order):
            r = rows_of(p.blk[which])
            if k >= 2:
                moves[k - 2].wait_send()
            give[k % 2] = dot(left(r), weight(pal_cols)).astype(bf16)
            moves.append(m.to(p.pal, give.at[k % 2], take.at[k]))
            held[k % 2] = dot(left(r), weight(p.cols))
            if k:
                moves[k - 1].wait_recv()
                yield held[(k - 1) % 2] + take[k - 1].astype(f32)
            ar(names[k])
        moves[3].wait_recv()
        moves[2].wait_send()
        moves[3].wait_send()
        yield held[1] + take[3].astype(f32)

    def scatter(letter):
        return ScatterY(m, p, n.staged, n.held, *(getattr(n, letter + name) for name in ("low", "high", "flow", "fhigh")))

    g = two_sided(lambda r: n.guV[r, :], lambda c: n.WguV[:, c], n.take, n.give, n.two, ("b0", "b1", "b2", "b3"))
    rs = scatter("A")
    rs.far(next(g))
    rs.next_up(next(g))
    rs.next_down(next(g))
    n.part[...] = next(g)
    ar("own")
    bring("Wd", n.Wd, n.WguV.at[pl.ds(0, COLS)])
    bring("P", n.P, n.WguV.at[pl.ds(COLS, HEADS * BLOCK)])
    bring("Wo", n.Wo, n.WguV.at[pl.ds(1920, 384)])
    load["nt"].wait()
    rs.relay()
    weight_grad(1, n.guV, 0, n.ntV)
    ar("gate")
    n.part[...] = rs.result(n.part[...])
    ar("result")
    load["mid"].wait()
    load["r2"].wait()
    r2 = n.r2V[:, :1]
    y2 = n.midV[...] * r2
    w2 = n.part[...] * n.g2[...].reshape(1, HALF)
    n.gain2[...] = jnp.broadcast_to(jnp.sum(n.part[...] * y2, axis=0, keepdims=True), (8, HALF))
    n.sums[0] = jnp.broadcast_to(jnp.sum(w2 * y2, axis=1, keepdims=True), (BLOCK, HEAD))
    sum_move = m.to(p.pal, n.sums.at[0], n.sums.at[1])
    sum_move.wait_recv()
    total = (n.sums[0] + n.sums[1])[:, :1] * (1.0 / D)
    n.mg[...] = n.og[...].astype(f32) + r2 * (w2 - y2 * total)
    n.mlo[...] = n.mg[...].astype(bf16)
    gather = GatherY(m, p, n.mlo, n.ml)
    gather.start()
    n.ml[rows_of(gy), p.cols] = n.mlo[...]
    ar("ml")
    weight_grad(2, n.guV, COLS, n.ntV)
    ar("up")
    bring("hid", n.hid, n.guV.at[:, pl.ds(0, COLS)])
    bring("nx", n.nx, n.guV.at[:, pl.ds(COLS, HALF)])
    bring("att", n.att, n.guV.at[:, pl.ds(COLS + HALF, 384)])
    left_row = aligned(768 + gx * 32, 32, 32)
    bring("left", n.G.at[pl.ds(LEFT, 32), p.cols], n.M.at[left_row])
    left_move = m.to(p.pal, n.G.at[pl.ds(LEFT, 32), pal_cols], n.M.at[left_row])

    load["hid"].wait()
    load["Wd"].wait()
    g = two_sided(lambda r: n.guV[r, :COLS], lambda c: n.WguV[:COLS, c], n.take, n.give, n.two, ("c0", "c1", "c2", "c3"))
    n.later[0] = next(g).astype(bf16)
    gather.relay()
    ar("ml1")
    for k in (1, 2):
        n.later[k] = next(g).astype(bf16)
    n.part[...] = next(g) + n.midV[...]
    ar("ml2")
    gather.relay_pal()
    m.settle([rs.a, rs.b, rs.c, rs.d, rs.e, rs.f])
    rs = scatter("B")
    rs.far(n.later[0].astype(f32))
    rs.next_up(n.later[1].astype(f32))
    rs.next_down(n.later[2].astype(f32))
    gather.own_ready()
    gather.low_ready()
    gather.high_ready()
    ar("ml3")

    for name in ("att", "Q", "K", "V", "cos", "sin", "nx", "Wo", "r1", "P", "left"):
        load[name].wait()
    gather.far_ready()
    n.M[0:384, :] = dg(n.guV[:, COLS + HALF:], n.ml[:, p.cols], 0, 0).astype(bf16)
    own_blocks = [gx, 3 - gx]
    q_moves = []
    for i in (1, 0):
        b = rows_of(own_blocks[i])
        keys, at = 512 * (i + 1), 512 * i
        n.ag[...] = dg(n.ml[b, :], n.WguV[1920:, :], 1, 1).astype(bf16)
        for h in range(HEADS):
            c = slice(h * HEAD, (h + 1) * HEAD)
            probs = n.WguV[COLS + h * BLOCK:COLS + (h + 1) * BLOCK, at:at + keys]
            probs_f = probs.astype(f32)
            prob_grads = dg(n.ag[:, c], n.VV[:keys, :], 1, 1)
            centre = jnp.sum(probs_f * prob_grads, axis=1, keepdims=True)
            score_grads = (probs_f * (prob_grads - centre)).astype(bf16)
            dq = dot(score_grads, n.KV[:keys, :]) * SCALE
            dk = dg(score_grads, n.QV[i * BLOCK:(i + 1) * BLOCK, c], 0, 0) * SCALE
            dv = dg(probs, n.ag[:, c], 0, 0)
            if i == 1 and h == 0:
                n.dkv[:, :HEAD] = dk
                n.dkv[:, HEAD:] = dv
            else:
                n.dkv[:keys, :HEAD] += dk
                n.dkv[:keys, HEAD:] += dv
            n.ql[b, c] = turned(dq, n.cosV[b, :], -n.sinV[b, :]).astype(bf16)
            ar(f"a{i}{h}")
        q_moves.append(m.to(p.pal, n.ql.at[b], n.ql.at[b]))
        if i == 1:
            rs.relay()
            ar("relay2")
    n.S[0] = n.dkv[...].astype(bf16)
    s_move = m.to(p.pal, n.S.at[0], n.S.at[1])
    n.block_out[...] = rs.result(n.part[...])
    s_move.wait_recv()
    both = n.S[0].astype(f32) + n.S[1].astype(f32)
    n.dkv[...] = both
    n.S2[...] = both.astype(bf16)
    odd = lax.rem(gy, 2)
    pair = {"gy": gy + 1 - 2 * odd}
    pair_move = m.to(pair, n.S2.at[:, pl.ds(pl.multiple_of((1 - odd) * HEAD, HEAD), HEAD)], n.pin)
    ar("pair")
    for copy in q_moves:
        copy.wait_recv()
    n.M[384:768, :] = dg(n.ql[...], n.guV[:, COLS:COLS + HALF], 0, 0).astype(bf16)
    pair_move.wait_recv()
    kv = n.dkv[:, pl.ds(pl.multiple_of(odd * HEAD, HEAD), HEAD)] + n.pin[...].astype(f32)
    is_key = (1 - odd).astype(f32)
    cosine = n.cosV[...] * is_key + (1.0 - is_key)
    sine = n.sinV[...] * is_key
    n.plow[...] = turned(kv, cosine, -sine).astype(bf16)
    n.M[832:960, :] = dg(n.plow[...], n.guV[:, COLS:COLS + HALF], 0, 0).astype(bf16)
    bias = jnp.concatenate([
        jnp.sum(n.ql[...].astype(f32), axis=0, keepdims=True),
        jnp.sum(n.plow[...].astype(f32), axis=0, keepdims=True),
        jnp.zeros((1, 256), f32)], axis=1)
    row = lax.broadcasted_iota(jnp.int32, (64, HALF), 0)
    n.M[960:, :] = jnp.where(row == 0, n.gain2[0:1, :], jnp.where(row == 1, bias, 0.0)).astype(bf16)

    def norm_one_part(block):
        r = rows_of(block)
        kvw = n.kvw[:, pl.ds(pl.multiple_of(gy * HEAD, HEAD), HEAD)]
        return dg(n.ql[r, :], n.qw[...], 1, 1) + dg(n.plow[r, :], kvw, 1, 1)

    m.settle([rs.a, rs.b, rs.c, rs.d, rs.e, rs.f])
    rs = scatter("A")
    rs.far(norm_one_part(p.blk[2]))
    rs.next_up(norm_one_part(p.blk[1]))
    rs.next_down(norm_one_part(p.blk[3]))
    n.part[...] = norm_one_part(p.blk[0])
    left_move.wait_recv()
    gens["m"] = small_piece(n, m, p)
    ar("m1")
    rs.relay()
    ar("m2")
    n.part[...] = rs.result(n.part[...])
    r1 = n.r1V[:, :1]
    y1 = n.x[...].astype(f32) * r1
    w1 = n.part[...] * n.g1[...].reshape(1, HALF)
    gain1 = jnp.sum(n.part[...] * y1, axis=0, keepdims=True)
    m.settle([sum_move])
    n.sums[0] = jnp.broadcast_to(jnp.sum(w1 * y1, axis=1, keepdims=True), (BLOCK, HEAD))
    sum_move = m.to(p.pal, n.sums.at[0], n.sums.at[2])
    n.gain1[...] = jnp.broadcast_to(gain1, (8, HALF))
    gens["v"] = vector_sum(n, m, p)
    ar("m3")
    sum_move.wait_recv()
    total = (n.sums[0] + n.sums[2])[:, :1] * (1.0 / D)
    n.input_grad[...] = n.mg[...] + r1 * (w1 - y1 * total)
    ar("tail")
    for _ in range(14):
        ar("rest")


def back(f, layer_input, norm1_gain, q_weight, kv_weight, norm2_gain, out_grad):
    vm, hbm = pltpu.VMEM, pl.ANY
    inputs = dict(
        x=(layer_input, vm), og=(out_grad, vm), g1=(norm1_gain, vm), g2=(norm2_gain, vm),
        qw=(q_weight, vm), kvw=(kv_weight, vm),
        ogf=(f.ogO, hbm), nt=(f.ntO, hbm), gu=(f.guO, hbm), Wgu=(f.WguO, hbm), hid=(f.hidO, hbm), Wd=(f.WdO, hbm), mid=(f.midO, hbm),
        r1=(f.r1, hbm), r2=(f.r2, hbm), att=(f.attO, hbm), P=(f.PO, hbm), Q=(f.QO, hbm), K=(f.KO, hbm),
        V=(f.VO, hbm), cos=(f.cosO, hbm), sin=(f.sinO, hbm), nx=(f.nxO, hbm), Wo=(f.WoO, hbm))
    outputs = dict(
        block_out=((BLOCK, HALF), f32, vm), input_grad=((BLOCK, HALF), f32, vm),
        O=((2, 3 * REAL, HALF), bf16, hbm), O4=((TOKENS, HALF), bf16, hbm), Oy=((4, 144, HALF), bf16, hbm),
        gain1_sum=((8, HALF), f32, vm), G=((3 * REAL, D), bf16, hbm))
    v = pltpu.VMEM
    scratch = dict(
        guV=v((TOKENS, 2 * COLS), bf16), WguV=v((2 * COLS, D), bf16), midV=v((BLOCK, HALF), f32),
        r1V=v((BLOCK, HEAD), f32), r2V=v((BLOCK, HEAD), f32), QV=v((512, 384), bf16),
        KV=v((TOKENS, HEAD), bf16), VV=v((TOKENS, HEAD), bf16), cosV=v((TOKENS, HEAD), f32),
        sinV=v((TOKENS, HEAD), f32), ntV=v((TOKENS, D), bf16),
        take=v((4, BLOCK, HALF), bf16), give=v((2, BLOCK, HALF), bf16), two=v((2, BLOCK, HALF), f32),
        staged=v((3, BLOCK, HALF), bf16), held=v((2, 128, HALF), f32),
        part=v((BLOCK, HALF), f32), later=v((3, BLOCK, HALF), bf16), stage=v((2, BLOCK, D), bf16),
        gain1=v((8, HALF), f32), vectors=v((3, 4, 8, HALF), f32), gain2=v((8, HALF), f32), sums=v((3, BLOCK, HEAD), f32),
        mg=v((BLOCK, HALF), f32), mlo=v((BLOCK, HALF), bf16), ml=v((TOKENS, D), bf16),
        ag=v((BLOCK, 384), bf16), dkv=v((TOKENS, 256), f32), ql=v((TOKENS, 384), bf16), S=v((2, TOKENS, 256), bf16),
        S2=v((TOKENS, 256), bf16), pin=v((TOKENS, HEAD), bf16), plow=v((TOKENS, HEAD), bf16), M=v((TOKENS, HALF), bf16),
        Em=v((2, 3, 256, 384), bf16), Tm=v((2, 256, 384), bf16), Fm=v((2, 3, 64, 384), bf16), Um=v((2, 64, 384), bf16))
    for letter in "AB":
        scratch.update({letter + "low": v((128, HALF), bf16), letter + "high": v((128, HALF), bf16),
                        letter + "flow": v((BLOCK, HALF), bf16), letter + "fhigh": v((BLOCK, HALF), bf16)})
    for i, k in enumerate(UNITS):
        r1, r2 = 64 * k, 16 * k
        scratch.update({
            f"own{i}": v((2, r1, HALF), bf16), f"a{i}": v((2, 2, r1, 384), bf16), f"s1{i}": v((2, 2, r1, 384), bf16),
            f"s2{i}": v((2, 2, r1, HALF), bf16), f"b{i}": v((2, 2, r2, 384), bf16), f"t1{i}": v((2, 2, r2, 384), bf16),
            f"t2{i}": v((2, 2, r2, HALF), bf16), f"T{i}": v((2, r2, HALF), bf16)})
    scratch.update(send=pltpu.SemaphoreType.DMA((200,)), recv=pltpu.SemaphoreType.DMA((200,)),
                   local=pltpu.SemaphoreType.DMA((64,)), gsem=pltpu.SemaphoreType.DMA((2,)))
    return kernel_call("back", back_body, inputs, outputs, scratch, 2, flops=16 * 10**9, moved=60 * 2**20)


def finish(b):
    PART = 224
    big = b.O.reshape(2, 3, REAL, HALF)

    def kernel(down, gate, up, small, shared, block, grad, gain, down_out, gate_out, up_out, o_out, q_out, kv_out,
               block_out, grad_out, gain1_out, gain2_out, q_bias_out, kv_bias_out):
        down_out[...] = down[0].astype(f32)
        gate_out[...] = gate[0].astype(f32)
        up_out[...] = up[0].astype(f32)
        block_out[...] = block[...]
        grad_out[...] = grad[...]

        @pl.when((pl.program_id(0) == 0) & (pl.program_id(1) == 0))
        def _():
            o_out[...] = small[:384, :].astype(f32)
            q_out[...] = small[384:768, :].astype(f32).T
            total = jnp.zeros((16, HALF), f32)
            for k in range(4):
                kv_out[:, k * HEAD:(k + 1) * HEAD] = shared[k, :HEAD, :].astype(f32).T
                vectors = shared[k, HEAD:, :].astype(f32)
                total = total + vectors
                kv_bias_out[k * HEAD:(k + 1) * HEAD] = vectors[1, 384:512]
            gain1_out[...] = gain[0]
            gain2_out[...] = total[0]
            q_bias_out[...] = small[960:976, :].astype(f32)[1, :384]

    def block(t):
        return pl.BlockSpec((1, 1, PART, HALF), lambda i, j, t=t: (i, t, j, 0))

    def whole(*shape):
        return pl.BlockSpec(shape, lambda i, j: (0,) * len(shape))

    def array(*shape):
        return jax.ShapeDtypeStruct(shape, f32)

    out = pl.BlockSpec((1, PART, HALF), lambda i, j: (i, j, 0))
    rows = pl.BlockSpec((BLOCK // 2, HALF), lambda i, j: (i, 0))
    weight = array(2, REAL, HALF)
    down, gate, up, o, q, kv, block_out, grad, gain1, gain2, q_bias, kv_bias = pl.pallas_call(
        kernel,
        grid=(2, REAL // PART),
        in_specs=[block(0), block(1), block(2), whole(TOKENS, HALF), whole(4, 144, HALF), rows, rows, whole(8, HALF)],
        out_specs=[out, out, out, whole(384, HALF), whole(HALF, 384), whole(HALF, 512), rows, rows,
                   whole(HALF), whole(HALF), whole(384), whole(512)],
        out_shape=[weight, weight, weight, array(384, HALF), array(HALF, 384), array(HALF, 512),
                   array(BLOCK, HALF), array(BLOCK, HALF), array(HALF), array(HALF), array(384), array(512)],
        compiler_params=pltpu.CompilerParams(vmem_limit_bytes=60 * 2**20),
        name="finish",
    )(big, big, big, b.O4, b.Oy, b.block_out, b.input_grad, b.gain1_sum)

    def flat(w):
        return w.reshape(2 * REAL, HALF)

    return block_out, grad, gain1, q, q_bias, kv, kv_bias, o, gain2, flat(gate).T, flat(up).T, flat(down)


def per_device(layer_input, norm1_gain, q_weight, q_bias, kv_weight, kv_bias, o_weight, norm2_gain,
               gate_weight, up_weight, down_weight, seq_lengths, out_grad):
    f = front(layer_input, norm1_gain, q_weight, q_bias, kv_weight, kv_bias, o_weight, norm2_gain,
              gate_weight, up_weight, down_weight, seq_lengths, out_grad)
    b = back(f, layer_input, norm1_gain, q_weight, kv_weight, norm2_gain, out_grad)
    return finish(b)


def solution(mesh):
    rows, width = P(("dp", "gy"), "gx"), P("gx", "gy")
    return jax.shard_map(
        per_device,
        mesh=mesh,
        in_specs=(rows, P("gx"), width, P("gy"), P("gx", None), P(), P("gy", "gx"), P("gx"), width, width,
                  P("gy", "gx"), P("dp", None), rows),
        out_specs=(rows, rows, P("gx"), width, P("gy"), P("gx", None), P(), P("gy", "gx"), P("gx"), width, width,
                   P("gy", "gx")),
        check_vma=False,
    )
```

```python
import jax
import jax.numpy as jnp
import numpy as np
from jax import lax
from jax.experimental import pallas as pl
from jax.experimental.pallas import tpu as pltpu
from jax.sharding import PartitionSpec as P

f32 = jnp.float32
bf16 = jnp.bfloat16
MESH = pl.DeviceIdType.MESH
EPSILON = 1e-06
THETA = 1000000.0
NEGATIVE = -1e30
D = 1536
HALF = 768
BLOCK = 256
TOKENS = 1024
COLS = 1152
REAL = 1120
HEADS = 3
HEAD = 128


def dg(left, right, left_dim, right_dim):
    return lax.dot_general(
        left, right, (((left_dim,), (right_dim,)), ((), ())), preferred_element_type=f32
    )


def dot(left, right):
    return jnp.dot(left, right, preferred_element_type=f32)


class Names:
    def __init__(self, pairs):
        self.__dict__.update(pairs)


def rows_of(block, size=BLOCK):
    return pl.ds(pl.multiple_of(block * size, size), size)


class Copy:
    def __init__(self, copy, remote):
        self.copy, self.remote = copy, remote
        self.left = self.came = False
        copy.start()

    def wait_send(self):
        if not self.left:
            self.left = True
            self.copy.wait_send()

    def wait_recv(self):
        if not self.came:
            self.came = True
            self.copy.wait_recv()

    def wait(self):
        if not self.left:
            self.left = True
            self.copy.wait()


class Moves:
    def __init__(self, send, recv, local):
        self.send, self.recv, self.local = send, recv, local
        self.remotes = []
        self.locals = []

    def to(self, device, src, dst):
        i = len(self.remotes)
        copy = Copy(pltpu.make_async_remote_copy(
            src_ref=src, dst_ref=dst, send_sem=self.send.at[i], recv_sem=self.recv.at[i],
            device_id=device, device_id_type=MESH), True)
        self.remotes.append(copy)
        return copy

    def own(self, src, dst):
        copy = Copy(pltpu.make_async_copy(src, dst, self.local.at[len(self.locals)]), False)
        self.locals.append(copy)
        return copy

    out = own

    def settle(self, copies):
        for copy in copies:
            copy.wait_send()

    def finish(self):
        for copy in self.remotes:
            copy.wait_send()
            copy.wait_recv()
        for copy in self.locals:
            copy.wait()


class Place:
    def __init__(self):
        self.gx = lax.axis_index("gx")
        self.gy = lax.axis_index("gy")
        self.up = {"gy": lax.rem(self.gy + 1, 4)}
        self.down = {"gy": lax.rem(self.gy + 3, 4)}
        self.pal = {"gx": 1 - self.gx}
        self.blk = [lax.rem(self.gy + i, 4) for i in range(4)]
        self.cols = pl.ds(pl.multiple_of(self.gx * HALF, 128), HALF)


class GatherY:
    def __init__(self, moves, place, src, buf):
        self.m, self.p, self.src, self.buf = moves, place, src, buf

    def part(self, block, first, count):
        r = pl.ds(pl.multiple_of(block * BLOCK + first, 128), count)
        return self.buf.at[r, self.p.cols]

    def start(self):
        p = self.p
        there = self.part(p.blk[0], 0, BLOCK)
        self.a = self.m.to(p.up, self.src, there)
        self.b = self.m.to(p.down, self.src, there)
        self.c = self.m.to(p.pal, self.src, there)

    def own_ready(self):
        self.c.wait_recv()

    def relay(self):
        p, m = self.p, self.m
        low, high = p.blk[3], p.blk[1]
        self.a.wait_recv()
        x = self.part(low, 0, 128)
        self.d = m.to(p.up, x, x)
        self.b.wait_recv()
        x = self.part(high, 128, 128)
        self.e = m.to(p.down, x, x)
        x = self.part(low, 0, BLOCK)
        self.f = m.to(p.pal, x, x)
        x = self.part(high, 0, BLOCK)
        self.g = m.to(p.pal, x, x)

    def low_ready(self):
        self.f.wait_recv()

    def high_ready(self):
        self.g.wait_recv()

    def relay_pal(self):
        p, m = self.p, self.m
        far = p.blk[2]
        self.d.wait_recv()
        x = self.part(far, 0, 128)
        self.h = m.to(p.pal, x, x)
        self.e.wait_recv()
        x = self.part(far, 128, 128)
        self.i = m.to(p.pal, x, x)

    def far_ready(self):
        self.h.wait_recv()
        self.i.wait_recv()


class ScatterY:
    def __init__(self, moves, place, staged, held, low_half, high_half, from_low, from_high):
        self.m, self.p = moves, place
        self.staged, self.held = staged, held
        self.low_half, self.high_half = low_half, high_half
        self.from_low, self.from_high = from_low, from_high

    def far(self, value):
        p, m = self.p, self.m
        self.staged[0] = value.astype(bf16)
        self.a = m.to(p.up, self.staged.at[0, pl.ds(0, 128)], self.low_half)
        self.b = m.to(p.down, self.staged.at[0, pl.ds(128, 128)], self.high_half)

    def next_up(self, value):
        p, m = self.p, self.m
        self.staged[1, 128:] = value[128:].astype(bf16)
        self.c = m.to(p.up, self.staged.at[1, pl.ds(128, 128)], self.from_low.at[pl.ds(128, 128)])
        self.held[0] = value[:128]

    def next_down(self, value):
        p, m = self.p, self.m
        self.staged[2, :128] = value[:128].astype(bf16)
        self.d = m.to(p.down, self.staged.at[2, pl.ds(0, 128)], self.from_high.at[pl.ds(0, 128)])
        self.held[1] = value[128:]

    def relay(self):
        p, m = self.p, self.m
        self.a.wait_recv()
        self.staged[1, :128] = (self.held[0] + self.low_half[...].astype(f32)).astype(bf16)
        self.e = m.to(p.up, self.staged.at[1, pl.ds(0, 128)], self.from_low.at[pl.ds(0, 128)])
        self.b.wait_recv()
        self.staged[2, 128:] = (self.held[1] + self.high_half[...].astype(f32)).astype(bf16)
        self.f = m.to(p.down, self.staged.at[2, pl.ds(128, 128)], self.from_high.at[pl.ds(128, 128)])

    def result(self, own):
        self.c.wait_recv()
        self.d.wait_recv()
        self.e.wait_recv()
        self.f.wait_recv()
        return own + self.from_low[...].astype(f32) + self.from_high[...].astype(f32)


def enter(devices):
    barrier = pltpu.get_barrier_semaphore()
    for device in devices:
        pl.semaphore_signal(barrier, inc=1, device_id=device, device_id_type=MESH)
    return lambda: pl.semaphore_wait(barrier, len(devices))


def turned(value, cosine, signed_sine):
    return value * cosine + pltpu.roll(value, 64, 1) * signed_sine


def opening_of(ends, places):
    opening = jnp.zeros_like(places)
    for e in ends:
        opening = jnp.where(places >= e, jnp.maximum(opening, e), opening)
    return opening


def front_body(n):
    m = Moves(n.send, n.recv, n.local)
    front_steps(n, m)
    m.finish()


def front_steps(n, m):
    p = Place()
    gx, gy = p.gx, p.gy

    mine = pl.ds(pl.multiple_of(gx * REAL, 16), REAL)
    theirs = pl.ds(pl.multiple_of((1 - gx) * REAL, 16), REAL)
    weights = ((n.dw, n.Wd, 0), (n.gw, n.Wgu, 0), (n.uw, n.Wgu, COLS))
    loads = [m.own(w.at[mine], W.at[pl.ds(at, REAL), p.cols]) for w, W, at in weights]
    n.g1f[:, p.cols] = jnp.broadcast_to(n.g1[...].reshape(1, HALF), (8, HALF))
    enter([p.up, p.down, p.pal])()

    gather_x = GatherY(m, p, n.x, n.xb)
    gather_x.start()
    gain_move = m.to(p.pal, n.g1f.at[:, p.cols], n.g1f.at[:, p.cols])
    pair = p.gy // 2
    pair_cols = pl.ds(pl.multiple_of(pair * 256, 128), 256)
    own_rows = pl.ds(pl.multiple_of(gx * HALF, 128), HALF)
    kv_move = m.to(p.pal, n.kvw.at[:, pair_cols], n.Wkv.at[own_rows])
    q_move = m.to(p.pal, n.qw, n.Wq.at[own_rows])
    o_move = m.to(p.pal, n.ow, n.Wo.at[:, p.cols])

    n.xb[rows_of(gy), p.cols] = n.x[...]
    n.Wkv[own_rows, :] = n.kvw[:, pair_cols]
    n.Wq[own_rows, :] = n.qw[...]
    n.Wo[:, p.cols] = n.ow[...]

    ends = []
    running = jnp.int32(0)
    for k in range(4):
        running = running + n.seq[0, k]
        ends.append(running)
    lane = lax.broadcasted_iota(jnp.int32, (BLOCK, HEAD), 1)

    def table(i):
        places = lax.broadcasted_iota(jnp.int32, (BLOCK, HEAD), 0) + i * BLOCK
        position = places - opening_of(ends, places)
        angles = position.astype(f32) * n.freqs[...]
        r = rows_of(i)
        n.cosT[r, :] = jnp.cos(angles)
        n.sinT[r, :] = jnp.where(lane < 64, -jnp.sin(angles), jnp.sin(angles))

    pl.loop(0, 4)(table)
    m.out(n.cosT, n.cosO)
    m.out(n.sinT, n.sinO)

    gather_x.relay()

    def norm_block(block):
        r = rows_of(block)
        xf = n.xb[r, :].astype(f32)
        inverse = lax.rsqrt(jnp.sum(xf * xf, axis=1, keepdims=True) * (1.0 / D) + EPSILON)
        normed = (xf * inverse * n.g1f[0:1, :]).astype(bf16)
        n.nx[r, :] = normed
        kv = dot(normed, n.Wkv[...]) + n.kvb[pair_cols].reshape(1, 256)
        n.K[r, :] = turned(kv[:, :HEAD], n.cosT[r, :], n.sinT[r, :]).astype(bf16)
        n.V[r, :] = kv[:, HEAD:].astype(bf16)
        return inverse

    gain_move.wait_recv()
    kv_move.wait_recv()
    gather_x.own_ready()
    inverse = norm_block(p.blk[0])
    n.r1T[...] = jnp.broadcast_to(inverse, (BLOCK, HEAD))
    m.out(n.r1T, n.r1)
    gather_x.low_ready()
    norm_block(p.blk[3])
    gather_x.high_ready()
    norm_block(p.blk[1])
    gather_x.relay_pal()
    gather_og = GatherY(m, p, n.og, n.ogb)
    gather_og.start()
    weight_moves = [m.to(p.pal, w.at[theirs], W.at[pl.ds(at, REAL), p.cols]) for w, W, at in weights]
    n.ogb[rows_of(gy), p.cols] = n.og[...]
    for _, W, at in weights:
        W[at + REAL:at + COLS, :] = jnp.zeros((COLS - REAL, D), bf16)
    gather_x.far_ready()
    norm_block(p.blk[2])
    m.out(n.nx.at[:, p.cols], n.nxO)
    m.out(n.K, n.KO)
    m.out(n.V, n.VO)

    q_move.wait_recv()
    own_blocks = [gx, 3 - gx]
    for i, b in enumerate(own_blocks):
        r = rows_of(b)
        q = dot(n.nx[r, :], n.Wq[...]) + n.qb[...].reshape(1, 384)
        for h in range(HEADS):
            c = slice(h * HEAD, (h + 1) * HEAD)
            n.Q[i * BLOCK:(i + 1) * BLOCK, c] = turned(q[:, c], n.cosT[r, :], n.sinT[r, :]).astype(bf16)
    m.out(n.Q, n.QO)

    def attention(i, h):
        b = own_blocks[i]
        keys = 512 * (i + 1)
        at = 512 * i
        c = slice(h * HEAD, (h + 1) * HEAD)
        s = dg(n.Q[i * BLOCK:(i + 1) * BLOCK, c], n.K[:keys, :], 1, 1) * HEAD ** (-0.5)
        query = lax.broadcasted_iota(jnp.int32, (BLOCK, 1), 0) + b * BLOCK
        opening = opening_of(ends, query)
        key = lax.broadcasted_iota(jnp.int32, (BLOCK, keys), 1)
        s = jnp.where((key >= opening) & (key <= query), s, NEGATIVE)
        e = jnp.exp(s - jnp.max(s, axis=1, keepdims=True))
        probs = (e / jnp.sum(e, axis=1, keepdims=True)).astype(bf16)
        n.Pr[h * BLOCK:(h + 1) * BLOCK, at:at + keys] = probs
        out = dot(probs, n.V[:keys, :])
        n.att[rows_of(b), c] = out.astype(bf16)

    att_moves = []
    for i in (1, 0):
        for h in range(HEADS):
            attention(i, h)
        b = rows_of(own_blocks[i])
        att_moves.append(m.to(p.pal, n.att.at[b], n.att.at[b]))
        if i == 1:
            gather_og.relay()
    m.out(n.Pr, n.PO)
    gather_og.own_ready()
    loads[0].wait()
    weight_moves[0].wait_recv()

    def hidden_grad(block):
        r = rows_of(block)
        n.HG[r, :] = dg(n.ogb[r, :], n.Wd[...], 1, 1)

    for copy in att_moves:
        copy.wait_recv()

    m.settle([gather_x.a, gather_x.b, gather_x.c, gather_x.d, gather_x.e, gather_x.f, gather_x.g, gather_x.h, gather_x.i])

    def out_part(block):
        return dot(n.att[rows_of(block), :], n.ow[...])

    rs = ScatterY(m, p, n.staged, n.held, n.low_half, n.high_half, n.from_low, n.from_high)
    rs.far(out_part(p.blk[2]))
    rs.next_up(out_part(p.blk[1]))
    rs.next_down(out_part(p.blk[3]))
    n.mid[...] = out_part(p.blk[0]) + n.x[...].astype(f32)
    m.out(n.att, n.attO)
    gather_og.relay_pal()
    rs.relay()
    hidden_grad(p.blk[0])
    gather_og.low_ready()
    hidden_grad(p.blk[3])
    gather_og.high_ready()
    hidden_grad(p.blk[1])
    n.mid[...] = rs.result(n.mid[...])
    m.out(n.mid, n.midO)
    mid = n.mid[...]
    n.sums[0] = jnp.broadcast_to(jnp.sum(mid * mid, axis=1, keepdims=True), (BLOCK, HEAD))
    sum_move = m.to(p.pal, n.sums.at[0], n.sums.at[1])
    sum_move.wait_recv()
    r2 = lax.rsqrt((n.sums[0] + n.sums[1]) * (1.0 / D) + EPSILON)
    n.r2T[...] = r2
    m.out(n.r2T, n.r2)
    n.nto[...] = (n.mid[...] * r2[:, :1] * n.g2[...].reshape(1, HALF)).astype(bf16)
    gather_n = GatherY(m, p, n.nto, n.xb)
    gather_n.start()
    n.xb[rows_of(gy), p.cols] = n.nto[...]
    gather_og.far_ready()
    m.out(n.ogb, n.ogO)
    hidden_grad(p.blk[2])
    for k in (1, 2):
        loads[k].wait()
        weight_moves[k].wait_recv()
    m.out(n.Wgu, n.WguO)
    m.out(n.Wd, n.WdO)

    def feed_forward(block):
        r = rows_of(block)
        a = n.xb[r, :]
        both = dg(a, n.Wgu[...], 1, 1)
        gate = both[:, :COLS]
        upward = both[:, COLS:]
        back = n.HG[r, :]
        sg = jax.nn.sigmoid(gate)
        gs = gate * sg
        n.hid[r, :] = (gs * upward).astype(bf16)
        n.gu[r, :COLS] = (back * upward * sg * (1.0 + gate * (1.0 - sg))).astype(bf16)
        n.gu[r, COLS:] = (back * gs).astype(bf16)
        m.out(n.hid.at[r], n.hidO.at[r])
        m.out(n.gu.at[r], n.guO.at[r])

    gather_n.own_ready()
    feed_forward(p.blk[0])
    gather_n.relay()
    gather_n.low_ready()
    feed_forward(p.blk[3])
    gather_n.high_ready()
    feed_forward(p.blk[1])
    gather_n.relay_pal()
    gather_n.far_ready()
    m.out(n.xb, n.ntO)
    feed_forward(p.blk[2])

    o_move.wait_recv()
    m.out(n.Wo, n.WoO)


def kernel_call(name, body, inputs, outputs, scratch, collective_id, flops=0, moved=0):
    order = list(inputs) + list(outputs) + list(scratch)

    def kernel(*refs):
        body(Names(dict(zip(order, refs))))

    results = pl.pallas_call(
        kernel,
        out_shape=tuple(jax.ShapeDtypeStruct(s, d) for s, d, _ in outputs.values()),
        in_specs=[pl.BlockSpec(memory_space=s) for _, s in inputs.values()],
        out_specs=tuple(pl.BlockSpec(memory_space=s) for _, _, s in outputs.values()),
        scratch_shapes=list(scratch.values()),
        compiler_params=pltpu.CompilerParams(
            collective_id=collective_id, has_side_effects=True, vmem_limit_bytes=62 * 2**20),
        cost_estimate=pl.CostEstimate(flops=flops, bytes_accessed=moved, transcendentals=0),
        name=name,
    )(*[a for a, _ in inputs.values()])
    return Names(dict(zip(outputs, results)))


def frequencies():
    freqs = np.float32(THETA) ** (-np.arange(0, HEAD, 2, dtype=np.float32) / np.float32(HEAD))
    return np.concatenate([freqs, freqs])[None, :]


def front(layer_input, norm1_gain, q_weight, q_bias, kv_weight, kv_bias, o_weight, norm2_gain,
          gate_weight, up_weight, down_weight, seq_lengths, out_grad):
    vm, hbm, sm = pltpu.VMEM, pl.ANY, pltpu.SMEM
    inputs = dict(
        x=(layer_input, vm), og=(out_grad, vm), g1=(norm1_gain, vm), g2=(norm2_gain, vm),
        qw=(q_weight, vm), qb=(q_bias, vm), kvw=(kv_weight, vm), kvb=(kv_bias, vm),
        ow=(o_weight, vm), gw=(gate_weight.T, hbm), uw=(up_weight.T, hbm), dw=(down_weight, hbm),
        seq=(seq_lengths, sm), freqs=(frequencies(), vm))
    outputs = dict(
        ogO=((TOKENS, D), bf16, hbm), ntO=((TOKENS, D), bf16, hbm),
        hidO=((TOKENS, COLS), bf16, hbm), guO=((TOKENS, 2 * COLS), bf16, hbm),
        WguO=((2 * COLS, D), bf16, hbm), WdO=((COLS, D), bf16, hbm),
        midO=((BLOCK, HALF), f32, hbm), r1=((BLOCK, HEAD), f32, hbm), r2=((BLOCK, HEAD), f32, hbm),
        attO=((TOKENS, 384), bf16, hbm), PO=((HEADS * BLOCK, 1536), bf16, hbm), QO=((512, 384), bf16, hbm),
        KO=((TOKENS, HEAD), bf16, hbm), VO=((TOKENS, HEAD), bf16, hbm),
        cosO=((TOKENS, HEAD), f32, hbm), sinO=((TOKENS, HEAD), f32, hbm), nxO=((TOKENS, HALF), bf16, hbm),
        WoO=((384, D), bf16, hbm))
    v = pltpu.VMEM
    scratch = dict(
        Wgu=v((2 * COLS, D), bf16), Wd=v((COLS, D), bf16),
        Wkv=v((D, 256), bf16), Wq=v((D, 384), bf16), Wo=v((384, D), bf16), g1f=v((8, D), f32),
        xb=v((TOKENS, D), bf16), nx=v((TOKENS, D), bf16), ogb=v((TOKENS, D), bf16),
        cosT=v((TOKENS, HEAD), f32), sinT=v((TOKENS, HEAD), f32),
        K=v((TOKENS, HEAD), bf16), V=v((TOKENS, HEAD), bf16), Q=v((512, 384), bf16),
        Pr=v((HEADS * BLOCK, 1536), bf16), att=v((TOKENS, 384), bf16),
        staged=v((3, BLOCK, HALF), bf16), held=v((2, 128, HALF), f32),
        low_half=v((128, HALF), bf16), high_half=v((128, HALF), bf16),
        from_low=v((BLOCK, HALF), bf16), from_high=v((BLOCK, HALF), bf16),
        mid=v((BLOCK, HALF), f32), sums=v((2, BLOCK, HEAD), f32), r1T=v((BLOCK, HEAD), f32),
        r2T=v((BLOCK, HEAD), f32), nto=v((BLOCK, HALF), bf16),
        HG=v((TOKENS, COLS), f32), hid=v((TOKENS, COLS), bf16), gu=v((TOKENS, 2 * COLS), bf16),

        send=pltpu.SemaphoreType.DMA((48,)), recv=pltpu.SemaphoreType.DMA((48,)),
        local=pltpu.SemaphoreType.DMA((48,)))
    return kernel_call("front", front_body, inputs, outputs, scratch, 1, flops=30 * 10**9, moved=60 * 2**20)


UNITS = (4, 4, 5)
LEFT = 3328
SCALE = HEAD ** (-0.5)


class Ring:
    def __init__(self, place, along_x):
        z, x = place.z, place.x
        if isinstance(along_x, bool):
            c = x if along_x else z
            ids = [z * 4 + lax.rem(x + s, 4) if along_x else lax.rem(z + s, 4) * 4 + x for s in (1, 3, 2)]
        else:
            c = jnp.where(along_x, x, z)
            ids = [jnp.where(along_x, z * 4 + lax.rem(x + s, 4), lax.rem(z + s, 4) * 4 + x) for s in (1, 3, 2)]
        self.c = c
        self.up, self.down, self.over = ({"dp": i} for i in ids)
        self.next, self.far, self.last = [lax.rem(c + s, 4) for s in (1, 2, 3)]


def scatter_sum(m, ring, src, base, own, out, a, s1, s2, w):
    low, high = slice(0, w), slice(w, None)
    k1 = m.to(ring.up, src(ring.far, low), s1[0])
    k2 = m.to(ring.down, src(ring.far, high), s1[1])
    k3 = m.to(ring.up, src(ring.next, high), s2[0].at[:, w:])
    k4 = m.to(ring.down, src(ring.last, low), s2[1].at[:, :w])
    yield
    k1.wait_recv()
    a[0][...] = (base(0).astype(f32) + s1[0][...].astype(f32)).astype(bf16)
    k5 = m.to(ring.up, a[0], s2[0].at[:, :w])
    k2.wait_recv()
    a[1][...] = (base(1).astype(f32) + s1[1][...].astype(f32)).astype(bf16)
    k6 = m.to(ring.down, a[1], s2[1].at[:, w:])
    yield
    for k in (k3, k4, k5, k6):
        k.wait_recv()
    out[...] = (own().astype(f32) + s2[0][...].astype(f32) + s2[1][...].astype(f32)).astype(bf16)
    yield


def gather_ring(m, ring, part):
    k1 = m.to(ring.up, part(ring.c, None), part(ring.c, None))
    k2 = m.to(ring.down, part(ring.c, None), part(ring.c, None))
    yield
    k1.wait_recv()
    x = part(ring.last, 0)
    k3 = m.to(ring.up, x, x)
    k2.wait_recv()
    x = part(ring.next, 1)
    k4 = m.to(ring.down, x, x)
    yield
    k3.wait_recv()
    k4.wait_recv()
    yield


def aligned_start(start):
    return pl.multiple_of(start, 32)


def aligned(start, size, unit=16):
    return pl.ds(pl.multiple_of(start, unit), size)


def main_piece(n, m, p, i):
    k = UNITS[i]
    base = 256 * sum(UNITS[:i])
    r1, r2 = 64 * k, 16 * k
    own, a, s1, s2 = (getattr(n, f"{name}{i}") for name in ("own", "a", "s1", "s2"))
    b, t1, t2, T2 = (getattr(n, f"{name}{i}") for name in ("b", "t1", "t2", "T"))
    rings = [Ring(p, True), Ring(p, False)]
    loads = []
    first, second = [], []
    for h in range(2):
        one, two = rings[h], rings[1 - h]

        def src(j, lanes, h=h):
            lo, hi = lanes.start + h * HALF, (lanes.stop or HALF) + h * HALF
            return n.G.at[aligned(base + j * r1, r1, 64), pl.ds(lo, hi - lo)]

        loads.append([(src(one.c, slice(0, HALF)), own.at[h]), (src(one.next, slice(0, 384)), a.at[h, 0]),
                      (src(one.last, slice(384, HALF)), a.at[h, 1])])
        first.append(scatter_sum(
            m, one, src, lambda d, h=h: a[h, d], lambda h=h: own[h], own.at[h],
            [a.at[h, 0], a.at[h, 1]], [s1.at[h, 0], s1.at[h, 1]], [s2.at[h, 0], s2.at[h, 1]], 384))

        def src2(j, lanes, h=h):
            return own.at[h, aligned(j * r2, r2), pl.ds(lanes.start, (lanes.stop or HALF) - lanes.start)]

        def base2(d, h=h, two=two):
            if d == 0:
                return own[h, aligned(two.next * r2, r2), :384]
            return own[h, aligned(two.last * r2, r2), 384:]

        second.append(scatter_sum(
            m, two, src2, base2, lambda h=h, two=two: own[h, aligned(two.c * r2, r2), :], T2.at[h],
            [b.at[h, 0], b.at[h, 1]], [t1.at[h, 0], t1.at[h, 1]], [t2.at[h, 0], t2.at[h, 1]], 384))
    for g in first:
        next(g)
    loads = [m.own(*pair) for pairs in loads for pair in pairs]
    yield
    for c in loads:
        c.wait()
    for g in first:
        next(g)
    yield
    for g, g2 in zip(first, second):
        next(g)
        next(g2)
    yield
    for g in second:
        next(g)
    yield
    for g in second:
        next(g)
    one = Ring(p, p.gx == 0)
    two = Ring(p, p.gx != 0)

    def place(c1, c2, rows):
        return aligned(base + c1 * r1 + c2 * r2, rows)

    there = (Ring(p, p.gx != 0), Ring(p, p.gx == 0))
    mine = m.own(T2.at[p.gx], n.O.at[p.gx, place(one.c, two.c, r2)])
    swap = m.to(p.pal, T2.at[1 - p.gx], n.O.at[p.gx, place(there[0].c, there[1].c, r2)])
    yield
    mine.wait()
    swap.wait_recv()

    def part_two(j, half):
        r = place(one.c, j, r2)
        return n.O.at[:, r] if half is None else n.O.at[half, r]

    def part_one(j, half):
        r = place(j, jnp.int32(0), r1)
        return n.O.at[:, r] if half is None else n.O.at[half, r]

    g = gather_ring(m, two, part_two)
    next(g)
    yield
    next(g)
    yield
    next(g)
    g = gather_ring(m, one, part_one)
    next(g)
    yield
    next(g)
    yield
    next(g)
    yield


def small_piece(n, m, p, k):
    rings = [Ring(p, True), Ring(p, False)]
    r1, r2, W, top = 128, 32, 384, 512 * k
    lanes = [pl.ds(h * W, W) for h in range(2)]
    E, T, F, U = (getattr(n, f"{name}m{k}") for name in "ETFU")

    def spread(ring, src, dst):
        return [m.to(d, src(j), dst(k)) for k, (d, j) in enumerate(
            ((ring.up, ring.next), (ring.down, ring.last), (ring.over, ring.far)))]

    def total(own, came):
        return (own.astype(f32) + came[0].astype(f32)) + (came[1].astype(f32) + came[2].astype(f32))

    moves = [spread(rings[h], lambda j, h=h: n.M.at[aligned(j * r1 + top, r1), lanes[h]], lambda i, h=h: E.at[h, i])
             for h in range(2)]
    yield
    for h in range(2):
        for c in moves[h]:
            c.wait_recv()
        T[h] = total(n.M[aligned(rings[h].c * r1 + top, r1), h * W:(h + 1) * W], E[h]).astype(bf16)
        moves[h] = spread(rings[1 - h], lambda j, h=h: T.at[h, aligned(j * r2, r2)], lambda i, h=h: F.at[h, i])
    yield
    for h in range(2):
        one, two = rings[h], rings[1 - h]
        for c in moves[h]:
            c.wait_recv()
        U[h] = total(T[h, aligned(two.c * r2, r2)], F[h]).astype(bf16)
        there = n.O4.at[aligned(one.c * r1 + two.c * r2 + top, r2), lanes[h]]
        moves[h] = spread(two, lambda j, h=h: U.at[h], lambda i, there=there: there)
        moves[h].append(m.own(U.at[h], there))
    yield
    for h in range(2):
        for c in moves[h][:3]:
            c.wait_recv()
        moves[h][3].wait()
        there = n.O4.at[aligned(rings[h].c * r1 + top, r1), lanes[h]]
        moves[h] = spread(rings[h], lambda j, there=there: there, lambda i, there=there: there)
    yield
    for h in range(2):
        for c in moves[h]:
            c.wait_recv()
    if k == 0:
        held = n.ntV.at[pl.ds(0, 64), pl.ds(0, HALF)]
        m.own(n.O4.at[pl.ds(384, 64)], held).wait()
        moves = []
        rest = [m.own(held.at[pl.ds(32 * core, 32)], n.O.at[core, pl.ds(LEFT, 32)]) for core in range(2)]
    else:
        block = pl.ds(896, HEAD)
        held = n.ntV.at[pl.ds(64, HEAD), pl.ds(0, HALF)]
        load = m.own(n.O4.at[block], held)
        moves = [m.to(d, n.O4.at[block], n.Oy.at[p.gy]) for d in (p.up, p.down, {"gy": lax.rem(p.gy + 2, 4)})]
        load.wait()
        rest = [m.own(held, n.Oy.at[p.gy])]
    yield
    for c in moves:
        c.wait_recv()
    for c in rest:
        c.wait()
    yield


SCHED = {
    "down": "0", "b0": "", "b1": "", "b2": "0", "b3": "", "own": "", "gate": "1",
    "result": "0", "ml": "", "up": "102",
    "c0": "", "c1": "", "ml1": "", "c2": "", "c3": "", "ml2": "10", "ml3": "0", "ml4": "o",
    "a10": "2", "a11": "", "a12": "10", "relay2": "", "a00": "", "a01": "", "a02": "21",
    "pair": "1o20", "m1": "12m", "m2": "2o", "m3": "v1",
    "tail": "vm20vmo2vm1o2mm", "rest": "om012v"}


def vector_sum(n, m, p):
    coordinates = (p.x, p.z, p.gy)
    devices = (lambda s: {"dp": p.z * 4 + lax.rem(p.x + s, 4)}, lambda s: {"dp": lax.rem(p.z + s, 4) * 4 + p.x},
               lambda s: {"gy": lax.rem(p.gy + s, 4)})
    value = n.gain1[...]
    for d in range(3):
        if d == 2:
            n.vector_dp[...] = value
        slot = n.vectors.at[d, coordinates[d]]
        slot[...] = value
        moves = [m.to(devices[d](s), slot, slot) for s in (1, 3, 2)]
        yield
        for c in moves:
            c.wait_recv()
        value = (n.vectors[d, 0] + n.vectors[d, 1]) + (n.vectors[d, 2] + n.vectors[d, 3])
    n.vector_all[...] = value
    for k in range(4):
        n.kv_bias[:, k * HEAD:(k + 1) * HEAD] = n.vectors[2, k, :, 384:512]
    yield


def back_body(n):
    m = Moves(n.send, n.recv, n.local)
    back_steps(n, m)
    m.finish()


def back_steps(n, m):
    p = Place()
    dp = lax.axis_index("dp")
    p.z, p.x = lax.div(dp, 4), lax.rem(dp, 4)
    gx, gy = p.gx, p.gy
    pal_cols = pl.ds(pl.multiple_of((1 - gx) * HALF, 128), HALF)
    vm = Names({})
    load = {}

    def bring(name, src, dst):
        load[name] = m.own(src, dst)

    bring("og", n.ogf, n.ml)
    bring("hid", n.hid, n.ntV.at[:, pl.ds(0, COLS)])
    bring("gu", n.gu, n.guV)
    bring("Wgu", n.Wgu, n.WguV)
    bring("mid", n.mid, n.midV)
    bring("r2", n.r2, n.r2V)
    for name in ("Q", "K", "V", "cos", "sin", "r1"):
        bring(name, getattr(n, name), getattr(n, name + "V"))
    rings = [Ring(p, True), Ring(p, False)]
    gens = {str(i): main_piece(n, m, p, i) for i in range(3)}
    entered = enter([p.up, p.down, p.pal, rings[0].up, rings[0].down, rings[1].up, rings[1].down])

    def ar(spot):
        for name in SCHED[spot]:
            next(gens[name], None)

    def leave(slot, k, i, rows):
        at = k * REAL + i * BLOCK
        at = pl.multiple_of(at, 32) if isinstance(i, int) else aligned_start(at)
        return pltpu.make_async_copy(
            n.stage.at[slot, pl.ds(0, rows)], n.G.at[pl.ds(at, rows)], n.gsem.at[slot])

    def weight_grad(k, left, at, right, before_tail=lambda: None):
        @pl.loop(0, 4)
        def _(i):
            slot = lax.rem(i, 2)

            @pl.when(i >= 2)
            def _():
                leave(slot, k, i, BLOCK).wait()

            c = pl.ds(pl.multiple_of(i * BLOCK + at, 128), BLOCK)
            n.stage[slot] = dg(left[:, c], right[...], 0, 0).astype(bf16)
            leave(slot, k, i, BLOCK).start()

        leave(0, k, 2, BLOCK).wait()
        leave(1, k, 3, BLOCK).wait()
        before_tail()
        tail = dg(left[:, at + 4 * BLOCK:at + COLS], right[...], 0, 0).astype(bf16)
        n.stage[0, :REAL - 4 * BLOCK] = tail[:REAL - 4 * BLOCK]
        leave(0, k, 4, REAL - 4 * BLOCK).start()
        leave(0, k, 4, REAL - 4 * BLOCK).wait()

    for name in ("og", "hid"):
        load[name].wait()

    def down_ready():
        entered()
        ar("down")

    weight_grad(0, n.ntV, 0, n.ml, down_ready)
    bring("nt", n.nt, n.ntV)

    for name in ("gu", "Wgu"):
        load[name].wait()

    def two_sided(left, weight, take, give, held, names):
        order = (2, 1, 3, 0)
        moves = []
        for k, which in enumerate(order):
            r = rows_of(p.blk[which])
            if k >= 2:
                moves[k - 2].wait_send()
            give[k % 2] = dot(left(r), weight(pal_cols)).astype(bf16)
            moves.append(m.to(p.pal, give.at[k % 2], take.at[k]))
            held[k % 2] = dot(left(r), weight(p.cols))
            if k:
                moves[k - 1].wait_recv()
                yield held[(k - 1) % 2] + take[k - 1].astype(f32)
            ar(names[k])
        moves[3].wait_recv()
        moves[2].wait_send()
        moves[3].wait_send()
        yield held[1] + take[3].astype(f32)

    def scatter(letter):
        return ScatterY(m, p, n.staged, n.held, *(getattr(n, letter + name) for name in ("low", "high", "flow", "fhigh")))

    g = two_sided(lambda r: n.guV[r, :], lambda c: n.WguV[:, c], n.take, n.give, n.two, ("b0", "b1", "b2", "b3"))
    rs = scatter("A")
    rs.far(next(g))
    rs.next_up(next(g))
    rs.next_down(next(g))
    n.part[...] = next(g)
    ar("own")
    bring("Wd", n.Wd, n.WguV.at[pl.ds(0, COLS)])
    bring("P", n.P, n.WguV.at[pl.ds(COLS, HEADS * BLOCK)])
    bring("Wo", n.Wo, n.WguV.at[pl.ds(1920, 384)])
    load["nt"].wait()
    rs.relay()
    weight_grad(1, n.guV, 0, n.ntV)
    ar("gate")
    n.part[...] = rs.result(n.part[...])
    ar("result")
    load["mid"].wait()
    load["r2"].wait()
    r2 = n.r2V[:, :1]
    y2 = n.midV[...] * r2
    w2 = n.part[...] * n.g2[...].reshape(1, HALF)
    n.gain2[...] = jnp.broadcast_to(jnp.sum(n.part[...] * y2, axis=0, keepdims=True), (8, HALF))
    n.sums[0] = jnp.broadcast_to(jnp.sum(w2 * y2, axis=1, keepdims=True), (BLOCK, HEAD))
    sum_move = m.to(p.pal, n.sums.at[0], n.sums.at[1])
    sum_move.wait_recv()
    total = (n.sums[0] + n.sums[1])[:, :1] * (1.0 / D)
    n.mg[...] = n.og[...].astype(f32) + r2 * (w2 - y2 * total)
    n.mlo[...] = n.mg[...].astype(bf16)
    gather = GatherY(m, p, n.mlo, n.ml)
    gather.start()
    n.ml[rows_of(gy), p.cols] = n.mlo[...]
    ar("ml")
    weight_grad(2, n.guV, COLS, n.ntV)
    ar("up")
    bring("hid", n.hid, n.guV.at[:, pl.ds(0, COLS)])
    bring("nx", n.nx, n.guV.at[:, pl.ds(COLS, HALF)])
    bring("att", n.att, n.guV.at[:, pl.ds(COLS + HALF, 384)])
    left_row = aligned(384 + gx * 32, 32, 32)
    bring("left", n.G.at[pl.ds(LEFT, 32), p.cols], n.M.at[left_row])
    left_move = m.to(p.pal, n.G.at[pl.ds(LEFT, 32), pal_cols], n.M.at[left_row])

    load["hid"].wait()
    load["Wd"].wait()
    g = two_sided(lambda r: n.guV[r, :COLS], lambda c: n.WguV[:COLS, c], n.take, n.give, n.two, ("c0", "c1", "c2", "c3"))
    n.later[0] = next(g).astype(bf16)
    gather.relay()
    ar("ml1")
    for k in (1, 2):
        n.later[k] = next(g).astype(bf16)
    n.part[...] = next(g) + n.midV[...]
    ar("ml2")
    gather.relay_pal()
    m.settle([rs.a, rs.b, rs.c, rs.d, rs.e, rs.f])
    rs = scatter("B")
    rs.far(n.later[0].astype(f32))
    rs.next_up(n.later[1].astype(f32))
    rs.next_down(n.later[2].astype(f32))
    gather.own_ready()
    gather.low_ready()
    gather.high_ready()
    ar("ml3")

    for name in ("att", "Q", "K", "V", "cos", "sin", "nx", "Wo", "r1", "P", "left"):
        load[name].wait()
    gather.far_ready()
    n.M[0:384, :] = dg(n.guV[:, COLS + HALF:], n.ml[:, p.cols], 0, 0).astype(bf16)
    n.M[448:512, :] = jnp.zeros((64, HALF), bf16)
    left_move.wait_recv()
    gens["o"] = small_piece(n, m, p, 0)
    ar("ml4")
    own_blocks = [gx, 3 - gx]
    q_moves = []
    for i in (1, 0):
        b = rows_of(own_blocks[i])
        keys, at = 512 * (i + 1), 512 * i
        n.ag[...] = dg(n.ml[b, :], n.WguV[1920:, :], 1, 1).astype(bf16)
        for h in range(HEADS):
            c = slice(h * HEAD, (h + 1) * HEAD)
            probs = n.WguV[COLS + h * BLOCK:COLS + (h + 1) * BLOCK, at:at + keys]
            probs_f = probs.astype(f32)
            prob_grads = dg(n.ag[:, c], n.VV[:keys, :], 1, 1)
            centre = jnp.sum(probs_f * prob_grads, axis=1, keepdims=True)
            score_grads = (probs_f * (prob_grads - centre)).astype(bf16)
            dq = dot(score_grads, n.KV[:keys, :]) * SCALE
            dk = dg(score_grads, n.QV[i * BLOCK:(i + 1) * BLOCK, c], 0, 0) * SCALE
            dv = dg(probs, n.ag[:, c], 0, 0)
            if i == 1 and h == 0:
                n.dkv[:, :HEAD] = dk
                n.dkv[:, HEAD:] = dv
            else:
                n.dkv[:keys, :HEAD] += dk
                n.dkv[:keys, HEAD:] += dv
            n.ql[b, c] = turned(dq, n.cosV[b, :], -n.sinV[b, :]).astype(bf16)
            ar(f"a{i}{h}")
        q_moves.append(m.to(p.pal, n.ql.at[b], n.ql.at[b]))
        if i == 1:
            rs.relay()
            ar("relay2")
    n.S[0] = n.dkv[...].astype(bf16)
    s_move = m.to(p.pal, n.S.at[0], n.S.at[1])
    n.block_out[...] = rs.result(n.part[...])
    s_move.wait_recv()
    both = n.S[0].astype(f32) + n.S[1].astype(f32)
    n.dkv[...] = both
    n.S2[...] = both.astype(bf16)
    odd = lax.rem(gy, 2)
    pair = {"gy": gy + 1 - 2 * odd}
    pair_move = m.to(pair, n.S2.at[:, pl.ds(pl.multiple_of((1 - odd) * HEAD, HEAD), HEAD)], n.pin)
    ar("pair")
    for copy in q_moves:
        copy.wait_recv()
    n.M[512:896, :] = dg(n.ql[...], n.guV[:, COLS:COLS + HALF], 0, 0).astype(bf16)
    pair_move.wait_recv()
    kv = n.dkv[:, pl.ds(pl.multiple_of(odd * HEAD, HEAD), HEAD)] + n.pin[...].astype(f32)
    is_key = (1 - odd).astype(f32)
    cosine = n.cosV[...] * is_key + (1.0 - is_key)
    sine = n.sinV[...] * is_key
    n.plow[...] = turned(kv, cosine, -sine).astype(bf16)
    n.M[896:, :] = dg(n.plow[...], n.guV[:, COLS:COLS + HALF], 0, 0).astype(bf16)
    bias = jnp.concatenate([
        jnp.sum(n.ql[...].astype(f32), axis=0, keepdims=True),
        jnp.sum(n.plow[...].astype(f32), axis=0, keepdims=True),
        jnp.zeros((1, 256), f32)], axis=1)

    def norm_one_part(block):
        r = rows_of(block)
        kvw = n.kvw[:, pl.ds(pl.multiple_of(gy * HEAD, HEAD), HEAD)]
        return dg(n.ql[r, :], n.qw[...], 1, 1) + dg(n.plow[r, :], kvw, 1, 1)

    m.settle([rs.a, rs.b, rs.c, rs.d, rs.e, rs.f])
    rs = scatter("A")
    rs.far(norm_one_part(p.blk[2]))
    rs.next_up(norm_one_part(p.blk[1]))
    rs.next_down(norm_one_part(p.blk[3]))
    n.part[...] = norm_one_part(p.blk[0])
    gens["m"] = small_piece(n, m, p, 1)
    ar("m1")
    rs.relay()
    ar("m2")
    n.part[...] = rs.result(n.part[...])
    r1 = n.r1V[:, :1]
    y1 = n.x[...].astype(f32) * r1
    w1 = n.part[...] * n.g1[...].reshape(1, HALF)
    gain1 = jnp.sum(n.part[...] * y1, axis=0, keepdims=True)
    m.settle([sum_move])
    n.sums[0] = jnp.broadcast_to(jnp.sum(w1 * y1, axis=1, keepdims=True), (BLOCK, HEAD))
    sum_move = m.to(p.pal, n.sums.at[0], n.sums.at[2])
    row = lax.broadcasted_iota(jnp.int32, (8, HALF), 0)
    n.gain1[...] = jnp.where(row == 0, gain1, jnp.where(row == 1, n.gain2[0:1, :], jnp.where(row == 2, bias, 0.0)))
    gens["v"] = vector_sum(n, m, p)
    ar("m3")
    sum_move.wait_recv()
    total = (n.sums[0] + n.sums[2])[:, :1] * (1.0 / D)
    n.input_grad[...] = n.mg[...] + r1 * (w1 - y1 * total)
    ar("tail")
    for _ in range(14):
        ar("rest")


def back(f, layer_input, norm1_gain, q_weight, kv_weight, norm2_gain, out_grad):
    vm, hbm = pltpu.VMEM, pl.ANY
    inputs = dict(
        x=(layer_input, vm), og=(out_grad, vm), g1=(norm1_gain, vm), g2=(norm2_gain, vm),
        qw=(q_weight, vm), kvw=(kv_weight, vm),
        ogf=(f.ogO, hbm), nt=(f.ntO, hbm), gu=(f.guO, hbm), Wgu=(f.WguO, hbm), hid=(f.hidO, hbm), Wd=(f.WdO, hbm), mid=(f.midO, hbm),
        r1=(f.r1, hbm), r2=(f.r2, hbm), att=(f.attO, hbm), P=(f.PO, hbm), Q=(f.QO, hbm), K=(f.KO, hbm),
        V=(f.VO, hbm), cos=(f.cosO, hbm), sin=(f.sinO, hbm), nx=(f.nxO, hbm), Wo=(f.WoO, hbm))
    outputs = dict(
        block_out=((BLOCK, HALF), f32, vm), input_grad=((BLOCK, HALF), f32, vm),
        O=((2, 3 * REAL, HALF), bf16, hbm), O4=((TOKENS, HALF), bf16, hbm), Oy=((4, HEAD, HALF), bf16, hbm),
        vector_all=((8, HALF), f32, vm), vector_dp=((8, HALF), f32, vm), kv_bias=((8, 512), f32, vm), G=((3 * REAL, D), bf16, hbm))
    v = pltpu.VMEM
    scratch = dict(
        guV=v((TOKENS, 2 * COLS), bf16), WguV=v((2 * COLS, D), bf16), midV=v((BLOCK, HALF), f32),
        r1V=v((BLOCK, HEAD), f32), r2V=v((BLOCK, HEAD), f32), QV=v((512, 384), bf16),
        KV=v((TOKENS, HEAD), bf16), VV=v((TOKENS, HEAD), bf16), cosV=v((TOKENS, HEAD), f32),
        sinV=v((TOKENS, HEAD), f32), ntV=v((TOKENS, D), bf16),
        take=v((4, BLOCK, HALF), bf16), give=v((2, BLOCK, HALF), bf16), two=v((2, BLOCK, HALF), f32),
        staged=v((3, BLOCK, HALF), bf16), held=v((2, 128, HALF), f32),
        part=v((BLOCK, HALF), f32), later=v((3, BLOCK, HALF), bf16), stage=v((2, BLOCK, D), bf16),
        gain1=v((8, HALF), f32), vectors=v((3, 4, 8, HALF), f32), gain2=v((8, HALF), f32), sums=v((3, BLOCK, HEAD), f32),
        mg=v((BLOCK, HALF), f32), mlo=v((BLOCK, HALF), bf16), ml=v((TOKENS, D), bf16),
        ag=v((BLOCK, 384), bf16), dkv=v((TOKENS, 256), f32), ql=v((TOKENS, 384), bf16), S=v((2, TOKENS, 256), bf16),
        S2=v((TOKENS, 256), bf16), pin=v((TOKENS, HEAD), bf16), plow=v((TOKENS, HEAD), bf16), M=v((TOKENS, HALF), bf16),
    )
    for k in range(2):
        scratch.update({f"Em{k}": v((2, 3, 128, 384), bf16), f"Tm{k}": v((2, 128, 384), bf16),
                        f"Fm{k}": v((2, 3, 32, 384), bf16), f"Um{k}": v((2, 32, 384), bf16)})
    for letter in "AB":
        scratch.update({letter + "low": v((128, HALF), bf16), letter + "high": v((128, HALF), bf16),
                        letter + "flow": v((BLOCK, HALF), bf16), letter + "fhigh": v((BLOCK, HALF), bf16)})
    for i, k in enumerate(UNITS):
        r1, r2 = 64 * k, 16 * k
        scratch.update({
            f"own{i}": v((2, r1, HALF), bf16), f"a{i}": v((2, 2, r1, 384), bf16), f"s1{i}": v((2, 2, r1, 384), bf16),
            f"s2{i}": v((2, 2, r1, HALF), bf16), f"b{i}": v((2, 2, r2, 384), bf16), f"t1{i}": v((2, 2, r2, 384), bf16),
            f"t2{i}": v((2, 2, r2, HALF), bf16), f"T{i}": v((2, r2, HALF), bf16)})
    scratch.update(send=pltpu.SemaphoreType.DMA((240,)), recv=pltpu.SemaphoreType.DMA((240,)),
                   local=pltpu.SemaphoreType.DMA((64,)), gsem=pltpu.SemaphoreType.DMA((2,)))
    return kernel_call("back", back_body, inputs, outputs, scratch, 2, flops=16 * 10**9, moved=60 * 2**20)


PART = 560
SLOTS = 6


def finish(b):
    jobs = [(core, t, j) for j in range(REAL // PART) for core in range(2) for t in range(3)]

    def kernel(big, small, shared, gain, dp_sums, kv_sums, block, grad, down, gate, up, o, q, kv, block_out, grad_out,
               gain1, gain2, q_bias, kv_bias, came, leaving, small_in, shared_in, o_to, q_to, kv_to, through,
               in_sem, out_sem, sem):
        outs = (down, gate, up)

        def read(i):
            core, t, j = jobs[i]
            return pltpu.make_async_copy(
                big.at[core, pl.ds(t * REAL + j * PART, PART)], came.at[i % SLOTS], in_sem.at[i % SLOTS])

        def write(i):
            core, t, j = jobs[i]
            return pltpu.make_async_copy(
                leaving.at[i % SLOTS], outs[t].at[pl.ds(core * REAL + j * PART, PART)], out_sem.at[i % SLOTS])

        for i in range(3):
            read(i).start()
        loads = [pltpu.make_async_copy(small, small_in, sem.at[0]), pltpu.make_async_copy(shared, shared_in, sem.at[1])]
        passes = [pltpu.make_async_copy(block, through.at[0], sem.at[2]),
                  pltpu.make_async_copy(grad, through.at[1], sem.at[3])]
        for c in loads:
            c.start()
        for i in range(3, SLOTS):
            read(i).start()
        for c in passes:
            c.start()
        rest = []
        for i in range(len(jobs)):
            read(i).wait()
            if i >= SLOTS:
                write(i - SLOTS).wait()
            leaving[i % SLOTS] = came[i % SLOTS].astype(f32)
            write(i).start()
            if i + SLOTS < len(jobs):
                read(i + SLOTS).start()
            if i == 3:
                for c in loads + passes:
                    c.wait()
                for k, c in enumerate((block_out, grad_out)):
                    rest.append(pltpu.make_async_copy(through.at[k], c, sem.at[7 + k]))
                    rest[-1].start()
                o_to[...] = small_in[:384, :].astype(f32)
                rest.append(pltpu.make_async_copy(o_to, o, sem.at[4]))
                rest[-1].start()
            if 4 <= i < 7:
                k = i - 4
                q_to[:, k * HEAD:(k + 1) * HEAD] = small_in[512 + k * HEAD:512 + (k + 1) * HEAD, :].T.astype(f32)
                if k == 2:
                    rest.append(pltpu.make_async_copy(q_to, q, sem.at[5]))
                    rest[-1].start()
            if 7 <= i < 11:
                k = i - 7
                kv_to[:, k * HEAD:(k + 1) * HEAD] = shared_in[k].T.astype(f32)
                if k == 3:
                    rest.append(pltpu.make_async_copy(kv_to, kv, sem.at[6]))
                    rest[-1].start()
            if i == 11:
                gain1[...] = gain[0]
                gain2[...] = gain[1]
                q_bias[...] = dp_sums[2, :384]
                kv_bias[...] = kv_sums[2]
        for i in range(len(jobs) - SLOTS, len(jobs)):
            write(i).wait()
        for c in rest:
            c.wait()

    def array(*shape):
        return jax.ShapeDtypeStruct(shape, f32)

    v = pltpu.VMEM
    hbm, vm = pl.BlockSpec(memory_space=pl.ANY), pl.BlockSpec(memory_space=v)
    weight = array(2 * REAL, HALF)
    down, gate, up, o, q, kv, block_out, grad, gain1, gain2, q_bias, kv_bias = pl.pallas_call(
        kernel,
        in_specs=[hbm] * 3 + [vm] * 3 + [hbm] * 2,
        out_specs=[hbm] * 8 + [vm] * 4,
        out_shape=[weight, weight, weight, array(384, HALF), array(HALF, 384), array(HALF, 512),
                   array(BLOCK, HALF), array(BLOCK, HALF), array(HALF), array(HALF), array(384), array(512)],
        scratch_shapes=[v((SLOTS, PART, HALF), bf16), v((SLOTS, PART, HALF), f32), v((TOKENS, HALF), bf16),
                        v((4, HEAD, HALF), bf16), v((384, HALF), f32), v((HALF, 384), f32), v((HALF, 512), f32), v((2, BLOCK, HALF), f32),
                        pltpu.SemaphoreType.DMA((SLOTS,)), pltpu.SemaphoreType.DMA((SLOTS,)),
                        pltpu.SemaphoreType.DMA((9,))],
        compiler_params=pltpu.CompilerParams(vmem_limit_bytes=60 * 2**20),
        name="finish",
    )(b.O, b.O4, b.Oy, b.vector_all, b.vector_dp, b.kv_bias, b.block_out, b.input_grad)
    return block_out, grad, gain1, q, q_bias, kv, kv_bias, o, gain2, gate.T, up.T, down


def per_device(layer_input, norm1_gain, q_weight, q_bias, kv_weight, kv_bias, o_weight, norm2_gain,
               gate_weight, up_weight, down_weight, seq_lengths, out_grad):
    f = front(layer_input, norm1_gain, q_weight, q_bias, kv_weight, kv_bias, o_weight, norm2_gain,
              gate_weight, up_weight, down_weight, seq_lengths, out_grad)
    b = back(f, layer_input, norm1_gain, q_weight, kv_weight, norm2_gain, out_grad)
    return finish(b)


def solution(mesh):
    rows, width = P(("dp", "gy"), "gx"), P("gx", "gy")
    return jax.shard_map(
        per_device,
        mesh=mesh,
        in_specs=(rows, P("gx"), width, P("gy"), P("gx", None), P(), P("gy", "gx"), P("gx"), width, width,
                  P("gy", "gx"), P("dp", None), rows),
        out_specs=(rows, rows, P("gx"), width, P("gy"), P("gx", None), P(), P("gy", "gx"), P("gx"), width, width,
                   P("gy", "gx")),
        check_vma=False,
    )
```

```python
import jax
import jax.numpy as jnp
import numpy as np
from jax import lax
from jax.experimental import pallas as pl
from jax.experimental.pallas import tpu as pltpu
from jax.sharding import PartitionSpec as P

f32 = jnp.float32
bf16 = jnp.bfloat16
MESH = pl.DeviceIdType.MESH
EPSILON = 1e-06
THETA = 1000000.0
NEGATIVE = -1e30
D = 1536
HALF = 768
BLOCK = 256
TOKENS = 1024
COLS = 1152
REAL = 1120
HEADS = 3
HEAD = 128


def dg(left, right, left_dim, right_dim):
    return lax.dot_general(
        left, right, (((left_dim,), (right_dim,)), ((), ())), preferred_element_type=f32
    )


def dot(left, right):
    return jnp.dot(left, right, preferred_element_type=f32)


class Names:
    def __init__(self, pairs):
        self.__dict__.update(pairs)


def rows_of(block, size=BLOCK):
    return pl.ds(pl.multiple_of(block * size, size), size)


class Copy:
    def __init__(self, copy, remote):
        self.copy, self.remote = copy, remote
        self.left = self.came = False
        copy.start()

    def wait_send(self):
        if not self.left:
            self.left = True
            self.copy.wait_send()

    def wait_recv(self):
        if not self.came:
            self.came = True
            self.copy.wait_recv()

    def wait(self):
        if not self.left:
            self.left = True
            self.copy.wait()


class Moves:
    def __init__(self, send, recv, local):
        self.send, self.recv, self.local = send, recv, local
        self.remotes = []
        self.locals = []

    def to(self, device, src, dst):
        i = len(self.remotes)
        copy = Copy(pltpu.make_async_remote_copy(
            src_ref=src, dst_ref=dst, send_sem=self.send.at[i], recv_sem=self.recv.at[i],
            device_id=device, device_id_type=MESH), True)
        self.remotes.append(copy)
        return copy

    def own(self, src, dst):
        copy = Copy(pltpu.make_async_copy(src, dst, self.local.at[len(self.locals)]), False)
        self.locals.append(copy)
        return copy

    out = own

    def settle(self, copies):
        for copy in copies:
            copy.wait_send()

    def finish(self):
        for copy in self.remotes:
            copy.wait_send()
            copy.wait_recv()
        for copy in self.locals:
            copy.wait()


class Place:
    def __init__(self):
        self.gx = lax.axis_index("gx")
        self.gy = lax.axis_index("gy")
        self.up = {"gy": lax.rem(self.gy + 1, 4)}
        self.down = {"gy": lax.rem(self.gy + 3, 4)}
        self.pal = {"gx": 1 - self.gx}
        self.blk = [lax.rem(self.gy + i, 4) for i in range(4)]
        self.cols = pl.ds(pl.multiple_of(self.gx * HALF, 128), HALF)


class GatherY:
    def __init__(self, moves, place, src, buf):
        self.m, self.p, self.src, self.buf = moves, place, src, buf

    def part(self, block, first, count):
        r = pl.ds(pl.multiple_of(block * BLOCK + first, 128), count)
        return self.buf.at[r, self.p.cols]

    def start(self):
        p = self.p
        there = self.part(p.blk[0], 0, BLOCK)
        self.a = self.m.to(p.up, self.src, there)
        self.b = self.m.to(p.down, self.src, there)
        self.c = self.m.to(p.pal, self.src, there)

    def own_ready(self):
        self.c.wait_recv()

    def relay(self):
        p, m = self.p, self.m
        low, high = p.blk[3], p.blk[1]
        self.a.wait_recv()
        x = self.part(low, 0, 128)
        self.d = m.to(p.up, x, x)
        self.b.wait_recv()
        x = self.part(high, 128, 128)
        self.e = m.to(p.down, x, x)
        x = self.part(low, 0, BLOCK)
        self.f = m.to(p.pal, x, x)
        x = self.part(high, 0, BLOCK)
        self.g = m.to(p.pal, x, x)

    def low_ready(self):
        self.f.wait_recv()

    def high_ready(self):
        self.g.wait_recv()

    def relay_pal(self):
        p, m = self.p, self.m
        far = p.blk[2]
        self.d.wait_recv()
        x = self.part(far, 0, 128)
        self.h = m.to(p.pal, x, x)
        self.e.wait_recv()
        x = self.part(far, 128, 128)
        self.i = m.to(p.pal, x, x)

    def far_ready(self):
        self.h.wait_recv()
        self.i.wait_recv()


class ScatterY:
    def __init__(self, moves, place, staged, held, low_half, high_half, from_low, from_high):
        self.m, self.p = moves, place
        self.staged, self.held = staged, held
        self.low_half, self.high_half = low_half, high_half
        self.from_low, self.from_high = from_low, from_high

    def far(self, value):
        p, m = self.p, self.m
        self.staged[0] = value.astype(bf16)
        self.a = m.to(p.up, self.staged.at[0, pl.ds(0, 128)], self.low_half)
        self.b = m.to(p.down, self.staged.at[0, pl.ds(128, 128)], self.high_half)

    def next_up(self, value):
        p, m = self.p, self.m
        self.staged[1, 128:] = value[128:].astype(bf16)
        self.c = m.to(p.up, self.staged.at[1, pl.ds(128, 128)], self.from_low.at[pl.ds(128, 128)])
        self.held[0] = value[:128]

    def next_down(self, value):
        p, m = self.p, self.m
        self.staged[2, :128] = value[:128].astype(bf16)
        self.d = m.to(p.down, self.staged.at[2, pl.ds(0, 128)], self.from_high.at[pl.ds(0, 128)])
        self.held[1] = value[128:]

    def relay(self):
        p, m = self.p, self.m
        self.a.wait_recv()
        self.staged[1, :128] = (self.held[0] + self.low_half[...].astype(f32)).astype(bf16)
        self.e = m.to(p.up, self.staged.at[1, pl.ds(0, 128)], self.from_low.at[pl.ds(0, 128)])
        self.b.wait_recv()
        self.staged[2, 128:] = (self.held[1] + self.high_half[...].astype(f32)).astype(bf16)
        self.f = m.to(p.down, self.staged.at[2, pl.ds(128, 128)], self.from_high.at[pl.ds(128, 128)])

    def result(self, own):
        self.c.wait_recv()
        self.d.wait_recv()
        self.e.wait_recv()
        self.f.wait_recv()
        return own + self.from_low[...].astype(f32) + self.from_high[...].astype(f32)


def enter(devices):
    barrier = pltpu.get_barrier_semaphore()
    for device in devices:
        pl.semaphore_signal(barrier, inc=1, device_id=device, device_id_type=MESH)
    return lambda: pl.semaphore_wait(barrier, len(devices))


def turned(value, cosine, signed_sine):
    return value * cosine + pltpu.roll(value, 64, 1) * signed_sine


def opening_of(ends, places):
    opening = jnp.zeros_like(places)
    for e in ends:
        opening = jnp.where(places >= e, jnp.maximum(opening, e), opening)
    return opening


def front_body(n):
    m = Moves(n.send, n.recv, n.local)
    front_steps(n, m)
    m.finish()


def front_steps(n, m):
    p = Place()
    gx, gy = p.gx, p.gy

    mine = pl.ds(pl.multiple_of(gx * REAL, 16), REAL)
    theirs = pl.ds(pl.multiple_of((1 - gx) * REAL, 16), REAL)
    weights = ((n.dw, n.Wd, 0), (n.gw, n.Wgu, 0), (n.uw, n.Wgu, COLS))
    loads = [m.own(w.at[mine], W.at[pl.ds(at, REAL), p.cols]) for w, W, at in weights]
    n.g1f[:, p.cols] = jnp.broadcast_to(n.g1[...].reshape(1, HALF), (8, HALF))
    enter([p.up, p.down, p.pal])()

    gather_x = GatherY(m, p, n.x, n.xb)
    gather_x.start()
    gain_move = m.to(p.pal, n.g1f.at[:, p.cols], n.g1f.at[:, p.cols])
    pair = p.gy // 2
    pair_cols = pl.ds(pl.multiple_of(pair * 256, 128), 256)
    own_rows = pl.ds(pl.multiple_of(gx * HALF, 128), HALF)
    kv_move = m.to(p.pal, n.kvw.at[:, pair_cols], n.Wkv.at[own_rows])
    q_move = m.to(p.pal, n.qw, n.Wq.at[own_rows])
    o_move = m.to(p.pal, n.ow, n.Wo.at[:, p.cols])

    n.xb[rows_of(gy), p.cols] = n.x[...]
    n.Wkv[own_rows, :] = n.kvw[:, pair_cols]
    n.Wq[own_rows, :] = n.qw[...]
    n.Wo[:, p.cols] = n.ow[...]

    ends = []
    running = jnp.int32(0)
    for k in range(4):
        running = running + n.seq[0, k]
        ends.append(running)
    lane = lax.broadcasted_iota(jnp.int32, (BLOCK, HEAD), 1)

    def table(i):
        places = lax.broadcasted_iota(jnp.int32, (BLOCK, HEAD), 0) + i * BLOCK
        position = places - opening_of(ends, places)
        angles = position.astype(f32) * n.freqs[...]
        r = rows_of(i)
        n.cosT[r, :] = jnp.cos(angles)
        n.sinT[r, :] = jnp.where(lane < 64, -jnp.sin(angles), jnp.sin(angles))

    pl.loop(0, 4)(table)
    m.out(n.cosT, n.cosO)
    m.out(n.sinT, n.sinO)

    gather_x.relay()

    def norm_block(block):
        r = rows_of(block)
        xf = n.xb[r, :].astype(f32)
        inverse = lax.rsqrt(jnp.sum(xf * xf, axis=1, keepdims=True) * (1.0 / D) + EPSILON)
        normed = (xf * inverse * n.g1f[0:1, :]).astype(bf16)
        n.nx[r, :] = normed
        kv = dot(normed, n.Wkv[...]) + n.kvb[pair_cols].reshape(1, 256)
        n.K[r, :] = turned(kv[:, :HEAD], n.cosT[r, :], n.sinT[r, :]).astype(bf16)
        n.V[r, :] = kv[:, HEAD:].astype(bf16)
        return inverse

    gain_move.wait_recv()
    kv_move.wait_recv()
    gather_x.own_ready()
    inverse = norm_block(p.blk[0])
    n.r1T[...] = jnp.broadcast_to(inverse, (BLOCK, HEAD))
    m.out(n.r1T, n.r1)
    gather_x.low_ready()
    norm_block(p.blk[3])
    gather_x.high_ready()
    norm_block(p.blk[1])
    gather_x.relay_pal()
    gather_og = GatherY(m, p, n.og, n.ogb)
    gather_og.start()
    weight_moves = [m.to(p.pal, w.at[theirs], W.at[pl.ds(at, REAL), p.cols]) for w, W, at in weights]
    n.ogb[rows_of(gy), p.cols] = n.og[...]
    for _, W, at in weights:
        W[at + REAL:at + COLS, :] = jnp.zeros((COLS - REAL, D), bf16)
    gather_x.far_ready()
    norm_block(p.blk[2])
    m.out(n.nx.at[:, p.cols], n.nxO)
    m.out(n.K, n.KO)
    m.out(n.V, n.VO)

    q_move.wait_recv()
    own_blocks = [gx, 3 - gx]
    for i, b in enumerate(own_blocks):
        r = rows_of(b)
        q = dot(n.nx[r, :], n.Wq[...]) + n.qb[...].reshape(1, 384)
        for h in range(HEADS):
            c = slice(h * HEAD, (h + 1) * HEAD)
            n.Q[i * BLOCK:(i + 1) * BLOCK, c] = turned(q[:, c], n.cosT[r, :], n.sinT[r, :]).astype(bf16)
    m.out(n.Q, n.QO)

    def attention(i, h):
        b = own_blocks[i]
        keys = 512 * (i + 1)
        at = 512 * i
        c = slice(h * HEAD, (h + 1) * HEAD)
        s = dg(n.Q[i * BLOCK:(i + 1) * BLOCK, c], n.K[:keys, :], 1, 1) * HEAD ** (-0.5)
        query = lax.broadcasted_iota(jnp.int32, (BLOCK, 1), 0) + b * BLOCK
        opening = opening_of(ends, query)
        key = lax.broadcasted_iota(jnp.int32, (BLOCK, keys), 1)
        s = jnp.where((key >= opening) & (key <= query), s, NEGATIVE)
        e = jnp.exp(s - jnp.max(s, axis=1, keepdims=True))
        probs = (e / jnp.sum(e, axis=1, keepdims=True)).astype(bf16)
        n.Pr[h * BLOCK:(h + 1) * BLOCK, at:at + keys] = probs
        out = dot(probs, n.V[:keys, :])
        n.att[rows_of(b), c] = out.astype(bf16)

    att_moves = []
    for i in (1, 0):
        for h in range(HEADS):
            attention(i, h)
        b = rows_of(own_blocks[i])
        att_moves.append(m.to(p.pal, n.att.at[b], n.att.at[b]))
        if i == 1:
            gather_og.relay()
    m.out(n.Pr, n.PO)
    gather_og.own_ready()
    loads[0].wait()
    weight_moves[0].wait_recv()

    def hidden_grad(block):
        r = rows_of(block)
        n.HG[r, :] = dg(n.ogb[r, :], n.Wd[...], 1, 1)

    for copy in att_moves:
        copy.wait_recv()

    m.settle([gather_x.a, gather_x.b, gather_x.c, gather_x.d, gather_x.e, gather_x.f, gather_x.g, gather_x.h, gather_x.i])

    def out_part(block):
        return dot(n.att[rows_of(block), :], n.ow[...])

    rs = ScatterY(m, p, n.staged, n.held, n.low_half, n.high_half, n.from_low, n.from_high)
    rs.far(out_part(p.blk[2]))
    rs.next_up(out_part(p.blk[1]))
    rs.next_down(out_part(p.blk[3]))
    n.mid[...] = out_part(p.blk[0]) + n.x[...].astype(f32)
    m.out(n.att, n.attO)
    gather_og.relay_pal()
    rs.relay()
    hidden_grad(p.blk[0])
    gather_og.low_ready()
    hidden_grad(p.blk[3])
    gather_og.high_ready()
    hidden_grad(p.blk[1])
    n.mid[...] = rs.result(n.mid[...])
    m.out(n.mid, n.midO)
    mid = n.mid[...]
    n.sums[0] = jnp.broadcast_to(jnp.sum(mid * mid, axis=1, keepdims=True), (BLOCK, HEAD))
    sum_move = m.to(p.pal, n.sums.at[0], n.sums.at[1])
    sum_move.wait_recv()
    r2 = lax.rsqrt((n.sums[0] + n.sums[1]) * (1.0 / D) + EPSILON)
    n.r2T[...] = r2
    m.out(n.r2T, n.r2)
    n.nto[...] = (n.mid[...] * r2[:, :1] * n.g2[...].reshape(1, HALF)).astype(bf16)
    gather_n = GatherY(m, p, n.nto, n.xb)
    gather_n.start()
    n.xb[rows_of(gy), p.cols] = n.nto[...]
    gather_og.far_ready()
    m.out(n.ogb, n.ogO)
    hidden_grad(p.blk[2])
    for k in (1, 2):
        loads[k].wait()
        weight_moves[k].wait_recv()
    m.out(n.Wgu, n.WguO)
    m.out(n.Wd, n.WdO)

    def feed_forward(block):
        r = rows_of(block)
        a = n.xb[r, :]
        both = dg(a, n.Wgu[...], 1, 1)
        gate = both[:, :COLS]
        upward = both[:, COLS:]
        back = n.HG[r, :]
        sg = jax.nn.sigmoid(gate)
        gs = gate * sg
        n.hid[r, :] = (gs * upward).astype(bf16)
        n.gu[r, :COLS] = (back * upward * sg * (1.0 + gate * (1.0 - sg))).astype(bf16)
        n.gu[r, COLS:] = (back * gs).astype(bf16)
        m.out(n.hid.at[r], n.hidO.at[r])
        m.out(n.gu.at[r], n.guO.at[r])

    gather_n.own_ready()
    feed_forward(p.blk[0])
    gather_n.relay()
    gather_n.low_ready()
    feed_forward(p.blk[3])
    gather_n.high_ready()
    feed_forward(p.blk[1])
    gather_n.relay_pal()
    gather_n.far_ready()
    m.out(n.xb, n.ntO)
    feed_forward(p.blk[2])

    o_move.wait_recv()
    m.out(n.Wo, n.WoO)


def kernel_call(name, body, inputs, outputs, scratch, collective_id, flops=0, moved=0):
    order = list(inputs) + list(outputs) + list(scratch)

    def kernel(*refs):
        body(Names(dict(zip(order, refs))))

    results = pl.pallas_call(
        kernel,
        out_shape=tuple(jax.ShapeDtypeStruct(s, d) for s, d, _ in outputs.values()),
        in_specs=[pl.BlockSpec(memory_space=s) for _, s in inputs.values()],
        out_specs=tuple(pl.BlockSpec(memory_space=s) for _, _, s in outputs.values()),
        scratch_shapes=list(scratch.values()),
        compiler_params=pltpu.CompilerParams(
            collective_id=collective_id, has_side_effects=True, vmem_limit_bytes=62 * 2**20),
        cost_estimate=pl.CostEstimate(flops=flops, bytes_accessed=moved, transcendentals=0),
        name=name,
    )(*[a for a, _ in inputs.values()])
    return Names(dict(zip(outputs, results)))


def frequencies():
    freqs = np.float32(THETA) ** (-np.arange(0, HEAD, 2, dtype=np.float32) / np.float32(HEAD))
    return np.concatenate([freqs, freqs])[None, :]


def front(layer_input, norm1_gain, q_weight, q_bias, kv_weight, kv_bias, o_weight, norm2_gain,
          gate_weight, up_weight, down_weight, seq_lengths, out_grad):
    vm, hbm, sm = pltpu.VMEM, pl.ANY, pltpu.SMEM
    inputs = dict(
        x=(layer_input, vm), og=(out_grad, vm), g1=(norm1_gain, vm), g2=(norm2_gain, vm),
        qw=(q_weight, vm), qb=(q_bias, vm), kvw=(kv_weight, vm), kvb=(kv_bias, vm),
        ow=(o_weight, vm), gw=(gate_weight.T, hbm), uw=(up_weight.T, hbm), dw=(down_weight, hbm),
        seq=(seq_lengths, sm), freqs=(frequencies(), vm))
    outputs = dict(
        ogO=((TOKENS, D), bf16, hbm), ntO=((TOKENS, D), bf16, hbm),
        hidO=((TOKENS, COLS), bf16, hbm), guO=((TOKENS, 2 * COLS), bf16, hbm),
        WguO=((2 * COLS, D), bf16, hbm), WdO=((COLS, D), bf16, hbm),
        midO=((BLOCK, HALF), f32, hbm), r1=((BLOCK, HEAD), f32, hbm), r2=((BLOCK, HEAD), f32, hbm),
        attO=((TOKENS, 384), bf16, hbm), PO=((HEADS * BLOCK, 1536), bf16, hbm), QO=((512, 384), bf16, hbm),
        KO=((TOKENS, HEAD), bf16, hbm), VO=((TOKENS, HEAD), bf16, hbm),
        cosO=((TOKENS, HEAD), f32, hbm), sinO=((TOKENS, HEAD), f32, hbm), nxO=((TOKENS, HALF), bf16, hbm),
        WoO=((384, D), bf16, hbm))
    v = pltpu.VMEM
    scratch = dict(
        Wgu=v((2 * COLS, D), bf16), Wd=v((COLS, D), bf16),
        Wkv=v((D, 256), bf16), Wq=v((D, 384), bf16), Wo=v((384, D), bf16), g1f=v((8, D), f32),
        xb=v((TOKENS, D), bf16), nx=v((TOKENS, D), bf16), ogb=v((TOKENS, D), bf16),
        cosT=v((TOKENS, HEAD), f32), sinT=v((TOKENS, HEAD), f32),
        K=v((TOKENS, HEAD), bf16), V=v((TOKENS, HEAD), bf16), Q=v((512, 384), bf16),
        Pr=v((HEADS * BLOCK, 1536), bf16), att=v((TOKENS, 384), bf16),
        staged=v((3, BLOCK, HALF), bf16), held=v((2, 128, HALF), f32),
        low_half=v((128, HALF), bf16), high_half=v((128, HALF), bf16),
        from_low=v((BLOCK, HALF), bf16), from_high=v((BLOCK, HALF), bf16),
        mid=v((BLOCK, HALF), f32), sums=v((2, BLOCK, HEAD), f32), r1T=v((BLOCK, HEAD), f32),
        r2T=v((BLOCK, HEAD), f32), nto=v((BLOCK, HALF), bf16),
        HG=v((TOKENS, COLS), f32), hid=v((TOKENS, COLS), bf16), gu=v((TOKENS, 2 * COLS), bf16),

        send=pltpu.SemaphoreType.DMA((48,)), recv=pltpu.SemaphoreType.DMA((48,)),
        local=pltpu.SemaphoreType.DMA((48,)))
    return kernel_call("front", front_body, inputs, outputs, scratch, 1, flops=30 * 10**9, moved=60 * 2**20)


UNITS = (4, 4, 5)
LEFT = 3328
SCALE = HEAD ** (-0.5)


class Ring:
    def __init__(self, place, along_x):
        z, x = place.z, place.x
        if isinstance(along_x, bool):
            c = x if along_x else z
            ids = [z * 4 + lax.rem(x + s, 4) if along_x else lax.rem(z + s, 4) * 4 + x for s in (1, 3, 2)]
        else:
            c = jnp.where(along_x, x, z)
            ids = [jnp.where(along_x, z * 4 + lax.rem(x + s, 4), lax.rem(z + s, 4) * 4 + x) for s in (1, 3, 2)]
        self.c = c
        self.up, self.down, self.over = ({"dp": i} for i in ids)
        self.next, self.far, self.last = [lax.rem(c + s, 4) for s in (1, 2, 3)]


def scatter_sum(m, ring, src, base, own, out, a, s1, s2, w):
    low, high = slice(0, w), slice(w, None)
    k1 = m.to(ring.up, src(ring.far, low), s1[0])
    k2 = m.to(ring.down, src(ring.far, high), s1[1])
    k3 = m.to(ring.up, src(ring.next, high), s2[0].at[:, w:])
    k4 = m.to(ring.down, src(ring.last, low), s2[1].at[:, :w])
    yield
    k1.wait_recv()
    a[0][...] = (base(0).astype(f32) + s1[0][...].astype(f32)).astype(bf16)
    k5 = m.to(ring.up, a[0], s2[0].at[:, :w])
    k2.wait_recv()
    a[1][...] = (base(1).astype(f32) + s1[1][...].astype(f32)).astype(bf16)
    k6 = m.to(ring.down, a[1], s2[1].at[:, w:])
    yield
    for k in (k3, k4, k5, k6):
        k.wait_recv()
    out[...] = (own().astype(f32) + s2[0][...].astype(f32) + s2[1][...].astype(f32)).astype(bf16)
    yield


def gather_ring(m, ring, part):
    k1 = m.to(ring.up, part(ring.c, None), part(ring.c, None))
    k2 = m.to(ring.down, part(ring.c, None), part(ring.c, None))
    yield
    k1.wait_recv()
    x = part(ring.last, 0)
    k3 = m.to(ring.up, x, x)
    k2.wait_recv()
    x = part(ring.next, 1)
    k4 = m.to(ring.down, x, x)
    yield
    k3.wait_recv()
    k4.wait_recv()
    yield


def aligned_start(start):
    return pl.multiple_of(start, 32)


def aligned(start, size, unit=16):
    return pl.ds(pl.multiple_of(start, unit), size)


def main_piece(n, m, p, i):
    k = UNITS[i]
    base = 256 * sum(UNITS[:i])
    r1, r2 = 64 * k, 16 * k
    own, a, s1, s2 = (getattr(n, f"{name}{i}") for name in ("own", "a", "s1", "s2"))
    b, t1, t2, T2 = (getattr(n, f"{name}{i}") for name in ("b", "t1", "t2", "T"))
    rings = [Ring(p, True), Ring(p, False)]
    loads = []
    first, second = [], []
    for h in range(2):
        one, two = rings[h], rings[1 - h]

        def src(j, lanes, h=h):
            lo, hi = lanes.start + h * HALF, (lanes.stop or HALF) + h * HALF
            return n.G.at[aligned(base + j * r1, r1, 64), pl.ds(lo, hi - lo)]

        loads.append([(src(one.c, slice(0, HALF)), own.at[h]), (src(one.next, slice(0, 384)), a.at[h, 0]),
                      (src(one.last, slice(384, HALF)), a.at[h, 1])])
        first.append(scatter_sum(
            m, one, src, lambda d, h=h: a[h, d], lambda h=h: own[h], own.at[h],
            [a.at[h, 0], a.at[h, 1]], [s1.at[h, 0], s1.at[h, 1]], [s2.at[h, 0], s2.at[h, 1]], 384))

        def src2(j, lanes, h=h):
            return own.at[h, aligned(j * r2, r2), pl.ds(lanes.start, (lanes.stop or HALF) - lanes.start)]

        def base2(d, h=h, two=two):
            if d == 0:
                return own[h, aligned(two.next * r2, r2), :384]
            return own[h, aligned(two.last * r2, r2), 384:]

        second.append(scatter_sum(
            m, two, src2, base2, lambda h=h, two=two: own[h, aligned(two.c * r2, r2), :], T2.at[h],
            [b.at[h, 0], b.at[h, 1]], [t1.at[h, 0], t1.at[h, 1]], [t2.at[h, 0], t2.at[h, 1]], 384))
    for g in first:
        next(g)
    loads = [m.own(*pair) for pairs in loads for pair in pairs]
    yield
    for c in loads:
        c.wait()
    for g in first:
        next(g)
    yield
    for g, g2 in zip(first, second):
        next(g)
        next(g2)
    yield
    for g in second:
        next(g)
    yield
    for g in second:
        next(g)
    one = Ring(p, p.gx == 0)
    two = Ring(p, p.gx != 0)

    def place(c1, c2, rows):
        return aligned(base + c1 * r1 + c2 * r2, rows)

    there = (Ring(p, p.gx != 0), Ring(p, p.gx == 0))
    mine = m.own(T2.at[p.gx], n.O.at[p.gx, place(one.c, two.c, r2)])
    swap = m.to(p.pal, T2.at[1 - p.gx], n.O.at[p.gx, place(there[0].c, there[1].c, r2)])
    yield
    mine.wait()
    swap.wait_recv()

    def part_two(j, half):
        r = place(one.c, j, r2)
        return n.O.at[:, r] if half is None else n.O.at[half, r]

    def part_one(j, half):
        r = place(j, jnp.int32(0), r1)
        return n.O.at[:, r] if half is None else n.O.at[half, r]

    g = gather_ring(m, two, part_two)
    next(g)
    yield
    next(g)
    yield
    next(g)
    g = gather_ring(m, one, part_one)
    next(g)
    yield
    next(g)
    yield
    next(g)
    yield


def small_piece(n, m, p, k):
    rings = [Ring(p, True), Ring(p, False)]
    r1, r2, W, top = 128, 32, 384, 512 * k
    lanes = [pl.ds(h * W, W) for h in range(2)]
    T, F, U = (getattr(n, f"{name}m{k}") for name in "TFU")

    def spread(ring, src, dst):
        return [m.to(d, src(j), dst(k)) for k, (d, j) in enumerate(
            ((ring.up, ring.next), (ring.down, ring.last), (ring.over, ring.far)))]

    def total(own, came):
        return (own.astype(f32) + came[0].astype(f32)) + (came[1].astype(f32) + came[2].astype(f32))

    first = []
    for h in range(2):
        one, w = rings[h], (256, 128)[h]

        def src(j, part, h=h):
            lo, hi = part.start + h * W, (part.stop or W) + h * W
            return n.M.at[aligned(j * r1 + top, r1), pl.ds(lo, hi - lo)]

        def base(d, h=h, one=one, w=w):
            if d == 0:
                return n.M[aligned(one.next * r1 + top, r1), h * W:h * W + w]
            return n.M[aligned(one.last * r1 + top, r1), h * W + w:(h + 1) * W]

        first.append(scatter_sum(
            m, one, src, base, lambda h=h, one=one: n.M[aligned(one.c * r1 + top, r1), h * W:(h + 1) * W], T.at[h],
            [getattr(n, f"am{k}{h}{d}") for d in range(2)], [getattr(n, f"sm{k}{h}{d}") for d in range(2)],
            [getattr(n, f"Em{k}").at[h, d] for d in range(2)], w))
    for g in first:
        next(g)
    yield
    for g in first:
        next(g)
    yield
    moves = [None, None]
    for h in range(2):
        next(first[h])
        moves[h] = spread(rings[1 - h], lambda j, h=h: T.at[h, aligned(j * r2, r2)], lambda i, h=h: F.at[h, i])
    yield
    for h in range(2):
        one, two = rings[h], rings[1 - h]
        for c in moves[h]:
            c.wait_recv()
        U[h] = total(T[h, aligned(two.c * r2, r2)], F[h]).astype(bf16)
        there = n.O4.at[aligned(one.c * r1 + two.c * r2 + top, r2), lanes[h]]
        moves[h] = spread(two, lambda j, h=h: U.at[h], lambda i, there=there: there)
        moves[h].append(m.own(U.at[h], there))
    yield
    for h in range(2):
        for c in moves[h][:3]:
            c.wait_recv()
        moves[h][3].wait()

        def part(j, half, h=h):
            at, rows = (0, r1) if half is None else (half * r1 // 2, r1 // 2)
            return n.O4.at[aligned(j * r1 + top + at, rows), lanes[h]]

        first[h] = gather_ring(m, rings[h], part)
        next(first[h])
    yield
    for g in first:
        next(g)
    yield
    for g in first:
        next(g)
    if k == 0:
        held = n.ntV.at[pl.ds(0, 64), pl.ds(0, HALF)]
        m.own(n.O4.at[pl.ds(384, 64)], held).wait()
        moves = []
        rest = [m.own(held.at[pl.ds(32 * core, 32)], n.O.at[core, pl.ds(LEFT, 32)]) for core in range(2)]
    else:
        block = pl.ds(896, HEAD)
        held = n.ntV.at[pl.ds(64, HEAD), pl.ds(0, HALF)]
        load = m.own(n.O4.at[block], held)
        moves = [m.to(d, n.O4.at[block], n.Oy.at[p.gy]) for d in (p.up, p.down, {"gy": lax.rem(p.gy + 2, 4)})]
        load.wait()
        rest = [m.own(held, n.Oy.at[p.gy])]
    yield
    for c in moves:
        c.wait_recv()
    for c in rest:
        c.wait()
    yield


SCHED = {
    "down": "0", "b0": "", "b1": "", "b2": "0", "b3": "", "own": "", "gate": "1",
    "result": "0", "ml": "", "up": "102",
    "c0": "", "c1": "", "ml1": "", "c2": "", "c3": "", "ml2": "10", "ml3": "0", "ml4": "o",
    "a10": "2", "a11": "", "a12": "10o", "relay2": "", "a00": "", "a01": "", "a02": "21",
    "pair": "1o20", "m1": "12om", "m2": "2om", "m3": "v1",
    "tail": "vm20vmo2vm1o2momm", "rest": "om012v"}


def vector_sum(n, m, p):
    coordinates = (p.x, p.z, p.gy)
    devices = (lambda s: {"dp": p.z * 4 + lax.rem(p.x + s, 4)}, lambda s: {"dp": lax.rem(p.z + s, 4) * 4 + p.x},
               lambda s: {"gy": lax.rem(p.gy + s, 4)})
    value = n.gain1[...]
    for d in range(3):
        if d == 2:
            n.vector_dp[...] = value
        slot = n.vectors.at[d, coordinates[d]]
        slot[...] = value
        moves = [m.to(devices[d](s), slot, slot) for s in (1, 3, 2)]
        yield
        for c in moves:
            c.wait_recv()
        value = (n.vectors[d, 0] + n.vectors[d, 1]) + (n.vectors[d, 2] + n.vectors[d, 3])
    n.vector_all[...] = value
    for k in range(4):
        n.kv_bias[:, k * HEAD:(k + 1) * HEAD] = n.vectors[2, k, :, 384:512]
    yield


def back_body(n):
    m = Moves(n.send, n.recv, n.local)
    back_steps(n, m)
    m.finish()


def back_steps(n, m):
    p = Place()
    dp = lax.axis_index("dp")
    p.z, p.x = lax.div(dp, 4), lax.rem(dp, 4)
    gx, gy = p.gx, p.gy
    pal_cols = pl.ds(pl.multiple_of((1 - gx) * HALF, 128), HALF)
    vm = Names({})
    load = {}

    def bring(name, src, dst):
        load[name] = m.own(src, dst)

    bring("og", n.ogf, n.ml)
    bring("hid", n.hid, n.ntV.at[:, pl.ds(0, COLS)])
    bring("gu", n.gu, n.guV)
    bring("Wgu", n.Wgu, n.WguV)
    bring("mid", n.mid, n.midV)
    bring("r2", n.r2, n.r2V)
    for name in ("Q", "K", "V", "cos", "sin", "r1"):
        bring(name, getattr(n, name), getattr(n, name + "V"))
    rings = [Ring(p, True), Ring(p, False)]
    gens = {str(i): main_piece(n, m, p, i) for i in range(3)}
    entered = enter([p.up, p.down, p.pal, rings[0].up, rings[0].down, rings[1].up, rings[1].down])

    def ar(spot):
        for name in SCHED[spot]:
            next(gens[name], None)

    def leave(slot, k, i, rows):
        at = k * REAL + i * BLOCK
        at = pl.multiple_of(at, 32) if isinstance(i, int) else aligned_start(at)
        return pltpu.make_async_copy(
            n.stage.at[slot, pl.ds(0, rows)], n.G.at[pl.ds(at, rows)], n.gsem.at[slot])

    def weight_grad(k, left, at, right, before_tail=lambda: None):
        @pl.loop(0, 4)
        def _(i):
            slot = lax.rem(i, 2)

            @pl.when(i >= 2)
            def _():
                leave(slot, k, i, BLOCK).wait()

            c = pl.ds(pl.multiple_of(i * BLOCK + at, 128), BLOCK)
            n.stage[slot] = dg(left[:, c], right[...], 0, 0).astype(bf16)
            leave(slot, k, i, BLOCK).start()

        leave(0, k, 2, BLOCK).wait()
        leave(1, k, 3, BLOCK).wait()
        before_tail()
        tail = dg(left[:, at + 4 * BLOCK:at + COLS], right[...], 0, 0).astype(bf16)
        n.stage[0, :REAL - 4 * BLOCK] = tail[:REAL - 4 * BLOCK]
        leave(0, k, 4, REAL - 4 * BLOCK).start()
        leave(0, k, 4, REAL - 4 * BLOCK).wait()

    for name in ("og", "hid"):
        load[name].wait()

    def down_ready():
        entered()
        ar("down")

    weight_grad(0, n.ntV, 0, n.ml, down_ready)
    bring("nt", n.nt, n.ntV)

    for name in ("gu", "Wgu"):
        load[name].wait()

    def two_sided(left, weight, take, give, held, names):
        order = (2, 1, 3, 0)
        moves = []
        for k, which in enumerate(order):
            r = rows_of(p.blk[which])
            if k >= 2:
                moves[k - 2].wait_send()
            give[k % 2] = dot(left(r), weight(pal_cols)).astype(bf16)
            moves.append(m.to(p.pal, give.at[k % 2], take.at[k]))
            held[k % 2] = dot(left(r), weight(p.cols))
            if k:
                moves[k - 1].wait_recv()
                yield held[(k - 1) % 2] + take[k - 1].astype(f32)
            ar(names[k])
        moves[3].wait_recv()
        moves[2].wait_send()
        moves[3].wait_send()
        yield held[1] + take[3].astype(f32)

    def scatter(letter):
        return ScatterY(m, p, n.staged, n.held, *(getattr(n, letter + name) for name in ("low", "high", "flow", "fhigh")))

    g = two_sided(lambda r: n.guV[r, :], lambda c: n.WguV[:, c], n.take, n.give, n.two, ("b0", "b1", "b2", "b3"))
    rs = scatter("A")
    rs.far(next(g))
    rs.next_up(next(g))
    rs.next_down(next(g))
    n.part[...] = next(g)
    ar("own")
    bring("Wd", n.Wd, n.WguV.at[pl.ds(0, COLS)])
    bring("P", n.P, n.WguV.at[pl.ds(COLS, HEADS * BLOCK)])
    bring("Wo", n.Wo, n.WguV.at[pl.ds(1920, 384)])
    load["nt"].wait()
    rs.relay()
    weight_grad(1, n.guV, 0, n.ntV)
    ar("gate")
    n.part[...] = rs.result(n.part[...])
    ar("result")
    load["mid"].wait()
    load["r2"].wait()
    r2 = n.r2V[:, :1]
    y2 = n.midV[...] * r2
    w2 = n.part[...] * n.g2[...].reshape(1, HALF)
    n.gain2[...] = jnp.broadcast_to(jnp.sum(n.part[...] * y2, axis=0, keepdims=True), (8, HALF))
    n.sums[0] = jnp.broadcast_to(jnp.sum(w2 * y2, axis=1, keepdims=True), (BLOCK, HEAD))
    sum_move = m.to(p.pal, n.sums.at[0], n.sums.at[1])
    sum_move.wait_recv()
    total = (n.sums[0] + n.sums[1])[:, :1] * (1.0 / D)
    n.mg[...] = n.og[...].astype(f32) + r2 * (w2 - y2 * total)
    n.mlo[...] = n.mg[...].astype(bf16)
    gather = GatherY(m, p, n.mlo, n.ml)
    gather.start()
    n.ml[rows_of(gy), p.cols] = n.mlo[...]
    ar("ml")
    weight_grad(2, n.guV, COLS, n.ntV)
    ar("up")
    bring("hid", n.hid, n.guV.at[:, pl.ds(0, COLS)])
    bring("nx", n.nx, n.guV.at[:, pl.ds(COLS, HALF)])
    bring("att", n.att, n.guV.at[:, pl.ds(COLS + HALF, 384)])
    left_row = aligned(384 + gx * 32, 32, 32)
    bring("left", n.G.at[pl.ds(LEFT, 32), p.cols], n.M.at[left_row])
    left_move = m.to(p.pal, n.G.at[pl.ds(LEFT, 32), pal_cols], n.M.at[left_row])

    load["hid"].wait()
    load["Wd"].wait()
    g = two_sided(lambda r: n.guV[r, :COLS], lambda c: n.WguV[:COLS, c], n.take, n.give, n.two, ("c0", "c1", "c2", "c3"))
    n.later[0] = next(g).astype(bf16)
    gather.relay()
    ar("ml1")
    for k in (1, 2):
        n.later[k] = next(g).astype(bf16)
    n.part[...] = next(g) + n.midV[...]
    ar("ml2")
    gather.relay_pal()
    m.settle([rs.a, rs.b, rs.c, rs.d, rs.e, rs.f])
    rs = scatter("B")
    rs.far(n.later[0].astype(f32))
    rs.next_up(n.later[1].astype(f32))
    rs.next_down(n.later[2].astype(f32))
    gather.own_ready()
    gather.low_ready()
    gather.high_ready()
    ar("ml3")

    for name in ("att", "Q", "K", "V", "cos", "sin", "nx", "Wo", "r1", "P", "left"):
        load[name].wait()
    gather.far_ready()
    n.M[0:384, :] = dg(n.guV[:, COLS + HALF:], n.ml[:, p.cols], 0, 0).astype(bf16)
    n.M[448:512, :] = jnp.zeros((64, HALF), bf16)
    left_move.wait_recv()
    gens["o"] = small_piece(n, m, p, 0)
    ar("ml4")
    own_blocks = [gx, 3 - gx]
    q_moves = []
    for i in (1, 0):
        b = rows_of(own_blocks[i])
        keys, at = 512 * (i + 1), 512 * i
        n.ag[...] = dg(n.ml[b, :], n.WguV[1920:, :], 1, 1).astype(bf16)
        for h in range(HEADS):
            c = slice(h * HEAD, (h + 1) * HEAD)
            probs = n.WguV[COLS + h * BLOCK:COLS + (h + 1) * BLOCK, at:at + keys]
            probs_f = probs.astype(f32)
            prob_grads = dg(n.ag[:, c], n.VV[:keys, :], 1, 1)
            centre = jnp.sum(probs_f * prob_grads, axis=1, keepdims=True)
            score_grads = (probs_f * (prob_grads - centre)).astype(bf16)
            dq = dot(score_grads, n.KV[:keys, :]) * SCALE
            dk = dg(score_grads, n.QV[i * BLOCK:(i + 1) * BLOCK, c], 0, 0) * SCALE
            dv = dg(probs, n.ag[:, c], 0, 0)
            if i == 1 and h == 0:
                n.dkv[:, :HEAD] = dk
                n.dkv[:, HEAD:] = dv
            else:
                n.dkv[:keys, :HEAD] += dk
                n.dkv[:keys, HEAD:] += dv
            n.ql[b, c] = turned(dq, n.cosV[b, :], -n.sinV[b, :]).astype(bf16)
            ar(f"a{i}{h}")
        q_moves.append(m.to(p.pal, n.ql.at[b], n.ql.at[b]))
        if i == 1:
            rs.relay()
            ar("relay2")
    n.S[0] = n.dkv[...].astype(bf16)
    s_move = m.to(p.pal, n.S.at[0], n.S.at[1])
    n.block_out[...] = rs.result(n.part[...])
    s_move.wait_recv()
    both = n.S[0].astype(f32) + n.S[1].astype(f32)
    n.dkv[...] = both
    n.S2[...] = both.astype(bf16)
    odd = lax.rem(gy, 2)
    pair = {"gy": gy + 1 - 2 * odd}
    pair_move = m.to(pair, n.S2.at[:, pl.ds(pl.multiple_of((1 - odd) * HEAD, HEAD), HEAD)], n.pin)
    ar("pair")
    for copy in q_moves:
        copy.wait_recv()
    n.M[512:896, :] = dg(n.ql[...], n.guV[:, COLS:COLS + HALF], 0, 0).astype(bf16)
    pair_move.wait_recv()
    kv = n.dkv[:, pl.ds(pl.multiple_of(odd * HEAD, HEAD), HEAD)] + n.pin[...].astype(f32)
    is_key = (1 - odd).astype(f32)
    cosine = n.cosV[...] * is_key + (1.0 - is_key)
    sine = n.sinV[...] * is_key
    n.plow[...] = turned(kv, cosine, -sine).astype(bf16)
    n.M[896:, :] = dg(n.plow[...], n.guV[:, COLS:COLS + HALF], 0, 0).astype(bf16)
    bias = jnp.concatenate([
        jnp.sum(n.ql[...].astype(f32), axis=0, keepdims=True),
        jnp.sum(n.plow[...].astype(f32), axis=0, keepdims=True),
        jnp.zeros((1, 256), f32)], axis=1)

    def norm_one_part(block):
        r = rows_of(block)
        kvw = n.kvw[:, pl.ds(pl.multiple_of(gy * HEAD, HEAD), HEAD)]
        return dg(n.ql[r, :], n.qw[...], 1, 1) + dg(n.plow[r, :], kvw, 1, 1)

    m.settle([rs.a, rs.b, rs.c, rs.d, rs.e, rs.f])
    rs = scatter("A")
    rs.far(norm_one_part(p.blk[2]))
    rs.next_up(norm_one_part(p.blk[1]))
    rs.next_down(norm_one_part(p.blk[3]))
    n.part[...] = norm_one_part(p.blk[0])
    gens["m"] = small_piece(n, m, p, 1)
    ar("m1")
    rs.relay()
    ar("m2")
    n.part[...] = rs.result(n.part[...])
    r1 = n.r1V[:, :1]
    y1 = n.x[...].astype(f32) * r1
    w1 = n.part[...] * n.g1[...].reshape(1, HALF)
    gain1 = jnp.sum(n.part[...] * y1, axis=0, keepdims=True)
    m.settle([sum_move])
    n.sums[0] = jnp.broadcast_to(jnp.sum(w1 * y1, axis=1, keepdims=True), (BLOCK, HEAD))
    sum_move = m.to(p.pal, n.sums.at[0], n.sums.at[2])
    row = lax.broadcasted_iota(jnp.int32, (8, HALF), 0)
    n.gain1[...] = jnp.where(row == 0, gain1, jnp.where(row == 1, n.gain2[0:1, :], jnp.where(row == 2, bias, 0.0)))
    gens["v"] = vector_sum(n, m, p)
    ar("m3")
    sum_move.wait_recv()
    total = (n.sums[0] + n.sums[2])[:, :1] * (1.0 / D)
    n.input_grad[...] = n.mg[...] + r1 * (w1 - y1 * total)
    ar("tail")
    for _ in range(14):
        ar("rest")


def back(f, layer_input, norm1_gain, q_weight, kv_weight, norm2_gain, out_grad):
    vm, hbm = pltpu.VMEM, pl.ANY
    inputs = dict(
        x=(layer_input, vm), og=(out_grad, vm), g1=(norm1_gain, vm), g2=(norm2_gain, vm),
        qw=(q_weight, vm), kvw=(kv_weight, vm),
        ogf=(f.ogO, hbm), nt=(f.ntO, hbm), gu=(f.guO, hbm), Wgu=(f.WguO, hbm), hid=(f.hidO, hbm), Wd=(f.WdO, hbm), mid=(f.midO, hbm),
        r1=(f.r1, hbm), r2=(f.r2, hbm), att=(f.attO, hbm), P=(f.PO, hbm), Q=(f.QO, hbm), K=(f.KO, hbm),
        V=(f.VO, hbm), cos=(f.cosO, hbm), sin=(f.sinO, hbm), nx=(f.nxO, hbm), Wo=(f.WoO, hbm))
    outputs = dict(
        block_out=((BLOCK, HALF), f32, vm), input_grad=((BLOCK, HALF), f32, vm),
        O=((2, 3 * REAL, HALF), bf16, hbm), O4=((TOKENS, HALF), bf16, hbm), Oy=((4, HEAD, HALF), bf16, hbm),
        vector_all=((8, HALF), f32, vm), vector_dp=((8, HALF), f32, vm), kv_bias=((8, 512), f32, vm), G=((3 * REAL, D), bf16, hbm))
    v = pltpu.VMEM
    scratch = dict(
        guV=v((TOKENS, 2 * COLS), bf16), WguV=v((2 * COLS, D), bf16), midV=v((BLOCK, HALF), f32),
        r1V=v((BLOCK, HEAD), f32), r2V=v((BLOCK, HEAD), f32), QV=v((512, 384), bf16),
        KV=v((TOKENS, HEAD), bf16), VV=v((TOKENS, HEAD), bf16), cosV=v((TOKENS, HEAD), f32),
        sinV=v((TOKENS, HEAD), f32), ntV=v((TOKENS, D), bf16),
        take=v((4, BLOCK, HALF), bf16), give=v((2, BLOCK, HALF), bf16), two=v((2, BLOCK, HALF), f32),
        staged=v((3, BLOCK, HALF), bf16), held=v((2, 128, HALF), f32),
        part=v((BLOCK, HALF), f32), later=v((3, BLOCK, HALF), bf16), stage=v((2, BLOCK, D), bf16),
        gain1=v((8, HALF), f32), vectors=v((3, 4, 8, HALF), f32), gain2=v((8, HALF), f32), sums=v((3, BLOCK, HEAD), f32),
        mg=v((BLOCK, HALF), f32), mlo=v((BLOCK, HALF), bf16), ml=v((TOKENS, D), bf16),
        ag=v((BLOCK, 384), bf16), dkv=v((TOKENS, 256), f32), ql=v((TOKENS, 384), bf16), S=v((2, TOKENS, 256), bf16),
        S2=v((TOKENS, 256), bf16), pin=v((TOKENS, HEAD), bf16), plow=v((TOKENS, HEAD), bf16), M=v((TOKENS, HALF), bf16),
    )
    for k in range(2):
        scratch.update({f"Em{k}": v((2, 2, 128, 384), bf16), f"Tm{k}": v((2, 128, 384), bf16),
                        f"Fm{k}": v((2, 3, 32, 384), bf16), f"Um{k}": v((2, 32, 384), bf16)})
        for h in range(2):
            for d in range(2):
                w = (256, 128)[(h + d) % 2]
                scratch.update({f"am{k}{h}{d}": v((128, w), bf16), f"sm{k}{h}{d}": v((128, w), bf16)})
    for letter in "AB":
        scratch.update({letter + "low": v((128, HALF), bf16), letter + "high": v((128, HALF), bf16),
                        letter + "flow": v((BLOCK, HALF), bf16), letter + "fhigh": v((BLOCK, HALF), bf16)})
    for i, k in enumerate(UNITS):
        r1, r2 = 64 * k, 16 * k
        scratch.update({
            f"own{i}": v((2, r1, HALF), bf16), f"a{i}": v((2, 2, r1, 384), bf16), f"s1{i}": v((2, 2, r1, 384), bf16),
            f"s2{i}": v((2, 2, r1, HALF), bf16), f"b{i}": v((2, 2, r2, 384), bf16), f"t1{i}": v((2, 2, r2, 384), bf16),
            f"t2{i}": v((2, 2, r2, HALF), bf16), f"T{i}": v((2, r2, HALF), bf16)})
    scratch.update(send=pltpu.SemaphoreType.DMA((240,)), recv=pltpu.SemaphoreType.DMA((240,)),
                   local=pltpu.SemaphoreType.DMA((64,)), gsem=pltpu.SemaphoreType.DMA((2,)))
    return kernel_call("back", back_body, inputs, outputs, scratch, 2, flops=16 * 10**9, moved=60 * 2**20)


PART = 560
SLOTS = 6


def finish(b):
    jobs = [(core, t, j) for j in range(REAL // PART) for core in range(2) for t in range(3)]

    def kernel(big, small, shared, gain, dp_sums, kv_sums, block, grad, down, gate, up, o, q, kv, block_out, grad_out,
               gain1, gain2, q_bias, kv_bias, came, leaving, small_in, shared_in, o_to, q_to, kv_to, through,
               in_sem, out_sem, sem):
        outs = (down, gate, up)

        def read(i):
            core, t, j = jobs[i]
            return pltpu.make_async_copy(
                big.at[core, pl.ds(t * REAL + j * PART, PART)], came.at[i % SLOTS], in_sem.at[i % SLOTS])

        def write(i):
            core, t, j = jobs[i]
            return pltpu.make_async_copy(
                leaving.at[i % SLOTS], outs[t].at[pl.ds(core * REAL + j * PART, PART)], out_sem.at[i % SLOTS])

        for i in range(3):
            read(i).start()
        loads = [pltpu.make_async_copy(small, small_in, sem.at[0]), pltpu.make_async_copy(shared, shared_in, sem.at[1])]
        passes = [pltpu.make_async_copy(block, through.at[0], sem.at[2]),
                  pltpu.make_async_copy(grad, through.at[1], sem.at[3])]
        for c in loads:
            c.start()
        for i in range(3, SLOTS):
            read(i).start()
        for c in passes:
            c.start()
        rest = []
        for i in range(len(jobs)):
            read(i).wait()
            if i >= SLOTS:
                write(i - SLOTS).wait()
            leaving[i % SLOTS] = came[i % SLOTS].astype(f32)
            write(i).start()
            if i + SLOTS < len(jobs):
                read(i + SLOTS).start()
            if i == 3:
                for c in loads + passes:
                    c.wait()
                for k, c in enumerate((block_out, grad_out)):
                    rest.append(pltpu.make_async_copy(through.at[k], c, sem.at[7 + k]))
                    rest[-1].start()
                o_to[...] = small_in[:384, :].astype(f32)
                rest.append(pltpu.make_async_copy(o_to, o, sem.at[4]))
                rest[-1].start()
            if 4 <= i < 7:
                k = i - 4
                q_to[:, k * HEAD:(k + 1) * HEAD] = small_in[512 + k * HEAD:512 + (k + 1) * HEAD, :].T.astype(f32)
                if k == 2:
                    rest.append(pltpu.make_async_copy(q_to, q, sem.at[5]))
                    rest[-1].start()
            if 7 <= i < 11:
                k = i - 7
                kv_to[:, k * HEAD:(k + 1) * HEAD] = shared_in[k].T.astype(f32)
                if k == 3:
                    rest.append(pltpu.make_async_copy(kv_to, kv, sem.at[6]))
                    rest[-1].start()
            if i == 11:
                gain1[...] = gain[0]
                gain2[...] = gain[1]
                q_bias[...] = dp_sums[2, :384]
                kv_bias[...] = kv_sums[2]
        for i in range(len(jobs) - SLOTS, len(jobs)):
            write(i).wait()
        for c in rest:
            c.wait()

    def array(*shape):
        return jax.ShapeDtypeStruct(shape, f32)

    v = pltpu.VMEM
    hbm, vm = pl.BlockSpec(memory_space=pl.ANY), pl.BlockSpec(memory_space=v)
    weight = array(2 * REAL, HALF)
    down, gate, up, o, q, kv, block_out, grad, gain1, gain2, q_bias, kv_bias = pl.pallas_call(
        kernel,
        in_specs=[hbm] * 3 + [vm] * 3 + [hbm] * 2,
        out_specs=[hbm] * 8 + [vm] * 4,
        out_shape=[weight, weight, weight, array(384, HALF), array(HALF, 384), array(HALF, 512),
                   array(BLOCK, HALF), array(BLOCK, HALF), array(HALF), array(HALF), array(384), array(512)],
        scratch_shapes=[v((SLOTS, PART, HALF), bf16), v((SLOTS, PART, HALF), f32), v((TOKENS, HALF), bf16),
                        v((4, HEAD, HALF), bf16), v((384, HALF), f32), v((HALF, 384), f32), v((HALF, 512), f32), v((2, BLOCK, HALF), f32),
                        pltpu.SemaphoreType.DMA((SLOTS,)), pltpu.SemaphoreType.DMA((SLOTS,)),
                        pltpu.SemaphoreType.DMA((9,))],
        compiler_params=pltpu.CompilerParams(vmem_limit_bytes=60 * 2**20),
        name="finish",
    )(b.O, b.O4, b.Oy, b.vector_all, b.vector_dp, b.kv_bias, b.block_out, b.input_grad)
    return block_out, grad, gain1, q, q_bias, kv, kv_bias, o, gain2, gate.T, up.T, down


def per_device(layer_input, norm1_gain, q_weight, q_bias, kv_weight, kv_bias, o_weight, norm2_gain,
               gate_weight, up_weight, down_weight, seq_lengths, out_grad):
    f = front(layer_input, norm1_gain, q_weight, q_bias, kv_weight, kv_bias, o_weight, norm2_gain,
              gate_weight, up_weight, down_weight, seq_lengths, out_grad)
    b = back(f, layer_input, norm1_gain, q_weight, kv_weight, norm2_gain, out_grad)
    return finish(b)


def solution(mesh):
    rows, width = P(("dp", "gy"), "gx"), P("gx", "gy")
    return jax.shard_map(
        per_device,
        mesh=mesh,
        in_specs=(rows, P("gx"), width, P("gy"), P("gx", None), P(), P("gy", "gx"), P("gx"), width, width,
                  P("gy", "gx"), P("dp", None), rows),
        out_specs=(rows, rows, P("gx"), width, P("gy"), P("gx", None), P(), P("gy", "gx"), P("gx"), width, width,
                   P("gy", "gx")),
        check_vma=False,
    )
```
